128 devices in a mesh: row: 8 (over y, z_hi), col: 16 (over x, z_lo, core).
Axes of the slice: x: 4, y: 4, z: 4 (z_hi: 2, z_lo: 2; z = z_hi * 2 + z_lo), core: 2. Of those that a mesh axis runs over, the one named last changes fastest.
Arguments:
- amps: bfloat16 [8, 16, 2, 2, 768, 768], P('row', 'col'), may hold values from -6 to 6
- x_factor: bfloat16 [16, 64, 768], P('row'), may hold values from -0.21875 to 0.21875
- core: bfloat16 [768, 768], replicated, may hold values from -6 to 6
- cycle_w: bfloat16 [8, 2, 2, 1024, 1024], P('row', None, None, 'col'), may hold values from -0.15625 to 0.15625
- domain_tiles: int32 [8, 16, 12], P('row', 'col'), may hold values from 0 to 15, as said below
- domain_count: int32 [8, 16], P('row', 'col'), may hold values from 6 to 12, as said below
- tile_slot: int32 [16], replicated, may hold values from 0 to 15, each once
- occ_energy: float32 [8, 16, 2, 2], P('row', 'col'), may hold values from -2 to -0.5
- virt_energy: float32 [1024], replicated, may hold values from 0.5 to 3
Outputs:
- residual: float32 [8, 16, 2, 2, 768, 768], P('row', 'col')
- updated: bfloat16 [8, 16, 2, 2, 768, 768], P('row', 'col')
The draws below stay inside these ranges and needn't reach their ends.
Inputs may be any that keep to these rules, and one draw needn't show every extreme that they name: `domain_tiles`: each block's 12 entries are distinct tile numbers; the first domain_count of them form its domain. Blocks (r, c) and (r, c + 8) have the same list. `domain_count`: blocks (r, c) and (r, c + 8) have the same count. `tile_slot`: A permutation of the tile numbers.
All inputs are finite; a program needn't handle non-finite values.
Results may differ from the reference program's by a relative error of at most 0.0085.
Values may be sent and summed in bfloat16 or wider, within the bound.
A program may use at most 192 MiB of HBM per device.

```python
import jax
import jax.numpy as jnp
from jax import lax

TILE = 64
KMAX = 12
KMIN = 6
NVT = 16
OCC = 2
NP = 768
DV = 768
VW = 1024
N_ROW = 8
N_COL = 16


def draw_domain_tiles(key, part):
    key = jax.random.fold_in(key, 11)
    scores = jax.random.randint(key, (N_ROW, N_COL // 2, NVT), 0, 1 << 20) * NVT + jnp.arange(NVT, dtype=jnp.int32)
    ranked = jnp.argsort(scores, axis=-1, stable=True).astype(jnp.int32)[..., :KMAX]
    return jnp.concatenate([ranked, ranked], axis=1)


def draw_domain_count(key, part):
    key = jax.random.fold_in(key, 23)
    half_grid = jax.random.randint(key, (N_ROW, N_COL // 2), KMIN, KMAX + 1).astype(jnp.int32)
    half_grid = half_grid.at[0, 0].set(KMAX).at[0, 1].set(KMIN)
    return jnp.concatenate([half_grid, half_grid], axis=1)


def levels(stream_key, shape, shards, least, largest):
    def one(axis_at, blocks):
        steps = jax.random.uniform(jax.random.fold_in(jax.random.fold_in(stream_key, 6), axis_at), (blocks,), jnp.float32, least / len(shards), largest / len(shards))
        return jnp.repeat(jnp.exp(steps), shape[axis_at] // blocks).reshape((-1,) + (1,) * (len(shape) - axis_at - 1))

    level = one(*shards[0])
    for cut in shards[1:]:
        level = level * one(*cut)
    return level


def normal_values(own_key, extent, width, most, split=(), held_as=jnp.bfloat16):
    drawn = width * jax.random.normal(own_key, extent, jnp.float32)
    if split:
        drawn = drawn * levels(own_key, extent, split, -0.22, 0.18)
    return jnp.clip(drawn, -most, most).astype(held_as)


def setup_inputs(seed: int = 0) -> dict:
    seeds = jax.random.split(jax.random.key(seed), 10)
    amps = normal_values(seeds[0], (N_ROW, N_COL, OCC, OCC, DV, DV), 1.0, 6.0, ((0, 8), (1, 16)))
    x_factor = normal_values(seeds[1], (NVT, TILE, NP), DV ** -0.5, 0.21875, ((0, 8),))
    core = normal_values(seeds[2], (NP, NP), 1.0, 6.0)
    cycle_w = normal_values(seeds[3], (N_ROW, OCC, OCC, VW, VW), (OCC * DV) ** -0.5, 0.15625, ((0, 8), (3, 16)))
    domain_tiles = draw_domain_tiles(jax.random.fold_in(seeds[9], 71), 0)
    domain_count = draw_domain_count(jax.random.fold_in(seeds[9], 71), 0)
    tile_slot = jax.random.permutation(seeds[6], NVT).astype(jnp.int32)
    occ_energy = jnp.clip(-2.0 + 1.5 * jax.random.uniform(seeds[7], (N_ROW, N_COL, 2, OCC), jnp.float32) ** levels(seeds[7], (N_ROW, N_COL, 2, OCC), ((0, 8), (1, 16)), -0.2, 0.2), -2.0, -0.5)
    virt_energy = jnp.clip(jax.random.uniform(seeds[8], (VW,), jnp.float32, 0.5, 3.0), 0.5, 3.0)
    return {"amps": amps, "x_factor": x_factor, "core": core, "cycle_w": cycle_w, "domain_tiles": domain_tiles, "domain_count": domain_count, "tile_slot": tile_slot, "occ_energy": occ_energy, "virt_energy": virt_energy}


def ladder_term(domain_factors, core_float, pair_amps):
    projected = lax.dot_general(domain_factors, pair_amps, (((0,), (0,)), ((), ())), preferred_element_type=jnp.float32).astype(jnp.bfloat16)
    inner = jnp.dot(projected, domain_factors, preferred_element_type=jnp.float32)
    weighted = (core_float * inner).astype(jnp.bfloat16)
    spread = jnp.dot(domain_factors, weighted, preferred_element_type=jnp.float32).astype(jnp.bfloat16)
    return lax.dot_general(spread, domain_factors, (((1,), (1,)), ((), ())), preferred_element_type=jnp.float32)


def pair_residual(masked_amps, domain_factors, core_float, domain_cycle, first_occ, second_occ):
    total = ladder_term(domain_factors, core_float, masked_amps[first_occ, second_occ])
    for middle_occ in range(OCC):
        total = total + jnp.dot(domain_cycle[first_occ, middle_occ], masked_amps[middle_occ, second_occ], preferred_element_type=jnp.float32)
    return total


def block_residual(masked_amps, domain_factors, core_float, domain_cycle):
    rows_out = []
    for first_occ in range(OCC):
        rows_out.append(jnp.stack([pair_residual(masked_amps, domain_factors, core_float, domain_cycle, first_occ, second_occ) for second_occ in range(OCC)]))
    return jnp.stack(rows_out)


def domain_setup(tile_list, live_count):
    live_slots = jnp.arange(KMAX, dtype=jnp.int32) < live_count
    row_mask = jnp.repeat(live_slots, TILE)
    window_index = (tile_list[:, None] * TILE + jnp.arange(TILE, dtype=jnp.int32)[None, :]).reshape(DV)
    return row_mask, window_index


def reference(amps, x_factor, core, cycle_w, domain_tiles, domain_count, tile_slot, occ_energy, virt_energy):
    core_float = core.astype(jnp.float32)
    blocks_flat = amps.reshape(N_ROW * N_COL, OCC, OCC, DV, DV)
    tiles_flat = domain_tiles.reshape(N_ROW * N_COL, KMAX)
    counts_flat = domain_count.reshape(N_ROW * N_COL)
    row_numbers = jnp.arange(N_ROW * N_COL, dtype=jnp.int32) // N_COL

    def one_block(packed):
        block_amps, tile_list, live_count, row_number = packed
        row_mask, window_index = domain_setup(tile_list, live_count)
        pair_mask = row_mask[:, None] & row_mask[None, :]
        domain_factors = x_factor[tile_slot[tile_list]].reshape(DV, NP)
        domain_factors = jnp.where(row_mask[:, None], domain_factors, jnp.zeros_like(domain_factors))
        row_cycle = cycle_w[row_number]
        domain_cycle = jnp.take(jnp.take(row_cycle, window_index, axis=2), window_index, axis=3)
        domain_cycle = jnp.where(pair_mask, domain_cycle, jnp.zeros_like(domain_cycle))
        masked_amps = jnp.where(pair_mask, block_amps, jnp.zeros_like(block_amps))
        return block_residual(masked_amps, domain_factors, core_float, domain_cycle)

    raw_blocks = lax.map(one_block, (blocks_flat, tiles_flat, counts_flat, row_numbers))
    raw_blocks = raw_blocks.reshape(N_ROW, N_COL, OCC, OCC, DV, DV)
    mirror_blocks = jnp.roll(raw_blocks, N_COL // 2, axis=1)
    residual = raw_blocks + jnp.transpose(mirror_blocks, (0, 1, 3, 2, 5, 4))

    def finish(packed):
        block_residual_sym, block_amps, tile_list, live_count, block_occ = packed
        row_mask, window_index = domain_setup(tile_list, live_count)
        pair_mask = row_mask[:, None] & row_mask[None, :]
        masked_amps = jnp.where(pair_mask, block_amps, jnp.zeros_like(block_amps))
        virt_levels = virt_energy[window_index]
        denominator = block_occ[0][:, None, None, None] + block_occ[1][None, :, None, None] - virt_levels[None, None, :, None] - virt_levels[None, None, None, :]
        return (masked_amps.astype(jnp.float32) + block_residual_sym / denominator).astype(jnp.bfloat16)

    updated = lax.map(finish, (residual.reshape(N_ROW * N_COL, OCC, OCC, DV, DV), blocks_flat, tiles_flat, counts_flat, occ_energy.reshape(N_ROW * N_COL, 2, OCC)))
    return residual, updated.reshape(N_ROW, N_COL, OCC, OCC, DV, DV)
```

```python
import functools

import jax
import jax.numpy as jnp
from jax import lax
from jax.experimental import pallas as pl
from jax.experimental.pallas import tpu as pltpu
from jax.sharding import PartitionSpec as P

MESH = pl.DeviceIdType.MESH
VMEM_LIMIT = 56 * 1024 * 1024


def gather_kernel(x_ref, w_ref, xall_ref, wall_ref, wsend, wrecv, xsend, xrecv, local):
    r = lax.axis_index("row")
    c = lax.axis_index("col")
    rows = lax.axis_size("row")
    cols = lax.axis_size("col")
    forth = (c + 4) % cols
    back = (c + cols - 4) % cols
    zside = c + 2 - 4 * ((c // 2) % 2)
    twin = c + 1 - 2 * (c % 2)
    core = c % 2

    barrier = pltpu.get_barrier_semaphore()
    for other in (forth, back, zside, twin):
        pl.semaphore_signal(barrier, inc=1, device_id=(r, other), device_id_type=MESH)
    for step in range(1, rows):
        pl.semaphore_signal(barrier, inc=1, device_id=((r + step) % rows, c), device_id_type=MESH)
    pl.semaphore_wait(barrier, 4 + rows - 1)

    started = []

    def send(src, dst, sems, index, device):
        copy = pltpu.make_async_remote_copy(
            src_ref=src, dst_ref=dst, send_sem=sems[0].at[index], recv_sem=sems[1].at[index],
            device_id=device, device_id_type=MESH,
        )
        copy.start()
        started.append(copy)

    def arrived(dst, sems, index):
        pltpu.make_async_remote_copy(
            src_ref=dst, dst_ref=dst, send_sem=sems[0].at[index], recv_sem=sems[1].at[index],
            device_id=(r, twin), device_id_type=MESH,
        ).wait_recv()

    wsems = (wsend, wrecv)
    xsems = (xsend, xrecv)
    half = w_ref.shape[0] // 2

    def shard(offset, plane, side):
        x = (c // 4 + offset) % (cols // 4)
        z = (c // 2) % 2
        z = z + plane * (1 - 2 * z)
        k = core + side * (1 - 2 * core)
        return x * 4 + z * 2 + k

    send(w_ref, wall_ref.at[c], wsems, 0, (r, forth))
    send(w_ref, wall_ref.at[c], wsems, 1, (r, back))
    send(w_ref, wall_ref.at[c], wsems, 4, (r, zside))
    for step in range(1, rows):
        send(x_ref.at[core], xall_ref.at[r, core], xsems, step - 1, ((r + step) % rows, c))
    send(w_ref, wall_ref.at[c], wsems, 8, (r, twin))
    own_w = pltpu.make_async_copy(w_ref, wall_ref.at[c], local.at[0])
    own_x = pltpu.make_async_copy(x_ref, xall_ref.at[r], local.at[1])
    own_w.start()
    own_x.start()

    slot = shard(3, 0, 0)
    arrived(wall_ref.at[slot], wsems, 0)
    send(wall_ref.at[slot, :half], wall_ref.at[slot, :half], wsems, 2, (r, forth))
    send(wall_ref.at[slot], wall_ref.at[slot], wsems, 7, (r, zside))
    send(wall_ref.at[slot], wall_ref.at[slot], wsems, 11, (r, twin))
    slot = shard(1, 0, 0)
    arrived(wall_ref.at[slot], wsems, 1)
    send(wall_ref.at[slot, half:], wall_ref.at[slot, half:], wsems, 3, (r, back))
    send(wall_ref.at[slot], wall_ref.at[slot], wsems, 5, (r, zside))
    send(wall_ref.at[slot], wall_ref.at[slot], wsems, 9, (r, twin))
    for step in range(1, rows):
        origin = (r + rows - step) % rows
        arrived(xall_ref.at[origin, core], xsems, step - 1)
        send(xall_ref.at[origin, core], xall_ref.at[origin, core], xsems, rows - 2 + step, (r, twin))
    slot = shard(2, 0, 0)
    arrived(wall_ref.at[slot, :half], wsems, 2)
    arrived(wall_ref.at[slot, half:], wsems, 3)
    send(wall_ref.at[slot], wall_ref.at[slot], wsems, 6, (r, zside))
    send(wall_ref.at[slot], wall_ref.at[slot], wsems, 10, (r, twin))
    for offset in (0, 3, 1, 2):
        slot = shard(offset, 1, 0)
        arrived(wall_ref.at[slot], wsems, 4 + offset)
        send(wall_ref.at[slot], wall_ref.at[slot], wsems, 12 + offset, (r, twin))
    for plane in range(2):
        for offset in range(4):
            arrived(wall_ref.at[shard(offset, plane, 1)], wsems, 8 + 4 * plane + offset)
    for step in range(1, rows):
        origin = (r + rows - step) % rows
        arrived(xall_ref.at[origin, 1 - core], xsems, rows - 2 + step)
    for copy in started:
        copy.wait_send()
    own_w.wait()
    own_x.wait()


def gather_parts(x_factor, cycle_shard):
    rows = lax.axis_size("row")
    cols = lax.axis_size("col")
    any_spec = pl.BlockSpec(memory_space=pl.ANY)
    return pl.pallas_call(
        gather_kernel,
        out_shape=(
            jax.ShapeDtypeStruct((rows,) + x_factor.shape, x_factor.dtype),
            jax.ShapeDtypeStruct((cols,) + cycle_shard.shape, cycle_shard.dtype),
        ),
        in_specs=[any_spec, any_spec],
        out_specs=(any_spec, any_spec),
        scratch_shapes=[
            pltpu.SemaphoreType.DMA((16,)),
            pltpu.SemaphoreType.DMA((16,)),
            pltpu.SemaphoreType.DMA((2 * (rows - 1),)),
            pltpu.SemaphoreType.DMA((2 * (rows - 1),)),
            pltpu.SemaphoreType.DMA((2,)),
        ],
        compiler_params=pltpu.CompilerParams(collective_id=0, has_side_effects=True),
        name="gather_parts",
    )(x_factor, cycle_shard)


def dot(a, b):
    return jnp.dot(a, b, preferred_element_type=jnp.float32)


def dot_nt(a, b):
    return lax.dot_general(a, b, (((1,), (1,)), ((), ())), preferred_element_type=jnp.float32)


STRIP = 256


def strips(width):
    return [pl.ds(start, STRIP) for start in range(0, width, STRIP)]


def own_kernel(
    tiles_ref, wall_ref, amps_ref, x_ref, xt_ref, core_ref, pick_ref, pickt_ref,
    wd_ref, wdt_ref, wt_ref, cyc_ref, wsel, proj, sem,
):
    slots = tiles_ref.shape[0]
    tile = wall_ref.shape[2]
    width = x_ref.shape[0]
    copies = []
    for s in range(slots):
        copy = pltpu.make_async_copy(
            wall_ref.at[tiles_ref[s]], wsel.at[:, pl.ds(s * tile, tile), :], sem.at[s]
        )
        copy.start()
        copies.append(copy)

    def own_ladder(p, carry):
        for rows in strips(width):
            proj[rows, :] = dot(xt_ref[rows, :], amps_ref[p]).astype(proj.dtype)
            inner = dot(proj[rows, :], x_ref[...])
            wt_ref[p, rows, :] = (core_ref[rows, :].astype(jnp.float32) * inner).astype(wt_ref.dtype)
        return carry

    lax.fori_loop(0, 4, own_ladder, 0)
    for copy in copies:
        copy.wait()

    def pick(p, carry):
        for rows in strips(width):
            wd_ref[p, rows, :] = dot(wsel[p, rows, :], pick_ref[...]).astype(wd_ref.dtype)
        for rows in strips(width):
            wdt_ref[p, rows, :] = dot_nt(pickt_ref[rows, :], wsel[p]).astype(wdt_ref.dtype)
        return carry

    lax.fori_loop(0, 4, pick, 0)

    def own_cycle(p, carry):
        i, j = p // 2, p % 2
        for rows in strips(width):
            cyc_ref[p, rows, :] = dot(wd_ref[2 * i, rows, :], amps_ref[j]) + dot(
                wd_ref[2 * i + 1, rows, :], amps_ref[2 + j]
            )
        return carry

    lax.fori_loop(0, 4, own_cycle, 0)


def own_terms(tile_list, wall, amp4, x, xt, core, pick, pickt):
    width, points = x.shape
    vmem = pl.BlockSpec(memory_space=pltpu.VMEM)
    square = (4, width, width)
    return pl.pallas_call(
        own_kernel,
        out_shape=(
            jax.ShapeDtypeStruct(square, jnp.bfloat16),
            jax.ShapeDtypeStruct(square, jnp.bfloat16),
            jax.ShapeDtypeStruct((4, points, points), jnp.bfloat16),
            jax.ShapeDtypeStruct(square, jnp.float32),
        ),
        in_specs=[pl.BlockSpec(memory_space=pltpu.SMEM), pl.BlockSpec(memory_space=pl.ANY)] + [vmem] * 6,
        out_specs=(vmem,) * 4,
        scratch_shapes=[
            pltpu.VMEM((4, width, wall.shape[3]), jnp.bfloat16),
            pltpu.VMEM((points, width), jnp.bfloat16),
            pltpu.SemaphoreType.DMA((tile_list.shape[0],)),
        ],
        compiler_params=pltpu.CompilerParams(vmem_limit_bytes=VMEM_LIMIT),
        name="own_terms",
    )(tile_list, wall, amp4, x, xt, core, pick, pickt)


def finish_kernel(
    first, occ_ref, vcol_ref, vrow_ref, mcol_ref, mrow_ref, *refs,
):
    (b0_hbm, b1_hbm, xt_hbm, x_hbm, coret_hbm, wt_hbm, wdt_hbm, cyc_hbm, amps_hbm) = refs[:9]
    res_hbm, upd_hbm = refs[-18:-16]
    (b0, b1, xt, x, coret, wt, wdt, cyc, amps, proj, total, spread, res, upd, sem, osem) = refs[-16:]
    width = x.shape[0]
    pairs = pl.ds(2 * first, 2)
    plan = {
        "b0": (b0_hbm, b0), "xt": (xt_hbm, xt), "x": (x_hbm, x), "coret": (coret_hbm, coret),
        "wt": (wt_hbm.at[pairs], wt), "b1": (b1_hbm, b1), "wdt": (wdt_hbm, wdt),
        "cyc": (cyc_hbm.at[pairs], cyc), "amps": (amps_hbm.at[pairs], amps),
    }
    loads = {}
    for at, (name, (src, dst)) in enumerate(plan.items()):
        loads[name] = pltpu.make_async_copy(src, dst, sem.at[at])
        loads[name].start()

    def need(*names):
        for name in names:
            if name in loads:
                loads.pop(name).wait()

    outs = []
    for j, b in enumerate((b0, b1)):
        need("b0" if j == 0 else "b1", "xt", "x", "coret", "wt")
        for rows in strips(width):
            proj[rows, :] = dot(xt[rows, :], b[...]).astype(proj.dtype)
            inner = dot(proj[rows, :], x[...])
            total[rows, :] = (
                wt[j, rows, :].astype(jnp.float32) + coret[rows, :].astype(jnp.float32) * inner
            ).astype(total.dtype)
        need("b1", "wdt", "cyc", "amps")
        for at, rows in enumerate(strips(width)):
            spread[rows, :] = dot(x[rows, :], total[...]).astype(spread.dtype)
            raw = (
                dot(spread[rows, :], xt[...])
                + dot(b0[rows, :], wdt[2 * j])
                + dot(b1[rows, :], wdt[2 * j + 1])
                + cyc[j, rows, :]
            )
            live = (mcol_ref[rows, :] * mrow_ref[...]) > 0.0
            raw = jnp.where(live, raw, 0.0)
            own = jnp.where(live, amps[j, rows, :].astype(jnp.float32), 0.0)
            gap = (occ_ref[0, first] + occ_ref[1, j]) - vcol_ref[rows, :] - vrow_ref[...]
            res[j, rows, :] = raw
            upd[j, rows, :] = (own + raw / gap).astype(upd.dtype)
            pair = 2 * first + j
            for k, (src, dst) in enumerate(((res, res_hbm), (upd, upd_hbm))):
                copy = pltpu.make_async_copy(
                    src.at[j, rows, :], dst.at[pair, rows, :], osem.at[k, j, at]
                )
                copy.start()
                outs.append(copy)
    for copy in outs:
        copy.wait()


def finish(first, occ, vcol, vrow, mcol, mrow, b0, b1, xt, x, coret, wt, wdt, cyc, amp4, before):
    width, points = x.shape
    vmem = pl.BlockSpec(memory_space=pltpu.VMEM)
    hbm = pl.BlockSpec(memory_space=pl.ANY)
    square = (4, width, width)
    bf16 = jnp.bfloat16
    operands = [occ, vcol, vrow, mcol, mrow, b0, b1, xt, x, coret, wt, wdt, cyc, amp4]
    alias = {}
    if before is not None:
        alias = {len(operands): 0, len(operands) + 1: 1}
        operands += list(before)
    return pl.pallas_call(
        functools.partial(finish_kernel, first),
        out_shape=(
            jax.ShapeDtypeStruct(square, jnp.float32),
            jax.ShapeDtypeStruct(square, bf16),
        ),
        in_specs=[pl.BlockSpec(memory_space=pltpu.SMEM)] + [vmem] * 4 + [hbm] * (len(operands) - 5),
        out_specs=(hbm, hbm),
        scratch_shapes=[
            pltpu.VMEM((width, width), bf16),
            pltpu.VMEM((width, width), bf16),
            pltpu.VMEM((points, width), bf16),
            pltpu.VMEM((width, points), bf16),
            pltpu.VMEM((points, points), bf16),
            pltpu.VMEM((2, points, points), bf16),
            pltpu.VMEM((4, width, width), bf16),
            pltpu.VMEM((2, width, width), jnp.float32),
            pltpu.VMEM((2, width, width), bf16),
            pltpu.VMEM((points, width), bf16),
            pltpu.VMEM((points, points), bf16),
            pltpu.VMEM((width, points), bf16),
            pltpu.VMEM((2, width, width), jnp.float32),
            pltpu.VMEM((2, width, width), bf16),
            pltpu.SemaphoreType.DMA((9,)),
            pltpu.SemaphoreType.DMA((2, 2, width // STRIP)),
        ],
        input_output_aliases=alias,
        compiler_params=pltpu.CompilerParams(vmem_limit_bytes=VMEM_LIMIT),
        name="finish_%d" % first,
    )(*operands)


def per_device(
    amps, x_factor, core, cycle_w, domain_tiles, domain_count, tile_slot, occ_energy, virt_energy
):
    occ = amps.shape[2]
    width = amps.shape[4]
    slot_count = domain_tiles.shape[2]
    tile_width = x_factor.shape[1]
    grid_points = x_factor.shape[2]
    window = cycle_w.shape[4]
    cols = lax.axis_size("col")
    mirror = [(i, (i + cols // 2) % cols) for i in range(cols)]
    amp = amps[0, 0]
    amp4 = amp.reshape(occ * occ, width, width)

    turned = [[jnp.transpose(amp[j, i]) for j in range(occ)] for i in range(occ)]
    pieces = [[lax.ppermute(turned[i][j], "col", mirror) for j in range(occ)] for i in range(occ)]

    shard = cycle_w[0].reshape(occ * occ, tile_width, window)
    shard, _ = lax.optimization_barrier((shard, turned))
    xall, wall = gather_parts(x_factor, shard)
    xall = xall.reshape(-1, tile_width, grid_points)

    tile_list = domain_tiles[0, 0]
    live_slots = jnp.arange(slot_count, dtype=jnp.int32) < domain_count[0, 0]
    row_live = jnp.repeat(live_slots, tile_width)
    window_index = (
        tile_list[:, None] * tile_width + jnp.arange(tile_width, dtype=jnp.int32)[None, :]
    ).reshape(width)
    picked = jnp.where(row_live, window_index, -1)
    window_at = jnp.arange(window, dtype=jnp.int32)
    pick = (window_at[:, None] == picked[None, :]).astype(jnp.bfloat16)
    pickt = (picked[:, None] == window_at[None, :]).astype(jnp.bfloat16)
    virt_levels = virt_energy[window_index]
    mask = row_live.astype(jnp.float32)

    x = xall[tile_slot[tile_list]].reshape(width, grid_points)
    x = jnp.where(row_live[:, None], x, jnp.zeros_like(x))
    xt = jnp.transpose(x)
    coret = jnp.transpose(core)

    wd, wdt, wt, cyc = own_terms(tile_list, wall, amp4, x, xt, core, pick, pickt)
    out = None
    for i in range(occ):
        out = finish(
            i, occ_energy[0, 0], virt_levels[:, None], virt_levels[None, :], mask[:, None], mask[None, :],
            pieces[i][0], pieces[i][1], xt, x, coret, wt, wdt, cyc, amp4, out,
        )
    residual, updated = out
    return residual.reshape(amps.shape), updated.reshape(amps.shape)


def solution(mesh):
    in_specs = (
        P("row", "col", None, None, None, None),
        P("row", None, None),
        P(),
        P("row", None, None, "col", None),
        P("row", "col", None),
        P("row", "col"),
        P(),
        P("row", "col", None, None),
        P(),
    )
    out_specs = (P("row", "col", None, None, None, None), P("row", "col", None, None, None, None))
    return jax.shard_map(
        per_device, mesh=mesh, in_specs=in_specs, out_specs=out_specs, check_vma=False
    )
```

```python
import functools

import jax
import jax.numpy as jnp
from jax import lax
from jax.experimental import pallas as pl
from jax.experimental.pallas import tpu as pltpu
from jax.sharding import PartitionSpec as P

MESH = pl.DeviceIdType.MESH
VMEM_LIMIT = 56 * 1024 * 1024
STRIP = 384


def dot(a, b):
    return jnp.dot(a, b, preferred_element_type=jnp.float32)


def dot_nt(a, b):
    return lax.dot_general(a, b, (((1,), (1,)), ((), ())), preferred_element_type=jnp.float32)


def strips(width, step):
    return [pl.ds(start, step) for start in range(0, width, step)]


def gather_kernel(
    x_ref, w_ref, amps_ref, xall_ref, wall_ref, far_ref, turned0_ref, turned1_ref, turned2_ref, turned3_ref,
    plain, turn, wsend, wrecv, xsend, xrecv, local, tsem,
):
    r = lax.axis_index("row")
    c = lax.axis_index("col")
    rows = lax.axis_size("row")
    cols = lax.axis_size("col")
    forth = (c + 4) % cols
    back = (c + cols - 4) % cols
    zside = c + 2 - 4 * ((c // 2) % 2)
    twin = c + 1 - 2 * (c % 2)
    core = c % 2
    half = w_ref.shape[0] // 2

    amps_in = pltpu.make_async_copy(amps_ref, plain, local.at[2])
    amps_in.start()

    barrier = pltpu.get_barrier_semaphore()
    for other in (forth, back, zside, twin):
        pl.semaphore_signal(barrier, inc=1, device_id=(r, other), device_id_type=MESH)
    for step in range(1, rows):
        pl.semaphore_signal(barrier, inc=1, device_id=((r + step) % rows, c), device_id_type=MESH)
    pl.semaphore_wait(barrier, 4 + rows - 1)

    started = []
    wsems = (wsend, wrecv)
    xsems = (xsend, xrecv)

    def send(src, dst, sems, index, device):
        copy = pltpu.make_async_remote_copy(
            src_ref=src, dst_ref=dst, send_sem=sems[0].at[index], recv_sem=sems[1].at[index],
            device_id=device, device_id_type=MESH,
        )
        copy.start()
        started.append(copy)

    def arrived(dst, sems, index):
        pltpu.make_async_remote_copy(
            src_ref=dst, dst_ref=dst, send_sem=sems[0].at[index], recv_sem=sems[1].at[index],
            device_id=(r, twin), device_id_type=MESH,
        ).wait_recv()

    def shard(offset, plane, side):
        x = (c // 4 + offset) % (cols // 4)
        z = (c // 2) % 2
        z = z + plane * (1 - 2 * z)
        k = core + side * (1 - 2 * core)
        return x * 4 + z * 2 + k

    send(w_ref, wall_ref.at[c], wsems, 0, (r, forth))
    send(w_ref, far_ref.at[0], wsems, 1, (r, back))
    send(w_ref, wall_ref.at[c], wsems, 4, (r, zside))
    for step in range(1, rows):
        send(x_ref.at[core], xall_ref.at[r, core], xsems, step - 1, ((r + step) % rows, c))
    send(w_ref, wall_ref.at[c], wsems, 6, (r, twin))
    own_w = pltpu.make_async_copy(w_ref, wall_ref.at[c], local.at[0])
    own_x = pltpu.make_async_copy(x_ref, xall_ref.at[r], local.at[1])
    own_w.start()
    own_x.start()

    turned_refs = (turned0_ref, turned1_ref, turned2_ref, turned3_ref)
    amps_in.wait()
    turned_out = []
    for p, q in enumerate((0, 2, 1, 3)):
        for cut in strips(turn.shape[1], 256):
            turn[p, :, cut] = plain[q, cut, :].T
        copy = pltpu.make_async_copy(turn.at[p], turned_refs[p], tsem.at[p])
        copy.start()
        turned_out.append(copy)

    slot = shard(3, 0, 0)
    arrived(wall_ref.at[slot], wsems, 0)
    send(wall_ref.at[slot, :half], far_ref.at[1, :half], wsems, 2, (r, forth))
    send(wall_ref.at[slot], wall_ref.at[slot], wsems, 5, (r, zside))
    send(wall_ref.at[slot], wall_ref.at[slot], wsems, 7, (r, twin))
    arrived(far_ref.at[0], wsems, 1)
    send(far_ref.at[0, half:], far_ref.at[1, half:], wsems, 3, (r, back))
    slot = shard(1, 0, 0)
    send(far_ref.at[0], wall_ref.at[slot], wsems, 8, (r, twin))
    slot = shard(0, 1, 0)
    arrived(wall_ref.at[slot], wsems, 4)
    send(wall_ref.at[slot], wall_ref.at[slot], wsems, 9, (r, twin))
    for step in range(1, rows):
        origin = (r + rows - step) % rows
        arrived(xall_ref.at[origin, core], xsems, step - 1)
        send(xall_ref.at[origin, core], xall_ref.at[origin, core], xsems, rows - 2 + step, (r, twin))
    arrived(far_ref.at[1, :half], wsems, 2)
    arrived(far_ref.at[1, half:], wsems, 3)
    slot = shard(2, 0, 0)
    send(far_ref.at[1], wall_ref.at[slot], wsems, 10, (r, twin))
    slot = shard(3, 1, 0)
    arrived(wall_ref.at[slot], wsems, 5)
    send(wall_ref.at[slot], wall_ref.at[slot], wsems, 11, (r, twin))
    for step in range(1, rows):
        origin = (r + rows - step) % rows
        arrived(xall_ref.at[origin, 1 - core], xsems, rows - 2 + step)
    arrived(wall_ref.at[shard(0, 0, 1)], wsems, 6)
    arrived(wall_ref.at[shard(3, 0, 1)], wsems, 7)
    arrived(wall_ref.at[shard(1, 0, 1)], wsems, 8)
    arrived(wall_ref.at[shard(0, 1, 1)], wsems, 9)
    arrived(wall_ref.at[shard(2, 0, 1)], wsems, 10)
    arrived(wall_ref.at[shard(3, 1, 1)], wsems, 11)
    for copy in started:
        copy.wait_send()
    own_w.wait()
    own_x.wait()
    for copy in turned_out:
        copy.wait()


def gather_parts(x_factor, cycle_shard, amp4):
    rows = lax.axis_size("row")
    cols = lax.axis_size("col")
    hbm = pl.BlockSpec(memory_space=pl.ANY)
    bf16 = jnp.bfloat16
    return pl.pallas_call(
        gather_kernel,
        out_shape=(
            jax.ShapeDtypeStruct((rows,) + x_factor.shape, bf16),
            jax.ShapeDtypeStruct((cols,) + cycle_shard.shape, bf16),
            jax.ShapeDtypeStruct((2,) + cycle_shard.shape, bf16),
        ) + (jax.ShapeDtypeStruct(amp4.shape[1:], bf16),) * 4,
        in_specs=[hbm] * 3,
        out_specs=(hbm,) * 7,
        scratch_shapes=[
            pltpu.VMEM(amp4.shape, bf16),
            pltpu.VMEM(amp4.shape, bf16),
            pltpu.SemaphoreType.DMA((12,)),
            pltpu.SemaphoreType.DMA((12,)),
            pltpu.SemaphoreType.DMA((2 * (rows - 1),)),
            pltpu.SemaphoreType.DMA((2 * (rows - 1),)),
            pltpu.SemaphoreType.DMA((3,)),
            pltpu.SemaphoreType.DMA((4,)),
        ],
        compiler_params=pltpu.CompilerParams(
            collective_id=0, has_side_effects=True, vmem_limit_bytes=VMEM_LIMIT
        ),
        name="gather_parts",
    )(x_factor, cycle_shard, amp4)


def own_ladder_kernel(
    slots_ref, mask_ref, xall_ref, amps_ref, core_ref, x_ref, xt_ref, wt_ref, gathered, proj, sem
):
    tile = xall_ref.shape[1]
    copies = []
    for s in range(slots_ref.shape[0]):
        copy = pltpu.make_async_copy(
            xall_ref.at[slots_ref[s]], gathered.at[pl.ds(s * tile, tile), :], sem.at[s]
        )
        copy.start()
        copies.append(copy)
    for copy in copies:
        copy.wait()
    x_ref[...] = jnp.where(mask_ref[...] > 0.0, gathered[...].astype(jnp.float32), 0.0).astype(x_ref.dtype)
    for cut in strips(x_ref.shape[0], 256):
        xt_ref[:, cut] = x_ref[cut, :].T

    def one(p, carry):
        proj[...] = dot(xt_ref[...], amps_ref[p]).astype(proj.dtype)
        inner = dot(proj[...], x_ref[...])
        wt_ref[p] = (core_ref[...].astype(jnp.float32) * inner).astype(wt_ref.dtype)
        return carry

    lax.fori_loop(0, 4, one, 0)


def own_ladder(slots, mcol, xall, amp4, core):
    width = amp4.shape[1]
    points = core.shape[0]
    vmem = pl.BlockSpec(memory_space=pltpu.VMEM)
    smem = pl.BlockSpec(memory_space=pltpu.SMEM)
    bf16 = jnp.bfloat16
    return pl.pallas_call(
        own_ladder_kernel,
        out_shape=(
            jax.ShapeDtypeStruct((width, points), bf16),
            jax.ShapeDtypeStruct((points, width), bf16),
            jax.ShapeDtypeStruct((4, points, points), bf16),
        ),
        in_specs=[smem, vmem, pl.BlockSpec(memory_space=pl.ANY), vmem, vmem],
        out_specs=(vmem,) * 3,
        scratch_shapes=[
            pltpu.VMEM((width, points), bf16),
            pltpu.VMEM((points, width), bf16),
            pltpu.SemaphoreType.DMA((slots.shape[0],)),
        ],
        compiler_params=pltpu.CompilerParams(vmem_limit_bytes=VMEM_LIMIT),
        name="own_ladder",
    )(slots, mcol, xall, amp4, core)


def own_cycle_kernel(
    kind_ref, at_ref, picked_ref, wall_ref, far_ref, side_ref, twin_ref, amps_ref,
    wd_ref, cyc_ref, wsel, pick, sem,
):
    tile = wall_ref.shape[2]
    slots = kind_ref.shape[0]
    for s in range(slots):
        for kind, source in enumerate((wall_ref, far_ref, side_ref, twin_ref)):

            @pl.when(kind_ref[s] == kind)
            def _(s=s, source=source):
                pltpu.make_async_copy(
                    source.at[at_ref[s]], wsel.at[:, pl.ds(s * tile, tile), :], sem.at[s]
                ).start()

    window = lax.broadcasted_iota(jnp.int32, pick.shape, 0)
    pick[...] = jnp.where(window == picked_ref[...], 1.0, 0.0).astype(pick.dtype)
    for s in range(slots):
        pltpu.make_async_copy(
            wall_ref.at[0], wsel.at[:, pl.ds(s * tile, tile), :], sem.at[s]
        ).wait()

    def select(p, carry):
        wd_ref[p] = dot(wsel[p], pick[...]).astype(wd_ref.dtype)
        return carry

    lax.fori_loop(0, 4, select, 0)

    def one(p, carry):
        i, j = p // 2, p % 2
        cyc_ref[p] = dot(wd_ref[2 * i], amps_ref[j]) + dot(wd_ref[2 * i + 1], amps_ref[2 + j])
        return carry

    lax.fori_loop(0, 4, one, 0)


def own_cycle(kind, at, picked, wall, far, side, twin, amp4):
    width = amp4.shape[1]
    slots, window = kind.shape[0], wall.shape[3]
    vmem = pl.BlockSpec(memory_space=pltpu.VMEM)
    smem = pl.BlockSpec(memory_space=pltpu.SMEM)
    hbm = pl.BlockSpec(memory_space=pl.ANY)
    return pl.pallas_call(
        own_cycle_kernel,
        out_shape=(
            jax.ShapeDtypeStruct((4, width, width), jnp.bfloat16),
            jax.ShapeDtypeStruct((4, width, width), jnp.float32),
        ),
        in_specs=[smem, smem, vmem, hbm, hbm, hbm, hbm, vmem],
        out_specs=(vmem,) * 2,
        scratch_shapes=[
            pltpu.VMEM((4, width, window), jnp.bfloat16),
            pltpu.VMEM((window, width), jnp.bfloat16),
            pltpu.SemaphoreType.DMA((slots,)),
        ],
        compiler_params=pltpu.CompilerParams(vmem_limit_bytes=VMEM_LIMIT),
        name="own_cycle",
    )(kind, at, picked, wall, far, side, twin, amp4)


def piece_kernel(i, k, last, occ_ref, vcol_ref, vrow_ref, mcol_ref, mrow_ref, *refs):
    (b_hbm, xt_hbm, x_hbm, coret_hbm, wt_hbm, wd_hbm, amps_hbm, part_hbm) = refs[:8]
    (xt, coret, wt, right, left, part, amps, proj, total, upd, sem, osem) = refs[-12:]
    outs_at = refs[8:-12]
    res_hbm = outs_at[-2] if last else outs_at[-1]
    upd_hbm = outs_at[-1] if last else None
    width, points = x_hbm.shape
    head, rest = pl.ds(0, points), pl.ds(points, width)
    plan = {
        "b": (b_hbm, left.at[:, rest]),
        "xt": (xt_hbm, xt),
        "x": (x_hbm, right.at[k, :, head]),
        "coret": (coret_hbm, coret),
        "wt": (wt_hbm.at[2 * i + k], wt),
        "w0": (wd_hbm.at[k], right.at[0, :, rest]),
        "w1": (wd_hbm.at[2 + k], right.at[1, :, rest]),
        "part": (part_hbm.at[pl.ds(2 * i, 2)], part),
    }
    if last:
        plan["amps"] = (amps_hbm.at[pl.ds(2 * i, 2)], amps)
    loads = {}
    for at, (name, (src, dst)) in enumerate(plan.items()):
        loads[name] = pltpu.make_async_copy(src, dst, sem.at[at])
        loads[name].start()

    outs = []

    def put(src, dst, at):
        copy = pltpu.make_async_copy(src, dst, osem.at[at])
        copy.start()
        outs.append(copy)

    def emit(j, rows, at, raw):
        raw = raw + part[j, rows, :]
        pair = 2 * i + j
        if last:
            live = (mcol_ref[rows, :] * mrow_ref[...]) > 0.0
            raw = jnp.where(live, raw, 0.0)
            own = jnp.where(live, amps[j, rows, :].astype(jnp.float32), 0.0)
            gap = (occ_ref[0, i] + occ_ref[1, j]) - vcol_ref[rows, :] - vrow_ref[...]
            upd[j, rows, :] = (own + raw / gap).astype(upd.dtype)
            put(upd.at[j, rows, :], upd_hbm.at[pair, rows, :], 4 + 2 * j + at)
        part[j, rows, :] = raw
        put(part.at[j, rows, :], res_hbm.at[pair, rows, :], 2 * j + at)

    loads["b"].wait()
    loads["xt"].wait()
    proj[...] = dot(xt[...], left[:, rest]).astype(proj.dtype)
    loads["x"].wait()
    loads["coret"].wait()
    loads["wt"].wait()
    inner = dot(proj[...], right[k, :, head])
    total[...] = (wt[...].astype(jnp.float32) + coret[...].astype(jnp.float32) * inner).astype(total.dtype)
    for name in ("w0", "w1", "part", "amps"):
        if name in loads:
            loads[name].wait()
    other = 1 - k
    for at, rows in enumerate(strips(width, STRIP)):
        emit(other, rows, at, dot_nt(left[rows, rest], right[other, :, rest]))
    left[:, head] = dot(right[k, :, head], total[...]).astype(left.dtype)
    for at, rows in enumerate(strips(width, STRIP)):
        emit(k, rows, at, dot_nt(left[rows, :], right[k]))
    for copy in outs:
        copy.wait()


def piece(i, k, occ, vcol, vrow, mcol, mrow, b, xt, x, coret, wt, wd, amp4, part, updated):
    width, points = x.shape
    last = k == 1
    vmem = pl.BlockSpec(memory_space=pltpu.VMEM)
    hbm = pl.BlockSpec(memory_space=pl.ANY)
    f32, bf16 = jnp.float32, jnp.bfloat16
    operands = [occ, vcol, vrow, mcol, mrow, b, xt, x, coret, wt, wd, amp4, part]
    out_shape = [jax.ShapeDtypeStruct(part.shape, f32)]
    alias = {len(operands) - 1: 0}
    if last:
        out_shape.append(jax.ShapeDtypeStruct(part.shape, bf16))
        if updated is not None:
            alias[len(operands)] = 1
            operands.append(updated)
    return pl.pallas_call(
        functools.partial(piece_kernel, i, k, last),
        out_shape=out_shape,
        in_specs=[pl.BlockSpec(memory_space=pltpu.SMEM)] + [vmem] * 4 + [hbm] * (len(operands) - 5),
        out_specs=[hbm] * len(out_shape),
        scratch_shapes=[
            pltpu.VMEM((points, width), bf16),
            pltpu.VMEM((points, points), bf16),
            pltpu.VMEM((points, points), bf16),
            pltpu.VMEM((2, width, points + width), bf16),
            pltpu.VMEM((width, points + width), bf16),
            pltpu.VMEM((2, width, width), f32),
            pltpu.VMEM((2, width, width), bf16),
            pltpu.VMEM((points, width), bf16),
            pltpu.VMEM((points, points), bf16),
            pltpu.VMEM((2, width, width), bf16),
            pltpu.SemaphoreType.DMA((9,)),
            pltpu.SemaphoreType.DMA((8,)),
        ],
        input_output_aliases=alias,
        compiler_params=pltpu.CompilerParams(vmem_limit_bytes=VMEM_LIMIT),
        name="piece_%d%d" % (i, k),
    )(*operands)


def per_device(
    amps, x_factor, core, cycle_w, domain_tiles, domain_count, tile_slot, occ_energy, virt_energy
):
    occ = amps.shape[2]
    width = amps.shape[4]
    slot_count = domain_tiles.shape[2]
    tile_width = x_factor.shape[1]
    grid_points = x_factor.shape[2]
    window = cycle_w.shape[4]
    cols = lax.axis_size("col")
    amp4 = amps[0, 0].reshape(occ * occ, width, width)
    shard = cycle_w[0].reshape(occ * occ, tile_width, window)
    xall, wall, far, *turned = gather_parts(x_factor, shard, amp4)
    xall = xall.reshape(-1, tile_width, grid_points)

    side = lax.ppermute(far, "col", [(i, i ^ 2) for i in range(cols)])
    mirror = [(i, (i + cols // 2) % cols) for i in range(cols)]
    pieces = [lax.ppermute(turned[p], "col", mirror) for p in range(occ * occ)]

    tile_list, count, tile_slot, virt_energy, core, _ = lax.optimization_barrier(
        (domain_tiles[0, 0], domain_count[0, 0], tile_slot, virt_energy, core, turned)
    )
    live_slots = jnp.arange(slot_count, dtype=jnp.int32) < count
    row_live = jnp.repeat(live_slots, tile_width)
    window_index = (
        tile_list[:, None] * tile_width + jnp.arange(tile_width, dtype=jnp.int32)[None, :]
    ).reshape(width)
    picked = jnp.where(row_live, window_index, -1)[None, :]
    virt_levels = virt_energy[window_index]
    mask = row_live.astype(jnp.float32)
    vcol, vrow, mcol, mrow = virt_levels[:, None], virt_levels[None, :], mask[:, None], mask[None, :]
    coret = jnp.transpose(core)

    me = lax.axis_index("col")
    offset = (tile_list // 4 + cols // 4 - me // 4) % (cols // 4)
    same_plane = (tile_list // 2) % 2 == (me // 2) % 2
    same_core = tile_list % 2 == me % 2
    apart = (offset == 1) | (offset == 2)
    kind = jnp.where(
        apart & same_core,
        jnp.where(same_plane, 1, 2),
        jnp.where(apart & ~same_plane, 3, 0),
    ).astype(jnp.int32)
    at = jnp.where(kind == 0, tile_list, offset - 1).astype(jnp.int32)

    x, xt, wt = own_ladder(tile_slot[tile_list], mcol, xall, amp4, core)
    side, wt = lax.optimization_barrier((side, wt))
    twin = lax.ppermute(side, "col", [(i, i ^ 1) for i in range(cols)])
    wd, part = own_cycle(kind, at, picked, wall, far, side, twin, amp4)
    updated = None
    for i in range(occ):
        for k in range(occ):
            out = piece(
                i, k, occ_energy[0, 0], vcol, vrow, mcol, mrow,
                pieces[occ * i + k], xt, x, coret, wt, wd, amp4, part, updated,
            )
            part = out[0]
        updated = out[1]
    return part.reshape(amps.shape), updated.reshape(amps.shape)


def solution(mesh):
    in_specs = (
        P("row", "col", None, None, None, None),
        P("row", None, None),
        P(),
        P("row", None, None, "col", None),
        P("row", "col", None),
        P("row", "col"),
        P(),
        P("row", "col", None, None),
        P(),
    )
    out_specs = (P("row", "col", None, None, None, None), P("row", "col", None, None, None, None))
    return jax.shard_map(
        per_device, mesh=mesh, in_specs=in_specs, out_specs=out_specs, check_vma=False
    )
```

```python
import functools

import jax
import jax.numpy as jnp
from jax import lax
from jax.experimental import pallas as pl
from jax.experimental.pallas import tpu as pltpu
from jax.sharding import PartitionSpec as P

MESH = pl.DeviceIdType.MESH
VMEM_LIMIT = 56 * 1024 * 1024
STRIP = 384


def dot(a, b):
    return jnp.dot(a, b, preferred_element_type=jnp.float32)


def dot_nt(a, b):
    return lax.dot_general(a, b, (((1,), (1,)), ((), ())), preferred_element_type=jnp.float32)


def strips(width, step):
    return [pl.ds(start, step) for start in range(0, width, step)]


def remote(src, dst, sems, index, device):
    return pltpu.make_async_remote_copy(
        src_ref=src, dst_ref=dst, send_sem=sems[0].at[index], recv_sem=sems[1].at[index],
        device_id=device, device_id_type=MESH,
    )


def greet(devices):
    barrier = pltpu.get_barrier_semaphore()
    for device in devices:
        pl.semaphore_signal(barrier, inc=1, device_id=device, device_id_type=MESH)
    pl.semaphore_wait(barrier, len(devices))


def gather_kernel(
    x_ref, w_ref, amps_ref, xall_ref, wall_ref, first_ref, *refs
):
    cuts, (plain, turned, wsend, wrecv, xsend, xrecv, msend, mrecv, local, tsem) = refs[:-10], refs[-10:]
    r = lax.axis_index("row")
    c = lax.axis_index("col")
    rows = lax.axis_size("row")
    cols = lax.axis_size("col")
    forth = (r, (c + 4) % cols)
    back = (r, (c + cols - 4) % cols)
    mirror = (r, (c + cols // 2) % cols)
    zside = (r, c + 2 - 4 * ((c // 2) % 2))
    twin = (r, c + 1 - 2 * (c % 2))
    beside = r + 1 - 2 * (r % 2)
    core = c % 2
    half = w_ref.shape[0] // 2
    width = plain.shape[1]
    y_steps = range(1, rows // 2)

    amps_in = [pltpu.make_async_copy(amps_ref.at[q], plain.at[q], tsem.at[q]) for q in range(4)]
    for copy in amps_in:
        copy.start()
    greet(
        [forth, back, mirror, zside, twin, (beside, c)]
        + [((r + 2 * step) % rows, c) for step in y_steps]
    )
    wsems, xsems = (wsend, wrecv), (xsend, xrecv)
    started = []

    def send(*args):
        copy = remote(*args)
        copy.start()
        started.append(copy)

    def arrived(part, sems, index):
        remote(part, part, sems, index, twin).wait_recv()

    def shard(offset, plane, side):
        x = (c // 4 + offset) % (cols // 4)
        z = (c // 2) % 2
        z = z + plane * (1 - 2 * z)
        k = core + side * (1 - 2 * core)
        return wall_ref.at[x * 4 + z * 2 + k]

    def pass_on(offset):
        part = shard(offset, 0, 0)
        send(part, part, wsems, 4 + offset, zside)
        send(part, part, wsems, 8 + offset, twin)

    def transpose(q, p):
        amps_in[q].wait()
        for cut in strips(width, 256):
            turned[p, :, cut] = plain[q, cut, :].T

    own = wall_ref.at[c]
    send(w_ref, own, wsems, 0, forth)
    send(w_ref, own, wsems, 1, back)
    send(w_ref, own, wsems, 4, zside)
    send(x_ref.at[core], xall_ref.at[r, core], xsems, 0, (beside, c))
    for step in y_steps:
        send(x_ref.at[core], xall_ref.at[r, core], xsems, step, ((r + 2 * step) % rows, c))
    send(w_ref, own, wsems, 8, twin)
    own_w = pltpu.make_async_copy(w_ref, own, local.at[0])
    own_x = pltpu.make_async_copy(x_ref, xall_ref.at[r], local.at[1])
    own_w.start()
    own_x.start()
    transpose(0, 0)

    part = xall_ref.at[beside, core]
    arrived(part, xsems, 0)
    for step in y_steps:
        send(part, part, xsems, 3 + step, ((r + 2 * step) % rows, c))
    send(part, part, xsems, 7, twin)

    arrived(shard(3, 0, 0), wsems, 0)
    part = shard(3, 0, 0).at[:half]
    send(part, part, wsems, 2, forth)
    arrived(shard(1, 0, 0), wsems, 1)
    part = shard(1, 0, 0).at[half:]
    send(part, part, wsems, 3, back)
    send(turned.at[0], first_ref, (msend, mrecv), 0, mirror)
    pass_on(3)
    pass_on(1)
    transpose(2, 1)
    for step in y_steps:
        origin = (r + rows - 2 * step) % rows
        arrived(xall_ref.at[origin, core], xsems, step)
        send(xall_ref.at[origin, core], xall_ref.at[origin, core], xsems, 7 + step, twin)
    transpose(1, 2)
    arrived(shard(2, 0, 0).at[:half], wsems, 2)
    arrived(shard(2, 0, 0).at[half:], wsems, 3)
    pass_on(2)
    transpose(3, 3)
    outs = [
        pltpu.make_async_copy(
            turned.at[p, :, pl.ds(low, out.shape[1])], out, local.at[2 + at]
        )
        for at, ((p, low), out) in enumerate(zip(((1, 0), (2, 0), (3, 0), (3, cuts[2].shape[1])), cuts))
    ]
    for copy in outs:
        copy.start()
    for step in y_steps:
        origin = (r + rows - 2 * step) % rows
        origin = origin + 1 - 2 * (origin % 2)
        arrived(xall_ref.at[origin, core], xsems, 3 + step)
        send(xall_ref.at[origin, core], xall_ref.at[origin, core], xsems, 10 + step, twin)
    for offset in (0, 3, 1, 2):
        part = shard(offset, 1, 0)
        arrived(part, wsems, 4 + offset)
        send(part, part, wsems, 12 + offset, twin)

    for offset in range(4):
        arrived(shard(offset, 0, 1), wsems, 8 + offset)
        arrived(shard(offset, 1, 1), wsems, 12 + offset)
    arrived(xall_ref.at[beside, 1 - core], xsems, 7)
    for step in y_steps:
        origin = (r + rows - 2 * step) % rows
        arrived(xall_ref.at[origin, 1 - core], xsems, 7 + step)
        origin = origin + 1 - 2 * (origin % 2)
        arrived(xall_ref.at[origin, 1 - core], xsems, 10 + step)
    remote(turned.at[0], first_ref, (msend, mrecv), 0, mirror).wait_recv()
    for copy in started:
        copy.wait_send()
    for copy in outs + [own_w, own_x]:
        copy.wait()


def gather_parts(x_factor, shard, amp4, split):
    rows = lax.axis_size("row")
    cols = lax.axis_size("col")
    width = amp4.shape[1]
    hbm = pl.BlockSpec(memory_space=pl.ANY)
    bf16 = jnp.bfloat16
    dma = pltpu.SemaphoreType.DMA
    shapes = [(rows,) + x_factor.shape, (cols,) + shard.shape] + [(width, width)] * 3
    shapes += [(width, split), (width, width - split)]
    return pl.pallas_call(
        gather_kernel,
        out_shape=[jax.ShapeDtypeStruct(shape, bf16) for shape in shapes],
        in_specs=[hbm] * 3,
        out_specs=[hbm] * len(shapes),
        scratch_shapes=[
            pltpu.VMEM(amp4.shape, bf16),
            pltpu.VMEM(amp4.shape, bf16),
            dma((16,)),
            dma((16,)),
            dma((14,)),
            dma((14,)),
            dma((1,)),
            dma((1,)),
            dma((6,)),
            dma((4,)),
        ],
        compiler_params=pltpu.CompilerParams(
            collective_id=0, has_side_effects=True, vmem_limit_bytes=VMEM_LIMIT
        ),
        name="gather_parts",
    )(x_factor, shard, amp4)


def own_ladder_kernel(
    slots_ref, mask_ref, xall_ref, amps_ref, core_ref, x_ref, xt_ref, wt_ref, gathered, proj, sem
):
    @pl.when(pl.program_id(0) == 0)
    def _():
        tile = xall_ref.shape[1]
        copies = []
        for s in range(slots_ref.shape[0]):
            copy = pltpu.make_async_copy(
                xall_ref.at[slots_ref[s]], gathered.at[pl.ds(s * tile, tile), :], sem.at[s]
            )
            copy.start()
            copies.append(copy)
        for copy in copies:
            copy.wait()
        x_ref[...] = jnp.where(
            mask_ref[...] > 0.0, gathered[...].astype(jnp.float32), 0.0
        ).astype(x_ref.dtype)
        for cut in strips(x_ref.shape[0], 256):
            xt_ref[:, cut] = x_ref[cut, :].T

    proj[...] = dot(xt_ref[...], amps_ref[0]).astype(proj.dtype)
    inner = dot(proj[...], x_ref[...])
    wt_ref[0] = (core_ref[...].astype(jnp.float32) * inner).astype(wt_ref.dtype)


def own_ladder(slots, mcol, xall, amp4, core):
    width = amp4.shape[1]
    points = core.shape[0]
    smem = pl.BlockSpec(memory_space=pltpu.SMEM)
    bf16 = jnp.bfloat16

    def whole(shape):
        return pl.BlockSpec(shape, lambda p: (0, 0))

    return pl.pallas_call(
        own_ladder_kernel,
        out_shape=(
            jax.ShapeDtypeStruct((width, points), bf16),
            jax.ShapeDtypeStruct((points, width), bf16),
            jax.ShapeDtypeStruct((4, points, points), bf16),
        ),
        grid=(4,),
        in_specs=[
            smem, whole((width, 1)), pl.BlockSpec(memory_space=pl.ANY),
            pl.BlockSpec((1, width, width), lambda p: (p, 0, 0)), whole((points, points)),
        ],
        out_specs=(
            whole((width, points)), whole((points, width)),
            pl.BlockSpec((1, points, points), lambda p: (p, 0, 0)),
        ),
        scratch_shapes=[
            pltpu.VMEM((width, points), bf16),
            pltpu.VMEM((points, width), bf16),
            pltpu.SemaphoreType.DMA((slots.shape[0],)),
        ],
        compiler_params=pltpu.CompilerParams(vmem_limit_bytes=VMEM_LIMIT),
        name="own_ladder",
    )(slots, mcol, xall, amp4, core)


def own_cycle_kernel(
    tiles_ref, picked_ref, wall_ref, a0_ref, a1_ref, wd_ref, cyc_ref, wsel, pick, sem
):
    p = pl.program_id(0)
    tile = wall_ref.shape[2]
    slots = tiles_ref.shape[0]

    def fetch(first, s):
        return pltpu.make_async_copy(
            wall_ref.at[tiles_ref[s], pl.ds(2 * first, 2)],
            wsel.at[pl.ds(2 * first, 2), pl.ds(s * tile, tile), :],
            sem.at[first, s],
        )

    @pl.when(p == 0)
    def _():
        for first in range(2):
            for s in range(slots):
                fetch(first, s).start()

        window = lax.broadcasted_iota(jnp.int32, pick.shape, 0)
        pick[...] = jnp.where(window == picked_ref[...], 1.0, 0.0).astype(pick.dtype)

    for first in range(2):

        @pl.when(p == 2 * first)
        def _(first=first):
            for s in range(slots):
                fetch(first, s).wait()
            for k in range(2):
                wd_ref[k] = dot(wsel[2 * first + k], pick[...]).astype(wd_ref.dtype)

    cyc_ref[0] = dot(wd_ref[0], a0_ref[0]) + dot(wd_ref[1], a1_ref[0])


def own_cycle(tiles, picked, wall, amp4):
    width = amp4.shape[1]
    slots, window = tiles.shape[0], wall.shape[3]
    smem = pl.BlockSpec(memory_space=pltpu.SMEM)
    hbm = pl.BlockSpec(memory_space=pl.ANY)
    return pl.pallas_call(
        own_cycle_kernel,
        out_shape=(
            jax.ShapeDtypeStruct((4, width, width), jnp.bfloat16),
            jax.ShapeDtypeStruct((4, width, width), jnp.float32),
        ),
        grid=(4,),
        in_specs=[
            smem,
            pl.BlockSpec((1, width), lambda p: (0, 0)),
            hbm,
            pl.BlockSpec((1, width, width), lambda p: (p % 2, 0, 0)),
            pl.BlockSpec((1, width, width), lambda p: (2 + p % 2, 0, 0)),
        ],
        out_specs=(
            pl.BlockSpec((2, width, width), lambda p: (p // 2, 0, 0)),
            pl.BlockSpec((1, width, width), lambda p: (p, 0, 0)),
        ),
        scratch_shapes=[
            pltpu.VMEM((4, width, window), jnp.bfloat16),
            pltpu.VMEM((window, width), jnp.bfloat16),
            pltpu.SemaphoreType.DMA((2, slots)),
        ],
        compiler_params=pltpu.CompilerParams(vmem_limit_bytes=VMEM_LIMIT),
        name="own_cycle",
    )(tiles, picked, wall, amp4, amp4)


def piece_kernel(i, k, low, high, end, occ_ref, vcol_ref, vrow_ref, mcol_ref, mrow_ref, *refs):
    last = k == 1 and end
    scratch = 13
    refs, (xt, coret, wt, right, left, part, amps, acc, proj, total, upd, sem, osem) = (
        refs[:-scratch], refs[-scratch:]
    )
    (b_hbm, xt_hbm, x_hbm, coret_hbm, wt_hbm, wd_hbm, amps_hbm, part_hbm) = refs[:8]
    refs = list(refs[8:])
    acc_in = refs.pop(0) if low > 0 else None
    if last:
        upd_hbm = refs.pop()
    acc_out = None if end else refs.pop()
    res_hbm = refs.pop()
    width, points = x_hbm.shape
    head, rest = pl.ds(0, points), pl.ds(points, high - low)
    cut = pl.ds(low, high - low)
    plan = {
        "b": (b_hbm, left.at[:, rest]),
        "xt": (xt_hbm, xt),
        "x": (x_hbm, right.at[k, :, head]),
    }
    if low > 0:
        plan["acc"] = (acc_in, acc)
    if end:
        plan["coret"] = (coret_hbm, coret)
        plan["wt"] = (wt_hbm.at[2 * i + k], wt)
    plan["w0"] = (wd_hbm.at[k, :, cut], right.at[0, :, rest])
    plan["w1"] = (wd_hbm.at[2 + k, :, cut], right.at[1, :, rest])
    plan["part"] = (part_hbm.at[pl.ds(2 * i, 2)], part)
    if last:
        plan["amps"] = (amps_hbm.at[pl.ds(2 * i, 2)], amps)
    loads = {}
    for at, (name, (src, dst)) in enumerate(plan.items()):
        loads[name] = pltpu.make_async_copy(src, dst, sem.at[at])
        loads[name].start()

    def need(*names):
        for name in names:
            if name in loads:
                loads.pop(name).wait()

    outs = []

    def put(src, dst, at):
        copy = pltpu.make_async_copy(src, dst, osem.at[at])
        copy.start()
        outs.append(copy)

    def emit(j, rows, at, raw):
        raw = raw + part[j, rows, :]
        pair = 2 * i + j
        if last:
            live = (mcol_ref[rows, :] * mrow_ref[...]) > 0.0
            raw = jnp.where(live, raw, 0.0)
            own = jnp.where(live, amps[j, rows, :].astype(jnp.float32), 0.0)
            gap = (occ_ref[0, i] + occ_ref[1, j]) - vcol_ref[rows, :] - vrow_ref[...]
            upd[j, rows, :] = (own + raw / gap).astype(upd.dtype)
            put(upd.at[j, rows, :], upd_hbm.at[pair, rows, :], 4 + 2 * j + at)
        part[j, rows, :] = raw
        put(part.at[j, rows, :], res_hbm.at[pair, rows, :], 2 * j + at)

    def cycle_alone(j):
        for at, rows in enumerate(strips(width, STRIP)):
            emit(j, rows, at, dot_nt(left[rows, rest], right[j, :, rest]))

    need("b", "xt")
    proj[...] = dot(xt[...], left[:, rest]).astype(proj.dtype)
    need("x", "acc", "coret", "wt")
    inner = dot(proj[...], right[k, cut, head])
    if low > 0:
        inner = inner + acc[...]
    if end:
        total[...] = (
            wt[...].astype(jnp.float32) + coret[...].astype(jnp.float32) * inner
        ).astype(total.dtype)
        need("w0", "w1", "part", "amps")
        cycle_alone(1 - k)
        left[:, head] = dot(right[k, :, head], total[...]).astype(left.dtype)
        for at, rows in enumerate(strips(width, STRIP)):
            emit(k, rows, at, dot_nt(left[rows, :], right[k]))
    else:
        acc[...] = inner
        put(acc, acc_out, 8)
        need("w0", "w1", "part")
        for j in range(2):
            cycle_alone(j)
    for copy in outs:
        copy.wait()


def piece(i, k, low, high, occ, vcol, vrow, mcol, mrow, b, xt, x, coret, wt, wd, amp4, part, acc, updated):
    width, points = x.shape
    end = high == width
    last = k == 1 and end
    vmem = pl.BlockSpec(memory_space=pltpu.VMEM)
    hbm = pl.BlockSpec(memory_space=pl.ANY)
    f32, bf16 = jnp.float32, jnp.bfloat16
    operands = [occ, vcol, vrow, mcol, mrow, b, xt, x, coret, wt, wd, amp4, part]
    out_shape = [jax.ShapeDtypeStruct(part.shape, f32)]
    alias = {len(operands) - 1: 0}
    if low > 0:
        operands.append(acc)
    if not end:
        out_shape.append(jax.ShapeDtypeStruct((points, points), f32))
    if last:
        out_shape.append(jax.ShapeDtypeStruct(part.shape, bf16))
        if updated is not None:
            alias[len(operands)] = 1
            operands.append(updated)
    return pl.pallas_call(
        functools.partial(piece_kernel, i, k, low, high, end),
        out_shape=out_shape,
        in_specs=[pl.BlockSpec(memory_space=pltpu.SMEM)] + [vmem] * 4 + [hbm] * (len(operands) - 5),
        out_specs=[hbm] * len(out_shape),
        scratch_shapes=[
            pltpu.VMEM((points, width), bf16),
            pltpu.VMEM((points, points), bf16),
            pltpu.VMEM((points, points), bf16),
            pltpu.VMEM((2, width, points + high - low), bf16),
            pltpu.VMEM((width, points + high - low), bf16),
            pltpu.VMEM((2, width, width), f32),
            pltpu.VMEM((2, width, width), bf16),
            pltpu.VMEM((points, points), f32),
            pltpu.VMEM((points, high - low), bf16),
            pltpu.VMEM((points, points), bf16),
            pltpu.VMEM((2, width, width), bf16),
            pltpu.SemaphoreType.DMA((10,)),
            pltpu.SemaphoreType.DMA((9,)),
        ],
        input_output_aliases=alias,
        compiler_params=pltpu.CompilerParams(vmem_limit_bytes=VMEM_LIMIT),
        name="piece_%d%d_%d" % (i, k, low),
    )(*operands)


def per_device(
    amps, x_factor, core, cycle_w, domain_tiles, domain_count, tile_slot, occ_energy, virt_energy
):
    occ = amps.shape[2]
    width = amps.shape[4]
    slot_count = domain_tiles.shape[2]
    tile_width = x_factor.shape[1]
    grid_points = x_factor.shape[2]
    window = cycle_w.shape[4]
    cols = lax.axis_size("col")
    amp4 = amps[0, 0].reshape(occ * occ, width, width)
    shard = cycle_w[0].reshape(occ * occ, tile_width, window)

    split = 512
    xall, wall, first, *turned = gather_parts(x_factor, shard, amp4, split)
    xall = xall.reshape(-1, tile_width, grid_points)
    mirror = [(i, (i + cols // 2) % cols) for i in range(cols)]

    def send_piece(i, k, low, high, part):
        return i, k, low, high, lax.ppermute(part, "col", mirror)

    pieces = [
        (0, 0, 0, width, first),
        send_piece(0, 1, 0, width, turned[0]),
        send_piece(1, 0, 0, width, turned[1]),
        send_piece(1, 1, 0, split, turned[2]),
    ]

    tile_list, count, tile_slot, virt_energy, core, _ = lax.optimization_barrier(
        (domain_tiles[0, 0], domain_count[0, 0], tile_slot, virt_energy, core, turned)
    )
    live_slots = jnp.arange(slot_count, dtype=jnp.int32) < count
    row_live = jnp.repeat(live_slots, tile_width)
    window_index = (
        tile_list[:, None] * tile_width + jnp.arange(tile_width, dtype=jnp.int32)[None, :]
    ).reshape(width)
    picked = jnp.where(row_live, window_index, -1)[None, :]
    virt_levels = virt_energy[window_index]
    mask = row_live.astype(jnp.float32)
    vcol, vrow, mcol, mrow = virt_levels[:, None], virt_levels[None, :], mask[:, None], mask[None, :]
    coret = jnp.transpose(core)

    x, xt, wt = own_ladder(tile_slot[tile_list], mcol, xall, amp4, core)
    tail, wt = lax.optimization_barrier((turned[3], wt))
    pieces.append(send_piece(1, 1, split, width, tail))
    picked, wt = lax.optimization_barrier((picked, wt))
    wd, part = own_cycle(tile_list, picked, wall, amp4)
    updated = acc = None
    for i, k, low, high, b in pieces:
        out = piece(
            i, k, low, high, occ_energy[0, 0], vcol, vrow, mcol, mrow,
            b, xt, x, coret, wt, wd, amp4, part, acc, updated,
        )
        part = out[0]
        if high < width:
            acc = out[1]
        elif k == 1:
            updated = out[1]
    return part.reshape(amps.shape), updated.reshape(amps.shape)


def solution(mesh):
    in_specs = (
        P("row", "col", None, None, None, None),
        P("row", None, None),
        P(),
        P("row", None, None, "col", None),
        P("row", "col", None),
        P("row", "col"),
        P(),
        P("row", "col", None, None),
        P(),
    )
    out_specs = (P("row", "col", None, None, None, None), P("row", "col", None, None, None, None))
    return jax.shard_map(
        per_device, mesh=mesh, in_specs=in_specs, out_specs=out_specs, check_vma=False
    )
```

```python
import functools

import jax
import jax.numpy as jnp
from jax import lax
from jax.experimental import pallas as pl
from jax.experimental.pallas import tpu as pltpu
from jax.sharding import PartitionSpec as P

MESH = pl.DeviceIdType.MESH
VMEM_LIMIT = 56 * 1024 * 1024
STRIP = 384


def dot(a, b):
    return jnp.dot(a, b, preferred_element_type=jnp.float32)


def dot_nt(a, b):
    return lax.dot_general(a, b, (((1,), (1,)), ((), ())), preferred_element_type=jnp.float32)


def strips(width, step):
    return [pl.ds(start, step) for start in range(0, width, step)]


def remote(src, dst, sems, index, device):
    return pltpu.make_async_remote_copy(
        src_ref=src, dst_ref=dst, send_sem=sems[0].at[index], recv_sem=sems[1].at[index],
        device_id=device, device_id_type=MESH,
    )


def greet(devices):
    barrier = pltpu.get_barrier_semaphore()
    for device in devices:
        pl.semaphore_signal(barrier, inc=1, device_id=device, device_id_type=MESH)
    pl.semaphore_wait(barrier, len(devices))


def gather_kernel(
    x_ref, w_ref, amps_ref, core_ref, xall_ref, wall_ref, far_ref, first_ref, coret_ref, *refs
):
    cuts, (plain, turned, fixed, wsend, wrecv, xsend, xrecv, msend, mrecv, local, tsem) = refs[:-11], refs[-11:]
    r = lax.axis_index("row")
    c = lax.axis_index("col")
    rows = lax.axis_size("row")
    cols = lax.axis_size("col")
    forth = (r, (c + 4) % cols)
    back = (r, (c + cols - 4) % cols)
    mirror = (r, (c + cols // 2) % cols)
    zside = (r, c + 2 - 4 * ((c // 2) % 2))
    twin = (r, c + 1 - 2 * (c % 2))
    beside = r + 1 - 2 * (r % 2)
    core = c % 2
    half = w_ref.shape[0] // 2
    width = plain.shape[1]
    y_steps = range(1, rows // 2)

    amps_in = [pltpu.make_async_copy(amps_ref.at[q], plain.at[q], tsem.at[q]) for q in range(4)]
    core_in = pltpu.make_async_copy(core_ref, fixed.at[0], tsem.at[4])
    for copy in amps_in + [core_in]:
        copy.start()
    greet(
        [forth, back, mirror, zside, twin, (beside, c)]
        + [((r + 2 * step) % rows, c) for step in y_steps]
    )
    wsems, xsems = (wsend, wrecv), (xsend, xrecv)
    started = []

    def send(*args):
        copy = remote(*args)
        copy.start()
        started.append(copy)

    def arrived(part, sems, index):
        remote(part, part, sems, index, twin).wait_recv()

    def shard(offset, plane, side):
        if offset in (1, 2) and plane + side == 0:
            return far_ref.at[offset - 1]
        x = (c // 4 + offset) % (cols // 4)
        z = (c // 2) % 2
        z = z + plane * (1 - 2 * z)
        k = core + side * (1 - 2 * core)
        return wall_ref.at[x * 4 + z * 2 + k]

    def to_twin(offset):
        x = (c // 4 + offset) % (cols // 4)
        send(shard(offset, 0, 0), wall_ref.at[x * 4 + c % 4], wsems, 6 + offset, twin)

    def transpose(q, p):
        amps_in[q].wait()
        for cut in strips(width, 256):
            turned[p, :, cut] = plain[q, cut, :].T

    own = wall_ref.at[c]
    send(w_ref, own, wsems, 0, forth)
    send(w_ref, far_ref.at[0], wsems, 1, back)
    send(w_ref, own, wsems, 4, zside)
    send(x_ref.at[core], xall_ref.at[r, core], xsems, 0, (beside, c))
    for step in y_steps:
        send(x_ref.at[core], xall_ref.at[r, core], xsems, step, ((r + 2 * step) % rows, c))
    send(w_ref, own, wsems, 6, twin)
    own_w = pltpu.make_async_copy(w_ref, own, local.at[0])
    own_x = pltpu.make_async_copy(x_ref, xall_ref.at[r], local.at[1])
    own_w.start()
    own_x.start()
    transpose(0, 0)

    part = xall_ref.at[beside, core]
    arrived(part, xsems, 0)
    for step in y_steps:
        send(part, part, xsems, 3 + step, ((r + 2 * step) % rows, c))
    send(part, part, xsems, 7, twin)

    part = shard(3, 0, 0)
    arrived(part, wsems, 0)
    send(part.at[:half], far_ref.at[1, :half], wsems, 2, forth)
    send(part, part, wsems, 5, zside)
    arrived(far_ref.at[0], wsems, 1)
    send(far_ref.at[0, half:], far_ref.at[1, half:], wsems, 3, back)
    send(turned.at[0], first_ref, (msend, mrecv), 0, mirror)
    to_twin(3)
    to_twin(1)
    transpose(2, 1)
    for step in y_steps:
        origin = (r + rows - 2 * step) % rows
        arrived(xall_ref.at[origin, core], xsems, step)
        send(xall_ref.at[origin, core], xall_ref.at[origin, core], xsems, 7 + step, twin)
    transpose(1, 2)
    part = shard(0, 1, 0)
    arrived(part, wsems, 4)
    send(part, part, wsems, 10, twin)
    for step in y_steps:
        origin = (r + rows - 2 * step) % rows
        origin = origin + 1 - 2 * (origin % 2)
        arrived(xall_ref.at[origin, core], xsems, 3 + step)
        send(xall_ref.at[origin, core], xall_ref.at[origin, core], xsems, 10 + step, twin)
    arrived(far_ref.at[1, :half], wsems, 2)
    arrived(far_ref.at[1, half:], wsems, 3)
    to_twin(2)
    transpose(3, 3)
    outs = [
        pltpu.make_async_copy(
            turned.at[p, :, pl.ds(low, out.shape[1])], out, local.at[2 + at]
        )
        for at, ((p, low), out) in enumerate(zip(((1, 0), (2, 0), (3, 0), (3, cuts[2].shape[1])), cuts))
    ]
    core_in.wait()
    for cut in strips(width, 256):
        fixed[1, :, cut] = fixed[0, cut, :].T
    outs.append(pltpu.make_async_copy(fixed.at[1], coret_ref, local.at[6]))
    for copy in outs:
        copy.start()
    part = shard(3, 1, 0)
    arrived(part, wsems, 5)
    send(part, part, wsems, 11, twin)

    for offset in range(4):
        arrived(shard(offset, 0, 1), wsems, 6 + offset)
    arrived(shard(0, 1, 1), wsems, 10)
    arrived(shard(3, 1, 1), wsems, 11)
    arrived(xall_ref.at[beside, 1 - core], xsems, 7)
    for step in y_steps:
        origin = (r + rows - 2 * step) % rows
        arrived(xall_ref.at[origin, 1 - core], xsems, 7 + step)
        origin = origin + 1 - 2 * (origin % 2)
        arrived(xall_ref.at[origin, 1 - core], xsems, 10 + step)
    remote(turned.at[0], first_ref, (msend, mrecv), 0, mirror).wait_recv()
    for copy in started:
        copy.wait_send()
    for copy in outs + [own_w, own_x]:
        copy.wait()


def gather_parts(x_factor, shard, amp4, core, split):
    rows = lax.axis_size("row")
    cols = lax.axis_size("col")
    width = amp4.shape[1]
    hbm = pl.BlockSpec(memory_space=pl.ANY)
    bf16 = jnp.bfloat16
    dma = pltpu.SemaphoreType.DMA
    shapes = [(rows,) + x_factor.shape, (cols,) + shard.shape, (2,) + shard.shape, (width, width), core.shape]
    shapes += [(width, width)] * 2
    shapes += [(width, split), (width, width - split)]
    return pl.pallas_call(
        gather_kernel,
        out_shape=[jax.ShapeDtypeStruct(shape, bf16) for shape in shapes],
        in_specs=[hbm] * 4,
        out_specs=[hbm] * len(shapes),
        scratch_shapes=[
            pltpu.VMEM(amp4.shape, bf16),
            pltpu.VMEM(amp4.shape, bf16),
            pltpu.VMEM((2,) + core.shape, bf16),
            dma((12,)),
            dma((12,)),
            dma((14,)),
            dma((14,)),
            dma((1,)),
            dma((1,)),
            dma((7,)),
            dma((5,)),
        ],
        compiler_params=pltpu.CompilerParams(
            collective_id=0, has_side_effects=True, vmem_limit_bytes=VMEM_LIMIT
        ),
        name="gather_parts",
    )(x_factor, shard, amp4, core)


def own_ladder_kernel(
    tiles_ref, count_ref, slot_ref, xall_ref, amps_ref, core_ref, x_ref, xt_ref, wt_ref, gathered, proj, sem
):
    @pl.when(pl.program_id(0) == 0)
    def _():
        tile = xall_ref.shape[1]
        copies = []
        for s in range(tiles_ref.shape[0]):
            copy = pltpu.make_async_copy(
                xall_ref.at[slot_ref[tiles_ref[s]]], gathered.at[pl.ds(s * tile, tile), :], sem.at[s]
            )
            copy.start()
            copies.append(copy)
        for copy in copies:
            copy.wait()
        live = lax.broadcasted_iota(jnp.int32, (x_ref.shape[0], 1), 0) < count_ref[0, 0] * tile
        x_ref[...] = jnp.where(live, gathered[...].astype(jnp.float32), 0.0).astype(x_ref.dtype)
        for cut in strips(x_ref.shape[0], 256):
            xt_ref[:, cut] = x_ref[cut, :].T

    proj[...] = dot(xt_ref[...], amps_ref[0]).astype(proj.dtype)
    inner = dot(proj[...], x_ref[...])
    wt_ref[0] = (core_ref[...].astype(jnp.float32) * inner).astype(wt_ref.dtype)


def own_ladder(tiles, count, tile_slot, xall, amp4, core):
    width = amp4.shape[1]
    points = core.shape[0]
    smem = pl.BlockSpec(memory_space=pltpu.SMEM)
    bf16 = jnp.bfloat16

    def whole(shape):
        return pl.BlockSpec(shape, lambda p: (0, 0))

    return pl.pallas_call(
        own_ladder_kernel,
        out_shape=(
            jax.ShapeDtypeStruct((width, points), bf16),
            jax.ShapeDtypeStruct((points, width), bf16),
            jax.ShapeDtypeStruct((4, points, points), bf16),
        ),
        grid=(4,),
        in_specs=[
            smem, smem, smem, pl.BlockSpec(memory_space=pl.ANY),
            pl.BlockSpec((1, width, width), lambda p: (p, 0, 0)), whole((points, points)),
        ],
        out_specs=(
            whole((width, points)), whole((points, width)),
            pl.BlockSpec((1, points, points), lambda p: (p, 0, 0)),
        ),
        scratch_shapes=[
            pltpu.VMEM((width, points), bf16),
            pltpu.VMEM((points, width), bf16),
            pltpu.SemaphoreType.DMA((tiles.shape[0],)),
        ],
        compiler_params=pltpu.CompilerParams(vmem_limit_bytes=VMEM_LIMIT),
        name="own_ladder",
    )(tiles, count, tile_slot, xall, amp4, core)


def window_index(tiles_ref, count_ref, tile, shape, axis):
    at = lax.broadcasted_iota(jnp.int32, shape, axis)
    index = jnp.full(shape, -1, jnp.int32)
    for s in range(tiles_ref.shape[0]):
        inside = (at >= s * tile) & (at < (s + 1) * tile) & (s < count_ref[0, 0])
        index = jnp.where(inside, at + (tiles_ref[s] - s) * tile, index)
    return index


def own_cycle_kernel(
    tiles_ref, count_ref, virt_ref, wall_ref, far_ref, side_ref, twin_ref, a0_ref, a1_ref,
    wd_ref, cyc_ref, vcol_ref, vrow_ref, wsel, pick, sem,
):
    p = pl.program_id(0)
    tile = wall_ref.shape[2]
    slots = tiles_ref.shape[0]
    width = wd_ref.shape[1]
    window = virt_ref.shape[1]

    @pl.when(p == 0)
    def _():
        me = lax.axis_index("col")
        for first in range(2):
            for s in range(slots):
                number = tiles_ref[s]
                offset = ((number >> 2) + 4 - (me >> 2)) & 3
                plane = ((number >> 1) + (me >> 1)) & 1
                side = (number + me) & 1
                apart = (offset == 1) | (offset == 2)
                dst = wsel.at[pl.ds(2 * first, 2), pl.ds(s * tile, tile), :]

                def fetch(source, at, dst=dst, done=sem.at[first, s], first=first):
                    pltpu.make_async_copy(source.at[at, pl.ds(2 * first, 2)], dst, done).start()

                @pl.when(jnp.logical_not(apart) | ((plane == 0) & (side == 1)))
                def _(number=number, fetch=fetch):
                    fetch(wall_ref, number)

                for source, at_plane, at_side in ((far_ref, 0, 0), (side_ref, 1, 0), (twin_ref, 1, 1)):

                    @pl.when(apart & (plane == at_plane) & (side == at_side))
                    def _(source=source, offset=offset, fetch=fetch):
                        fetch(source, offset - 1)

        along = lax.broadcasted_iota(jnp.int32, pick.shape, 0)
        picked = window_index(tiles_ref, count_ref, tile, (1, width), 1)
        pick[...] = jnp.where(along == picked, 1.0, 0.0).astype(pick.dtype)
        picked = window_index(tiles_ref, count_ref, tile, (width, 1), 0)
        along = lax.broadcasted_iota(jnp.int32, (width, window), 1)
        levels = jnp.sum(jnp.where(along == picked, virt_ref[...], 0.0), axis=1, keepdims=True)
        vcol_ref[...] = levels
        vrow_ref[...] = jnp.broadcast_to(levels, (width, 128)).T[:1, :]

    for first in range(2):

        @pl.when(p == 2 * first)
        def _(first=first):
            for s in range(slots):
                pltpu.make_async_copy(
                    wall_ref.at[0, pl.ds(0, 2)],
                    wsel.at[pl.ds(2 * first, 2), pl.ds(s * tile, tile), :],
                    sem.at[first, s],
                ).wait()
            for k in range(2):
                wd_ref[k] = dot(wsel[2 * first + k], pick[...]).astype(wd_ref.dtype)

    cyc_ref[0] = dot(wd_ref[0], a0_ref[0]) + dot(wd_ref[1], a1_ref[0])


def own_cycle(tiles, count, virt, wall, far, side, twin, amp4):
    width = amp4.shape[1]
    slots, window = tiles.shape[0], wall.shape[3]
    smem = pl.BlockSpec(memory_space=pltpu.SMEM)
    hbm = pl.BlockSpec(memory_space=pl.ANY)
    f32, bf16 = jnp.float32, jnp.bfloat16
    return pl.pallas_call(
        own_cycle_kernel,
        out_shape=(
            jax.ShapeDtypeStruct((4, width, width), bf16),
            jax.ShapeDtypeStruct((4, width, width), f32),
            jax.ShapeDtypeStruct((width, 1), f32),
            jax.ShapeDtypeStruct((1, width), f32),
        ),
        grid=(4,),
        in_specs=[
            smem,
            smem,
            pl.BlockSpec((1, window), lambda p: (0, 0)),
            hbm,
            hbm,
            hbm,
            hbm,
            pl.BlockSpec((1, width, width), lambda p: (p % 2, 0, 0)),
            pl.BlockSpec((1, width, width), lambda p: (2 + p % 2, 0, 0)),
        ],
        out_specs=(
            pl.BlockSpec((2, width, width), lambda p: (p // 2, 0, 0)),
            pl.BlockSpec((1, width, width), lambda p: (p, 0, 0)),
            pl.BlockSpec((width, 1), lambda p: (0, 0)),
            pl.BlockSpec((1, width), lambda p: (0, 0)),
        ),
        scratch_shapes=[
            pltpu.VMEM((4, width, window), bf16),
            pltpu.VMEM((window, width), bf16),
            pltpu.SemaphoreType.DMA((2, slots)),
        ],
        compiler_params=pltpu.CompilerParams(vmem_limit_bytes=VMEM_LIMIT),
        name="own_cycle",
    )(tiles, count, virt, wall, far, side, twin, amp4, amp4)


class Mover:
    def __init__(self, plan, in_sem, out_sem):
        self.out_sem = out_sem
        self.outs = []
        self.loads = {}
        for at, (name, (src, dst)) in enumerate(plan.items()):
            self.loads[name] = pltpu.make_async_copy(src, dst, in_sem.at[at])
            self.loads[name].start()

    def need(self, *names):
        for name in names:
            if name in self.loads:
                self.loads.pop(name).wait()

    def put(self, src, dst):
        copy = pltpu.make_async_copy(src, dst, self.out_sem.at[len(self.outs)])
        copy.start()
        self.outs.append(copy)

    def drain(self):
        for copy in self.outs:
            copy.wait()


def emit(mover, last, pair, j, rows, raw, count_ref, occ_ref, vcol_ref, vrow_ref, part, amps, upd, res_hbm, upd_hbm):
    raw = raw + part[j, rows, :]
    if last:
        count = count_ref[0, 0] * 64
        height, width = raw.shape
        live = (lax.broadcasted_iota(jnp.int32, (height, 1), 0) + rows.start < count) & (
            lax.broadcasted_iota(jnp.int32, (1, width), 1) < count
        )
        raw = jnp.where(live, raw, 0.0)
        own = jnp.where(live, amps[j, rows, :].astype(jnp.float32), 0.0)
        gap = (occ_ref[0, pair // 2] + occ_ref[1, pair % 2]) - vcol_ref[rows, :] - vrow_ref[...]
        upd[j, rows, :] = (own + raw / gap).astype(upd.dtype)
        mover.put(upd.at[j, rows, :], upd_hbm.at[pair, rows, :])
    part[j, rows, :] = raw
    mover.put(part.at[j, rows, :], res_hbm.at[pair, rows, :])


def row_kernel(
    i, count_ref, occ_ref, vcol_ref, vrow_ref, b0_hbm, b1_hbm, xt_hbm, x_hbm, coret_hbm, wt_hbm, wd_hbm,
    amps_hbm, part_hbm, res_hbm, upd_hbm, xt, coret, wt, right, left, part, amps, proj, total, upd, sem, osem,
):
    width, points = x_hbm.shape
    head = pl.ds(0, points)
    blocks = [pl.ds(points + k * width, width) for k in range(2)]
    plan = {
        "b0": (b0_hbm, left.at[:, blocks[0]]),
        "xt": (xt_hbm, xt),
        "x0": (x_hbm, right.at[0, :, head]),
        "wt": (wt_hbm.at[pl.ds(2 * i, 2)], wt),
        "coret": (coret_hbm, coret),
        "b1": (b1_hbm, left.at[:, blocks[1]]),
    }
    for j in range(2):
        for k in range(2):
            plan["w%d%d" % (j, k)] = (wd_hbm.at[2 * j + k], right.at[j, :, blocks[k]])
        plan["part%d" % j] = (part_hbm.at[2 * i + j], part.at[j])
        plan["amps%d" % j] = (amps_hbm.at[2 * i + j], amps.at[j])
        if j == 0:
            plan["x1"] = (x_hbm, right.at[1, :, head])
    mover = Mover(plan, sem, osem)
    for j in range(2):
        mover.need("b%d" % j, "xt")
        proj[...] = dot(xt[...], left[:, blocks[j]]).astype(proj.dtype)
        mover.need("x0", "coret", "wt")
        inner = dot(proj[...], right[0, :, head])
        total[j] = (
            wt[j].astype(jnp.float32) + coret[...].astype(jnp.float32) * inner
        ).astype(total.dtype)
    for j in range(2):
        left[:, head] = dot(right[0, :, head], total[j]).astype(left.dtype)
        mover.need("x%d" % j, "w%d0" % j, "w%d1" % j, "part%d" % j, "amps%d" % j)
        for rows in strips(width, STRIP):
            raw = dot_nt(left[rows, :], right[j])
            emit(
                mover, True, 2 * i + j, j, rows, raw, count_ref, occ_ref, vcol_ref, vrow_ref,
                part, amps, upd, res_hbm, upd_hbm,
            )
    mover.drain()


def row(i, count, occ, vcol, vrow, b0, b1, xt, x, coret, wt, wd, amp4, part):
    width, points = x.shape
    vmem = pl.BlockSpec(memory_space=pltpu.VMEM)
    smem = pl.BlockSpec(memory_space=pltpu.SMEM)
    hbm = pl.BlockSpec(memory_space=pl.ANY)
    f32, bf16 = jnp.float32, jnp.bfloat16
    depth = points + 2 * width
    return pl.pallas_call(
        functools.partial(row_kernel, i),
        out_shape=[jax.ShapeDtypeStruct(part.shape, f32), jax.ShapeDtypeStruct(part.shape, bf16)],
        in_specs=[smem, smem, vmem, vmem] + [hbm] * 9,
        out_specs=[hbm] * 2,
        scratch_shapes=[
            pltpu.VMEM((points, width), bf16),
            pltpu.VMEM((points, points), bf16),
            pltpu.VMEM((2, points, points), bf16),
            pltpu.VMEM((2, width, depth), bf16),
            pltpu.VMEM((width, depth), bf16),
            pltpu.VMEM((2, width, width), f32),
            pltpu.VMEM((2, width, width), bf16),
            pltpu.VMEM((points, width), bf16),
            pltpu.VMEM((2, points, points), bf16),
            pltpu.VMEM((2, width, width), bf16),
            pltpu.SemaphoreType.DMA((15,)),
            pltpu.SemaphoreType.DMA((4 * (width // STRIP),)),
        ],
        input_output_aliases={12: 0},
        compiler_params=pltpu.CompilerParams(vmem_limit_bytes=VMEM_LIMIT),
        name="row_%d" % i,
    )(count, occ, vcol, vrow, b0, b1, xt, x, coret, wt, wd, amp4, part)


def piece_kernel(i, k, low, high, end, count_ref, occ_ref, vcol_ref, vrow_ref, *refs):
    last = k == 1 and end
    scratch = 13
    refs, (xt, coret, wt, right, left, part, amps, acc, proj, total, upd, sem, osem) = (
        refs[:-scratch], refs[-scratch:]
    )
    (b_hbm, xt_hbm, x_hbm, coret_hbm, wt_hbm, wd_hbm, amps_hbm, part_hbm) = refs[:8]
    refs = list(refs[8:])
    acc_in = refs.pop(0) if low > 0 else None
    upd_hbm = refs.pop() if last else None
    acc_out = None if end else refs.pop()
    res_hbm = refs.pop()
    width, points = x_hbm.shape
    head, rest = pl.ds(0, points), pl.ds(points, high - low)
    cut = pl.ds(low, high - low)
    plan = {
        "b": (b_hbm, left.at[:, rest]),
        "xt": (xt_hbm, xt),
        "x": (x_hbm, right.at[k, :, head]),
    }
    if low > 0:
        plan["acc"] = (acc_in, acc)
    if end:
        plan["wt"] = (wt_hbm.at[2 * i + k], wt)
        plan["coret"] = (coret_hbm, coret)
    for j in (1 - k, k):
        plan["w%d" % j] = (wd_hbm.at[2 * j + k, :, cut], right.at[j, :, rest])
        plan["part%d" % j] = (part_hbm.at[2 * i + j], part.at[j])
        if last:
            plan["amps%d" % j] = (amps_hbm.at[2 * i + j], amps.at[j])
    mover = Mover(plan, sem, osem)

    def products(j, columns):
        mover.need("w%d" % j, "part%d" % j, "amps%d" % j)
        for rows in strips(width, STRIP):
            raw = dot_nt(left[rows, columns], right[j, :, columns])
            emit(
                mover, last, 2 * i + j, j, rows, raw, count_ref, occ_ref, vcol_ref, vrow_ref,
                part, amps, upd, res_hbm, upd_hbm,
            )

    mover.need("b", "xt")
    proj[...] = dot(xt[...], left[:, rest]).astype(proj.dtype)
    mover.need("x")
    inner = dot(proj[...], right[k, cut, head])
    if low > 0:
        mover.need("acc")
        inner = inner + acc[...]
    if end:
        mover.need("wt", "coret")
        total[...] = (
            wt[...].astype(jnp.float32) + coret[...].astype(jnp.float32) * inner
        ).astype(total.dtype)
        left[:, head] = dot(right[k, :, head], total[...]).astype(left.dtype)
        products(1 - k, rest)
        products(k, pl.ds(0, points + high - low))
    else:
        acc[...] = inner
        mover.put(acc, acc_out)
        for j in (1 - k, k):
            products(j, rest)
    mover.drain()


def piece(i, k, low, high, count, occ, vcol, vrow, b, xt, x, coret, wt, wd, amp4, part, acc, updated):
    width, points = x.shape
    end = high == width
    last = k == 1 and end
    vmem = pl.BlockSpec(memory_space=pltpu.VMEM)
    smem = pl.BlockSpec(memory_space=pltpu.SMEM)
    hbm = pl.BlockSpec(memory_space=pl.ANY)
    f32, bf16 = jnp.float32, jnp.bfloat16
    operands = [count, occ, vcol, vrow, b, xt, x, coret, wt, wd, amp4, part]
    out_shape = [jax.ShapeDtypeStruct(part.shape, f32)]
    alias = {len(operands) - 1: 0}
    if low > 0:
        operands.append(acc)
    if not end:
        out_shape.append(jax.ShapeDtypeStruct((points, points), f32))
    if last:
        out_shape.append(jax.ShapeDtypeStruct(part.shape, bf16))
        alias[len(operands)] = 1
        operands.append(updated)
    return pl.pallas_call(
        functools.partial(piece_kernel, i, k, low, high, end),
        out_shape=out_shape,
        in_specs=[smem, smem, vmem, vmem] + [hbm] * (len(operands) - 4),
        out_specs=[hbm] * len(out_shape),
        scratch_shapes=[
            pltpu.VMEM((points, width), bf16),
            pltpu.VMEM((points, points), bf16),
            pltpu.VMEM((points, points), bf16),
            pltpu.VMEM((2, width, points + high - low), bf16),
            pltpu.VMEM((width, points + high - low), bf16),
            pltpu.VMEM((2, width, width), f32),
            pltpu.VMEM((2, width, width), bf16),
            pltpu.VMEM((points, points), f32),
            pltpu.VMEM((points, high - low), bf16),
            pltpu.VMEM((points, points), bf16),
            pltpu.VMEM((2, width, width), bf16),
            pltpu.SemaphoreType.DMA((12,)),
            pltpu.SemaphoreType.DMA((9,)),
        ],
        input_output_aliases=alias,
        compiler_params=pltpu.CompilerParams(vmem_limit_bytes=VMEM_LIMIT),
        name="piece_%d%d_%d" % (i, k, low),
    )(*operands)


def per_device(
    amps, x_factor, core, cycle_w, domain_tiles, domain_count, tile_slot, occ_energy, virt_energy
):
    occ = amps.shape[2]
    width = amps.shape[4]
    tile_width = x_factor.shape[1]
    grid_points = x_factor.shape[2]
    window = cycle_w.shape[4]
    cols = lax.axis_size("col")
    amp4 = amps[0, 0].reshape(occ * occ, width, width)
    shard = cycle_w[0].reshape(occ * occ, tile_width, window)

    split = 512
    xall, wall, far, first, coret, *turned = gather_parts(x_factor, shard, amp4, core, split)
    xall = xall.reshape(-1, tile_width, grid_points)
    side = lax.ppermute(far, "col", [(i, i ^ 2) for i in range(cols)])
    mirror = [(i, (i + cols // 2) % cols) for i in range(cols)]
    second, third, fourth = [lax.ppermute(part, "col", mirror) for part in turned[:3]]

    tiles, count = domain_tiles[0, 0], domain_count
    x, xt, wt = own_ladder(tiles, count, tile_slot, xall, amp4, core)
    side, tail, wt = lax.optimization_barrier((side, turned[3], wt))
    fifth = lax.ppermute(tail, "col", mirror)
    twin = lax.ppermute(side, "col", [(i, i ^ 1) for i in range(cols)])
    wd, part, vcol, vrow = own_cycle(tiles, count, virt_energy[None, :], wall, far, side, twin, amp4)
    energies = (count, occ_energy[0, 0], vcol, vrow)
    part, updated = row(0, *energies, first, second, xt, x, coret, wt, wd, amp4, part)
    fixed = (xt, x, coret, wt, wd, amp4)
    part, = piece(1, 0, 0, width, *energies, third, *fixed, part, None, None)
    part, acc = piece(1, 1, 0, split, *energies, fourth, *fixed, part, None, None)
    part, updated = piece(1, 1, split, width, *energies, fifth, *fixed, part, acc, updated)
    return part.reshape(amps.shape), updated.reshape(amps.shape)


def solution(mesh):
    in_specs = (
        P("row", "col", None, None, None, None),
        P("row", None, None),
        P(),
        P("row", None, None, "col", None),
        P("row", "col", None),
        P("row", "col"),
        P(),
        P("row", "col", None, None),
        P(),
    )
    out_specs = (P("row", "col", None, None, None, None), P("row", "col", None, None, None, None))
    return jax.shard_map(
        per_device, mesh=mesh, in_specs=in_specs, out_specs=out_specs, check_vma=False
    )
```

```python
import functools

import jax
import jax.numpy as jnp
from jax import lax
from jax.experimental import pallas as pl
from jax.experimental.pallas import tpu as pltpu
from jax.sharding import PartitionSpec as P

MESH = pl.DeviceIdType.MESH
VMEM_LIMIT = 65300 * 1024
STRIP = 384


def dot(a, b):
    return jnp.dot(a, b, preferred_element_type=jnp.float32)


def dot_nt(a, b):
    return lax.dot_general(a, b, (((1,), (1,)), ((), ())), preferred_element_type=jnp.float32)


def strips(width, step):
    return [pl.ds(start, step) for start in range(0, width, step)]


def remote(src, dst, sems, index, device):
    return pltpu.make_async_remote_copy(
        src_ref=src, dst_ref=dst, send_sem=sems[0].at[index], recv_sem=sems[1].at[index],
        device_id=device, device_id_type=MESH,
    )


def greet(devices):
    barrier = pltpu.get_barrier_semaphore()
    for device in devices:
        pl.semaphore_signal(barrier, inc=1, device_id=device, device_id_type=MESH)
    pl.semaphore_wait(barrier, len(devices))


def gather_kernel(
    x_ref, w_ref, amps_ref, core_ref, xall_ref, wall_ref, far_ref, first_ref, coret_ref, *refs
):
    cuts, (plain, turned, fixed, wsend, wrecv, xsend, xrecv, msend, mrecv, local, tsem) = refs[:-11], refs[-11:]
    r = lax.axis_index("row")
    c = lax.axis_index("col")
    rows = lax.axis_size("row")
    cols = lax.axis_size("col")
    forth = (r, (c + 4) % cols)
    back = (r, (c + cols - 4) % cols)
    mirror = (r, (c + cols // 2) % cols)
    zside = (r, c + 2 - 4 * ((c // 2) % 2))
    twin = (r, c + 1 - 2 * (c % 2))
    beside = r + 1 - 2 * (r % 2)
    core = c % 2
    half = w_ref.shape[0] // 2
    width = plain.shape[1]
    y_steps = range(1, rows // 2)

    amps_in = [pltpu.make_async_copy(amps_ref.at[q], plain.at[q], tsem.at[q]) for q in range(4)]
    core_in = pltpu.make_async_copy(core_ref, fixed.at[0], tsem.at[4])
    for copy in amps_in + [core_in]:
        copy.start()
    greet(
        [forth, back, mirror, zside, twin, (beside, c)]
        + [((r + 2 * step) % rows, c) for step in y_steps]
    )
    wsems, xsems = (wsend, wrecv), (xsend, xrecv)
    started = []

    def send(*args):
        copy = remote(*args)
        copy.start()
        started.append(copy)

    def arrived(part, sems, index):
        remote(part, part, sems, index, twin).wait_recv()

    def shard(offset, plane, side):
        if offset in (1, 2) and plane + side == 0:
            return far_ref.at[offset - 1]
        x = (c // 4 + offset) % (cols // 4)
        z = (c // 2) % 2
        z = z + plane * (1 - 2 * z)
        k = core + side * (1 - 2 * core)
        return wall_ref.at[x * 4 + z * 2 + k]

    def to_twin(offset):
        x = (c // 4 + offset) % (cols // 4)
        send(shard(offset, 0, 0), wall_ref.at[x * 4 + c % 4], wsems, 6 + offset, twin)

    def transpose(q, p):
        amps_in[q].wait()
        for cut in strips(width, 256):
            turned[p, :, cut] = plain[q, cut, :].T

    own = wall_ref.at[c]
    send(w_ref, own, wsems, 0, forth)
    send(w_ref, far_ref.at[0], wsems, 1, back)
    send(x_ref.at[core], xall_ref.at[r, core], xsems, 0, (beside, c))
    send(w_ref, own, wsems, 4, zside)
    for step in y_steps:
        send(x_ref.at[core], xall_ref.at[r, core], xsems, step, ((r + 2 * step) % rows, c))
    send(w_ref, own, wsems, 6, twin)
    own_w = pltpu.make_async_copy(w_ref, own, local.at[0])
    own_x = pltpu.make_async_copy(x_ref, xall_ref.at[r], local.at[1])
    own_w.start()
    own_x.start()
    transpose(0, 0)

    part = xall_ref.at[beside, core]
    arrived(part, xsems, 0)
    for step in y_steps:
        send(part, part, xsems, 3 + step, ((r + 2 * step) % rows, c))
    send(part, part, xsems, 7, twin)

    part = shard(3, 0, 0)
    arrived(part, wsems, 0)
    send(part.at[:half], far_ref.at[1, :half], wsems, 2, forth)
    send(part, part, wsems, 5, zside)
    arrived(far_ref.at[0], wsems, 1)
    send(far_ref.at[0, half:], far_ref.at[1, half:], wsems, 3, back)
    send(turned.at[0, :, pl.ds(0, first_ref.shape[1])], first_ref, (msend, mrecv), 0, mirror)
    to_twin(3)
    to_twin(1)
    transpose(2, 1)
    for step in y_steps:
        origin = (r + rows - 2 * step) % rows
        arrived(xall_ref.at[origin, core], xsems, step)
        send(xall_ref.at[origin, core], xall_ref.at[origin, core], xsems, 7 + step, twin)
    transpose(1, 2)
    part = shard(0, 1, 0)
    arrived(part, wsems, 4)
    send(part, part, wsems, 10, twin)
    for step in y_steps:
        origin = (r + rows - 2 * step) % rows
        origin = origin + 1 - 2 * (origin % 2)
        arrived(xall_ref.at[origin, core], xsems, 3 + step)
        send(xall_ref.at[origin, core], xall_ref.at[origin, core], xsems, 10 + step, twin)
    arrived(far_ref.at[1, :half], wsems, 2)
    arrived(far_ref.at[1, half:], wsems, 3)
    to_twin(2)
    transpose(3, 3)
    early, split = first_ref.shape[1], cuts[2].shape[1]
    moves = (
        (0, pl.ds(early, width - early), 0, pl.ds(0, width - early)),
        (1, pl.ds(0, width), 0, pl.ds(width - early, width)),
        (2, pl.ds(0, width), 1, pl.ds(0, width)),
        (3, pl.ds(0, split), 2, pl.ds(0, split)),
        (3, pl.ds(split, width - split), 3, pl.ds(0, width - split)),
    )
    outs = [
        pltpu.make_async_copy(turned.at[p, :, source], cuts[q].at[:, target], local.at[3 + at])
        for at, (p, source, q, target) in enumerate(moves)
    ]
    core_in.wait()
    for cut in strips(width, 256):
        fixed[1, :, cut] = fixed[0, cut, :].T
    outs.append(pltpu.make_async_copy(fixed.at[1], coret_ref, local.at[2]))
    for copy in outs:
        copy.start()
    part = shard(3, 1, 0)
    arrived(part, wsems, 5)
    send(part, part, wsems, 11, twin)

    for offset in range(4):
        arrived(shard(offset, 0, 1), wsems, 6 + offset)
    arrived(shard(0, 1, 1), wsems, 10)
    arrived(shard(3, 1, 1), wsems, 11)
    arrived(xall_ref.at[beside, 1 - core], xsems, 7)
    for step in y_steps:
        origin = (r + rows - 2 * step) % rows
        arrived(xall_ref.at[origin, 1 - core], xsems, 7 + step)
        origin = origin + 1 - 2 * (origin % 2)
        arrived(xall_ref.at[origin, 1 - core], xsems, 10 + step)
    remote(first_ref, first_ref, (msend, mrecv), 0, mirror).wait_recv()
    for copy in started:
        copy.wait_send()
    for copy in outs + [own_w, own_x]:
        copy.wait()


def gather_parts(x_factor, shard, amp4, core, early, split):
    rows = lax.axis_size("row")
    cols = lax.axis_size("col")
    width = amp4.shape[1]
    hbm = pl.BlockSpec(memory_space=pl.ANY)
    bf16 = jnp.bfloat16
    dma = pltpu.SemaphoreType.DMA
    shapes = [(rows,) + x_factor.shape, (cols,) + shard.shape, (2,) + shard.shape, (width, early), core.shape]
    shapes += [(width, 2 * width - early), (width, width)]
    shapes += [(width, split), (width, width - split)]
    return pl.pallas_call(
        gather_kernel,
        out_shape=[jax.ShapeDtypeStruct(shape, bf16) for shape in shapes],
        in_specs=[hbm] * 4,
        out_specs=[hbm] * len(shapes),
        scratch_shapes=[
            pltpu.VMEM(amp4.shape, bf16),
            pltpu.VMEM(amp4.shape, bf16),
            pltpu.VMEM((2,) + core.shape, bf16),
            dma((12,)),
            dma((12,)),
            dma((14,)),
            dma((14,)),
            dma((1,)),
            dma((1,)),
            dma((8,)),
            dma((5,)),
        ],
        compiler_params=pltpu.CompilerParams(
            collective_id=0, has_side_effects=True, vmem_limit_bytes=VMEM_LIMIT
        ),
        name="gather_parts",
    )(x_factor, shard, amp4, core)


def own_ladder_kernel(
    tiles_ref, count_ref, slot_ref, xall_ref, amps_ref, core_ref, x_ref, xt_ref, wt_ref, gathered, proj, sem
):
    @pl.when(pl.program_id(0) == 0)
    def _():
        tile = xall_ref.shape[1]
        copies = []
        for s in range(tiles_ref.shape[0]):
            copy = pltpu.make_async_copy(
                xall_ref.at[slot_ref[tiles_ref[s]]], gathered.at[pl.ds(s * tile, tile), :], sem.at[s]
            )
            copy.start()
            copies.append(copy)
        for copy in copies:
            copy.wait()
        live = lax.broadcasted_iota(jnp.int32, (x_ref.shape[0], 1), 0) < count_ref[0, 0] * tile
        x_ref[...] = jnp.where(live, gathered[...].astype(jnp.float32), 0.0).astype(x_ref.dtype)
        for cut in strips(x_ref.shape[0], 256):
            xt_ref[:, cut] = x_ref[cut, :].T

    proj[...] = dot(xt_ref[...], amps_ref[0]).astype(proj.dtype)
    inner = dot(proj[...], x_ref[...])
    wt_ref[0] = (core_ref[...].astype(jnp.float32) * inner).astype(wt_ref.dtype)


def own_ladder(tiles, count, tile_slot, xall, amp4, core):
    width = amp4.shape[1]
    points = core.shape[0]
    smem = pl.BlockSpec(memory_space=pltpu.SMEM)
    bf16 = jnp.bfloat16

    def whole(shape):
        return pl.BlockSpec(shape, lambda p: (0, 0))

    return pl.pallas_call(
        own_ladder_kernel,
        out_shape=(
            jax.ShapeDtypeStruct((width, points), bf16),
            jax.ShapeDtypeStruct((points, width), bf16),
            jax.ShapeDtypeStruct((4, points, points), bf16),
        ),
        grid=(4,),
        in_specs=[
            smem, smem, smem, pl.BlockSpec(memory_space=pl.ANY),
            pl.BlockSpec((1, width, width), lambda p: (p, 0, 0)), whole((points, points)),
        ],
        out_specs=(
            whole((width, points)), whole((points, width)),
            pl.BlockSpec((1, points, points), lambda p: (p, 0, 0)),
        ),
        scratch_shapes=[
            pltpu.VMEM((width, points), bf16),
            pltpu.VMEM((points, width), bf16),
            pltpu.SemaphoreType.DMA((tiles.shape[0],)),
        ],
        compiler_params=pltpu.CompilerParams(vmem_limit_bytes=VMEM_LIMIT),
        name="own_ladder",
    )(tiles, count, tile_slot, xall, amp4, core)


def window_index(tiles_ref, count_ref, tile, shape, axis):
    at = lax.broadcasted_iota(jnp.int32, shape, axis)
    index = jnp.full(shape, -1, jnp.int32)
    for s in range(tiles_ref.shape[0]):
        inside = (at >= s * tile) & (at < (s + 1) * tile) & (s < count_ref[0, 0])
        index = jnp.where(inside, at + (tiles_ref[s] - s) * tile, index)
    return index


def own_cycle_kernel(
    tiles_ref, count_ref, virt_ref, wall_ref, far_ref, side_ref, twin_ref, a0_ref, a1_ref,
    wd_ref, cyc_ref, vcol_ref, vrow_ref, wsel, pick, sem,
):
    p = pl.program_id(0)
    tile = wall_ref.shape[2]
    slots = tiles_ref.shape[0]
    width = wd_ref.shape[1]
    window = virt_ref.shape[1]

    @pl.when(p == 0)
    def _():
        me = lax.axis_index("col")
        for first in range(2):
            for s in range(slots):
                number = tiles_ref[s]
                offset = ((number >> 2) + 4 - (me >> 2)) & 3
                plane = ((number >> 1) + (me >> 1)) & 1
                side = (number + me) & 1
                apart = (offset == 1) | (offset == 2)
                dst = wsel.at[pl.ds(2 * first, 2), pl.ds(s * tile, tile), :]

                def fetch(source, at, dst=dst, done=sem.at[first, s], first=first):
                    pltpu.make_async_copy(source.at[at, pl.ds(2 * first, 2)], dst, done).start()

                @pl.when(jnp.logical_not(apart) | ((plane == 0) & (side == 1)))
                def _(number=number, fetch=fetch):
                    fetch(wall_ref, number)

                for source, at_plane, at_side in ((far_ref, 0, 0), (side_ref, 1, 0), (twin_ref, 1, 1)):

                    @pl.when(apart & (plane == at_plane) & (side == at_side))
                    def _(source=source, offset=offset, fetch=fetch):
                        fetch(source, offset - 1)

        along = lax.broadcasted_iota(jnp.int32, pick.shape, 0)
        picked = window_index(tiles_ref, count_ref, tile, (1, width), 1)
        pick[...] = jnp.where(along == picked, 1.0, 0.0).astype(pick.dtype)
        picked = window_index(tiles_ref, count_ref, tile, (width, 1), 0)
        along = lax.broadcasted_iota(jnp.int32, (width, window), 1)
        levels = jnp.sum(jnp.where(along == picked, virt_ref[...], 0.0), axis=1, keepdims=True)
        vcol_ref[...] = levels
        vrow_ref[...] = jnp.broadcast_to(levels, (width, 128)).T[:1, :]

    for first in range(2):

        @pl.when(p == 2 * first)
        def _(first=first):
            for s in range(slots):
                pltpu.make_async_copy(
                    wall_ref.at[0, pl.ds(0, 2)],
                    wsel.at[pl.ds(2 * first, 2), pl.ds(s * tile, tile), :],
                    sem.at[first, s],
                ).wait()
            for k in range(2):
                wd_ref[k] = dot(wsel[2 * first + k], pick[...]).astype(wd_ref.dtype)

    cyc_ref[0] = dot(wd_ref[0], a0_ref[0]) + dot(wd_ref[1], a1_ref[0])


def own_cycle(tiles, count, virt, wall, far, side, twin, amp4):
    width = amp4.shape[1]
    slots, window = tiles.shape[0], wall.shape[3]
    smem = pl.BlockSpec(memory_space=pltpu.SMEM)
    hbm = pl.BlockSpec(memory_space=pl.ANY)
    f32, bf16 = jnp.float32, jnp.bfloat16
    return pl.pallas_call(
        own_cycle_kernel,
        out_shape=(
            jax.ShapeDtypeStruct((4, width, width), bf16),
            jax.ShapeDtypeStruct((4, width, width), f32),
            jax.ShapeDtypeStruct((width, 1), f32),
            jax.ShapeDtypeStruct((1, width), f32),
        ),
        grid=(4,),
        in_specs=[
            smem,
            smem,
            pl.BlockSpec((1, window), lambda p: (0, 0)),
            hbm,
            hbm,
            hbm,
            hbm,
            pl.BlockSpec((1, width, width), lambda p: (p % 2, 0, 0)),
            pl.BlockSpec((1, width, width), lambda p: (2 + p % 2, 0, 0)),
        ],
        out_specs=(
            pl.BlockSpec((2, width, width), lambda p: (p // 2, 0, 0)),
            pl.BlockSpec((1, width, width), lambda p: (p, 0, 0)),
            pl.BlockSpec((width, 1), lambda p: (0, 0)),
            pl.BlockSpec((1, width), lambda p: (0, 0)),
        ),
        scratch_shapes=[
            pltpu.VMEM((4, width, window), bf16),
            pltpu.VMEM((window, width), bf16),
            pltpu.SemaphoreType.DMA((2, slots)),
        ],
        compiler_params=pltpu.CompilerParams(vmem_limit_bytes=VMEM_LIMIT),
        name="own_cycle",
    )(tiles, count, virt, wall, far, side, twin, amp4, amp4)


class Mover:
    def __init__(self, plan, in_sem, out_sem):
        self.out_sem = out_sem
        self.outs = []
        self.loads = {}
        for at, (name, (src, dst)) in enumerate(plan.items()):
            self.loads[name] = pltpu.make_async_copy(src, dst, in_sem.at[at])
            self.loads[name].start()

    def need(self, *names):
        for name in names:
            if name in self.loads:
                self.loads.pop(name).wait()

    def put(self, src, dst):
        copy = pltpu.make_async_copy(src, dst, self.out_sem.at[len(self.outs)])
        copy.start()
        self.outs.append(copy)

    def drain(self):
        for copy in self.outs:
            copy.wait()


def emit(mover, last, pair, j, rows, raw, count_ref, occ_ref, vcol_ref, vrow_ref, part, amps, upd, res_hbm, upd_hbm):
    raw = raw + part[j, rows, :]
    if last:
        count = count_ref[0, 0] * 64
        height, width = raw.shape
        live = (lax.broadcasted_iota(jnp.int32, (height, 1), 0) + rows.start < count) & (
            lax.broadcasted_iota(jnp.int32, (1, width), 1) < count
        )
        raw = jnp.where(live, raw, 0.0)
        own = jnp.where(live, amps[j, rows, :].astype(jnp.float32), 0.0)
        gap = (occ_ref[0, pair // 2] + occ_ref[1, pair % 2]) - vcol_ref[rows, :] - vrow_ref[...]
        upd[j, rows, :] = (own + raw / gap).astype(upd.dtype)
        mover.put(upd.at[j, rows, :], upd_hbm.at[pair, rows, :])
    part[j, rows, :] = raw
    mover.put(part.at[j, rows, :], res_hbm.at[pair, rows, :])


def row_kernel(
    i, count_ref, occ_ref, vcol_ref, vrow_ref, b0_hbm, b1_hbm, xt_hbm, x_hbm, coret_hbm, wt_hbm, wd_hbm,
    amps_hbm, part_hbm, res_hbm, upd_hbm, xt, coret, wt, right, left, part, amps, proj, total, upd, sem, osem,
):
    width, points = x_hbm.shape
    early = b0_hbm.shape[1]
    head = pl.ds(0, points)
    blocks = [pl.ds(points + k * width, width) for k in range(2)]
    plan = {
        "b0": (b0_hbm, left.at[:, pl.ds(points, early)]),
        "b1": (b1_hbm, left.at[:, pl.ds(points + early, 2 * width - early)]),
        "xt": (xt_hbm, xt),
        "x0": (x_hbm, right.at[0, :, head]),
        "wt": (wt_hbm.at[pl.ds(2 * i, 2)], wt),
        "coret": (coret_hbm, coret),
    }
    for j in range(2):
        for k in range(2):
            plan["w%d%d" % (j, k)] = (wd_hbm.at[2 * j + k], right.at[j, :, blocks[k]])
        plan["part%d" % j] = (part_hbm.at[2 * i + j], part.at[j])
        plan["amps%d" % j] = (amps_hbm.at[2 * i + j], amps.at[j])
        if j == 0:
            plan["x1"] = (x_hbm, right.at[1, :, head])
    mover = Mover(plan, sem, osem)
    for j in range(2):
        mover.need("b0", "b1", "xt")
        proj[...] = dot(xt[...], left[:, blocks[j]]).astype(proj.dtype)
        mover.need("x0", "coret", "wt")
        inner = dot(proj[...], right[0, :, head])
        total[j] = (
            wt[j].astype(jnp.float32) + coret[...].astype(jnp.float32) * inner
        ).astype(total.dtype)
    for j in range(2):
        left[:, head] = dot(right[0, :, head], total[j]).astype(left.dtype)
        mover.need("x%d" % j, "w%d0" % j, "w%d1" % j, "part%d" % j, "amps%d" % j)
        for rows in strips(width, STRIP):
            raw = dot_nt(left[rows, :], right[j])
            emit(
                mover, True, 2 * i + j, j, rows, raw, count_ref, occ_ref, vcol_ref, vrow_ref,
                part, amps, upd, res_hbm, upd_hbm,
            )
    mover.drain()


def row(i, count, occ, vcol, vrow, b0, b1, xt, x, coret, wt, wd, amp4, part):
    width, points = x.shape
    vmem = pl.BlockSpec(memory_space=pltpu.VMEM)
    smem = pl.BlockSpec(memory_space=pltpu.SMEM)
    hbm = pl.BlockSpec(memory_space=pl.ANY)
    f32, bf16 = jnp.float32, jnp.bfloat16
    depth = points + 2 * width
    return pl.pallas_call(
        functools.partial(row_kernel, i),
        out_shape=[jax.ShapeDtypeStruct(part.shape, f32), jax.ShapeDtypeStruct(part.shape, bf16)],
        in_specs=[smem, smem, vmem, vmem] + [hbm] * 9,
        out_specs=[hbm] * 2,
        scratch_shapes=[
            pltpu.VMEM((points, width), bf16),
            pltpu.VMEM((points, points), bf16),
            pltpu.VMEM((2, points, points), bf16),
            pltpu.VMEM((2, width, depth), bf16),
            pltpu.VMEM((width, depth), bf16),
            pltpu.VMEM((2, width, width), f32),
            pltpu.VMEM((2, width, width), bf16),
            pltpu.VMEM((points, width), bf16),
            pltpu.VMEM((2, points, points), bf16),
            pltpu.VMEM((2, width, width), bf16),
            pltpu.SemaphoreType.DMA((15,)),
            pltpu.SemaphoreType.DMA((4 * (width // STRIP),)),
        ],
        input_output_aliases={12: 0},
        compiler_params=pltpu.CompilerParams(vmem_limit_bytes=VMEM_LIMIT),
        name="row_%d" % i,
    )(count, occ, vcol, vrow, b0, b1, xt, x, coret, wt, wd, amp4, part)


def piece_kernel(i, k, low, high, end, count_ref, occ_ref, vcol_ref, vrow_ref, *refs):
    last = k == 1 and end
    scratch = 13
    refs, (xt, coret, wt, right, left, part, amps, acc, proj, total, upd, sem, osem) = (
        refs[:-scratch], refs[-scratch:]
    )
    (b_hbm, xt_hbm, x_hbm, coret_hbm, wt_hbm, wd_hbm, amps_hbm, part_hbm) = refs[:8]
    refs = list(refs[8:])
    acc_in = refs.pop(0) if low > 0 else None
    upd_hbm = refs.pop() if last else None
    acc_out = None if end else refs.pop()
    res_hbm = refs.pop()
    width, points = x_hbm.shape
    head, rest = pl.ds(0, points), pl.ds(points, high - low)
    cut = pl.ds(low, high - low)
    plan = {
        "b": (b_hbm, left.at[:, rest]),
        "xt": (xt_hbm, xt),
        "x": (x_hbm, right.at[k, :, head]),
    }
    if low > 0:
        plan["acc"] = (acc_in, acc)
    if end:
        plan["wt"] = (wt_hbm.at[2 * i + k], wt)
        plan["coret"] = (coret_hbm, coret)
    for j in (1 - k, k):
        plan["w%d" % j] = (wd_hbm.at[2 * j + k, :, cut], right.at[j, :, rest])
        plan["part%d" % j] = (part_hbm.at[2 * i + j], part.at[j])
        if last:
            plan["amps%d" % j] = (amps_hbm.at[2 * i + j], amps.at[j])
    mover = Mover(plan, sem, osem)

    def products(j, columns):
        mover.need("w%d" % j, "part%d" % j, "amps%d" % j)
        for rows in strips(width, STRIP):
            raw = dot_nt(left[rows, columns], right[j, :, columns])
            emit(
                mover, last, 2 * i + j, j, rows, raw, count_ref, occ_ref, vcol_ref, vrow_ref,
                part, amps, upd, res_hbm, upd_hbm,
            )

    mover.need("b", "xt")
    proj[...] = dot(xt[...], left[:, rest]).astype(proj.dtype)
    mover.need("x")
    inner = dot(proj[...], right[k, cut, head])
    if low > 0:
        mover.need("acc")
        inner = inner + acc[...]
    if end:
        mover.need("wt", "coret")
        total[...] = (
            wt[...].astype(jnp.float32) + coret[...].astype(jnp.float32) * inner
        ).astype(total.dtype)
        left[:, head] = dot(right[k, :, head], total[...]).astype(left.dtype)
        products(1 - k, rest)
        products(k, pl.ds(0, points + high - low))
    else:
        acc[...] = inner
        mover.put(acc, acc_out)
        for j in (1 - k, k):
            products(j, rest)
    mover.drain()


def piece(i, k, low, high, count, occ, vcol, vrow, b, xt, x, coret, wt, wd, amp4, part, acc, updated):
    width, points = x.shape
    end = high == width
    last = k == 1 and end
    vmem = pl.BlockSpec(memory_space=pltpu.VMEM)
    smem = pl.BlockSpec(memory_space=pltpu.SMEM)
    hbm = pl.BlockSpec(memory_space=pl.ANY)
    f32, bf16 = jnp.float32, jnp.bfloat16
    operands = [count, occ, vcol, vrow, b, xt, x, coret, wt, wd, amp4, part]
    out_shape = [jax.ShapeDtypeStruct(part.shape, f32)]
    alias = {len(operands) - 1: 0}
    if low > 0:
        operands.append(acc)
    if not end:
        out_shape.append(jax.ShapeDtypeStruct((points, points), f32))
    if last:
        out_shape.append(jax.ShapeDtypeStruct(part.shape, bf16))
        alias[len(operands)] = 1
        operands.append(updated)
    return pl.pallas_call(
        functools.partial(piece_kernel, i, k, low, high, end),
        out_shape=out_shape,
        in_specs=[smem, smem, vmem, vmem] + [hbm] * (len(operands) - 4),
        out_specs=[hbm] * len(out_shape),
        scratch_shapes=[
            pltpu.VMEM((points, width), bf16),
            pltpu.VMEM((points, points), bf16),
            pltpu.VMEM((points, points), bf16),
            pltpu.VMEM((2, width, points + high - low), bf16),
            pltpu.VMEM((width, points + high - low), bf16),
            pltpu.VMEM((2, width, width), f32),
            pltpu.VMEM((2, width, width), bf16),
            pltpu.VMEM((points, points), f32),
            pltpu.VMEM((points, high - low), bf16),
            pltpu.VMEM((points, points), bf16),
            pltpu.VMEM((2, width, width), bf16),
            pltpu.SemaphoreType.DMA((12,)),
            pltpu.SemaphoreType.DMA((9,)),
        ],
        input_output_aliases=alias,
        compiler_params=pltpu.CompilerParams(vmem_limit_bytes=VMEM_LIMIT),
        name="piece_%d%d_%d" % (i, k, low),
    )(*operands)


def per_device(
    amps, x_factor, core, cycle_w, domain_tiles, domain_count, tile_slot, occ_energy, virt_energy
):
    occ = amps.shape[2]
    width = amps.shape[4]
    tile_width = x_factor.shape[1]
    grid_points = x_factor.shape[2]
    window = cycle_w.shape[4]
    cols = lax.axis_size("col")
    amp4 = amps[0, 0].reshape(occ * occ, width, width)
    shard = cycle_w[0].reshape(occ * occ, tile_width, window)

    early, split = width // 2, 512
    xall, wall, far, first, coret, *turned = gather_parts(x_factor, shard, amp4, core, early, split)
    xall = xall.reshape(-1, tile_width, grid_points)
    mirror = [(i, (i + cols // 2) % cols) for i in range(cols)]
    second, third, fourth = [lax.ppermute(part, "col", mirror) for part in turned[:3]]
    side = lax.ppermute(far, "col", [(i, i ^ 2) for i in range(cols)])

    tiles, count = domain_tiles[0, 0], domain_count
    x, xt, wt = own_ladder(tiles, count, tile_slot, xall, amp4, core)
    side, tail, wt = lax.optimization_barrier((side, turned[3], wt))
    fifth = lax.ppermute(tail, "col", mirror)
    twin = lax.ppermute(side, "col", [(i, i ^ 1) for i in range(cols)])
    wd, part, vcol, vrow = own_cycle(tiles, count, virt_energy[None, :], wall, far, side, twin, amp4)
    energies = (count, occ_energy[0, 0], vcol, vrow)
    part, updated = row(0, *energies, first, second, xt, x, coret, wt, wd, amp4, part)
    fixed = (xt, x, coret, wt, wd, amp4)
    part, = piece(1, 0, 0, width, *energies, third, *fixed, part, None, None)
    part, acc = piece(1, 1, 0, split, *energies, fourth, *fixed, part, None, None)
    part, updated = piece(1, 1, split, width, *energies, fifth, *fixed, part, acc, updated)
    return part.reshape(amps.shape), updated.reshape(amps.shape)


def solution(mesh):
    in_specs = (
        P("row", "col", None, None, None, None),
        P("row", None, None),
        P(),
        P("row", None, None, "col", None),
        P("row", "col", None),
        P("row", "col"),
        P(),
        P("row", "col", None, None),
        P(),
    )
    out_specs = (P("row", "col", None, None, None, None), P("row", "col", None, None, None, None))
    return jax.shard_map(
        per_device, mesh=mesh, in_specs=in_specs, out_specs=out_specs, check_vma=False
    )
```

```python
import functools

import jax
import jax.numpy as jnp
from jax import lax
from jax.experimental import pallas as pl
from jax.experimental.pallas import tpu as pltpu
from jax.sharding import PartitionSpec as P

MESH = pl.DeviceIdType.MESH
VMEM_LIMIT = 65300 * 1024
STRIP = 384


def dot(a, b):
    return jnp.dot(a, b, preferred_element_type=jnp.float32)


def dot_nt(a, b):
    return lax.dot_general(a, b, (((1,), (1,)), ((), ())), preferred_element_type=jnp.float32)


def strips(width, step):
    return [pl.ds(start, step) for start in range(0, width, step)]


def remote(src, dst, sems, index, device):
    return pltpu.make_async_remote_copy(
        src_ref=src, dst_ref=dst, send_sem=sems[0].at[index], recv_sem=sems[1].at[index],
        device_id=device, device_id_type=MESH,
    )


def greet(devices):
    barrier = pltpu.get_barrier_semaphore()
    for device in devices:
        pl.semaphore_signal(barrier, inc=1, device_id=device, device_id_type=MESH)
    pl.semaphore_wait(barrier, len(devices))


def gather_kernel(
    x_ref, w_ref, amps_ref, core_ref, xall_ref, wall_ref, far_ref, first_ref, coret_ref, *refs
):
    cuts, (plain, turned, fixed, wsend, wrecv, xsend, xrecv, msend, mrecv, local, tsem) = refs[:-11], refs[-11:]
    r = lax.axis_index("row")
    c = lax.axis_index("col")
    rows = lax.axis_size("row")
    cols = lax.axis_size("col")
    forth = (r, (c + 4) % cols)
    back = (r, (c + cols - 4) % cols)
    mirror = (r, (c + cols // 2) % cols)
    zside = (r, c + 2 - 4 * ((c // 2) % 2))
    twin = (r, c + 1 - 2 * (c % 2))
    beside = r + 1 - 2 * (r % 2)
    core = c % 2
    half = w_ref.shape[0] // 2
    width = plain.shape[1]
    y_steps = range(1, rows // 2)

    amps_in = [pltpu.make_async_copy(amps_ref.at[q], plain.at[q], tsem.at[q]) for q in range(4)]
    core_in = pltpu.make_async_copy(core_ref, fixed.at[0], tsem.at[4])
    for copy in amps_in + [core_in]:
        copy.start()
    greet(
        [forth, back, mirror, zside, twin, (beside, c)]
        + [((r + 2 * step) % rows, c) for step in y_steps]
    )
    wsems, xsems = (wsend, wrecv), (xsend, xrecv)
    started = []

    def send(*args):
        copy = remote(*args)
        copy.start()
        started.append(copy)

    def arrived(part, sems, index):
        remote(part, part, sems, index, twin).wait_recv()

    def shard(offset, plane, side):
        if offset in (1, 2) and plane + side == 0:
            return far_ref.at[offset - 1]
        x = (c // 4 + offset) % (cols // 4)
        z = (c // 2) % 2
        z = z + plane * (1 - 2 * z)
        k = core + side * (1 - 2 * core)
        return wall_ref.at[x * 4 + z * 2 + k]

    def to_twin(offset):
        x = (c // 4 + offset) % (cols // 4)
        send(shard(offset, 0, 0), wall_ref.at[x * 4 + c % 4], wsems, 6 + offset, twin)

    def transpose(q, p):
        amps_in[q].wait()
        for cut in strips(width, 256):
            turned[p, :, cut] = plain[q, cut, :].T

    own = wall_ref.at[c]
    send(w_ref, own, wsems, 0, forth)
    send(w_ref, far_ref.at[0], wsems, 1, back)
    send(x_ref.at[core], xall_ref.at[r, core], xsems, 0, (beside, c))
    send(w_ref, own, wsems, 4, zside)
    for step in y_steps:
        send(x_ref.at[core], xall_ref.at[r, core], xsems, step, ((r + 2 * step) % rows, c))
    send(w_ref, own, wsems, 6, twin)
    own_w = pltpu.make_async_copy(w_ref, own, local.at[0])
    own_x = pltpu.make_async_copy(x_ref, xall_ref.at[r], local.at[1])
    own_w.start()
    own_x.start()
    transpose(0, 0)

    part = xall_ref.at[beside, core]
    arrived(part, xsems, 0)
    for step in y_steps:
        send(part, part, xsems, 3 + step, ((r + 2 * step) % rows, c))
    send(part, part, xsems, 7, twin)

    part = shard(3, 0, 0)
    arrived(part, wsems, 0)
    send(part.at[:half], far_ref.at[1, :half], wsems, 2, forth)
    send(part, part, wsems, 5, zside)
    arrived(far_ref.at[0], wsems, 1)
    send(far_ref.at[0, half:], far_ref.at[1, half:], wsems, 3, back)
    send(turned.at[0, :, pl.ds(0, first_ref.shape[1])], first_ref, (msend, mrecv), 0, mirror)
    to_twin(3)
    to_twin(1)
    transpose(2, 1)
    for step in y_steps:
        origin = (r + rows - 2 * step) % rows
        arrived(xall_ref.at[origin, core], xsems, step)
        send(xall_ref.at[origin, core], xall_ref.at[origin, core], xsems, 7 + step, twin)
    transpose(1, 2)
    part = shard(0, 1, 0)
    arrived(part, wsems, 4)
    send(part, part, wsems, 10, twin)
    for step in y_steps:
        origin = (r + rows - 2 * step) % rows
        origin = origin + 1 - 2 * (origin % 2)
        arrived(xall_ref.at[origin, core], xsems, 3 + step)
        send(xall_ref.at[origin, core], xall_ref.at[origin, core], xsems, 10 + step, twin)
    arrived(far_ref.at[1, :half], wsems, 2)
    arrived(far_ref.at[1, half:], wsems, 3)
    to_twin(2)
    transpose(3, 3)
    early, split = first_ref.shape[1], cuts[2].shape[1]
    moves = (
        (0, pl.ds(early, width - early), 0, pl.ds(0, width - early)),
        (1, pl.ds(0, width), 0, pl.ds(width - early, width)),
        (2, pl.ds(0, width), 1, pl.ds(0, width)),
        (3, pl.ds(0, split), 2, pl.ds(0, split)),
        (3, pl.ds(split, width - split), 3, pl.ds(0, width - split)),
    )
    outs = [
        pltpu.make_async_copy(turned.at[p, :, source], cuts[q].at[:, target], local.at[3 + at])
        for at, (p, source, q, target) in enumerate(moves)
    ]
    core_in.wait()
    for cut in strips(width, 256):
        fixed[1, :, cut] = fixed[0, cut, :].T
    outs.append(pltpu.make_async_copy(fixed.at[1], coret_ref, local.at[2]))
    for copy in outs:
        copy.start()
    part = shard(3, 1, 0)
    arrived(part, wsems, 5)
    send(part, part, wsems, 11, twin)

    for offset in range(4):
        arrived(shard(offset, 0, 1), wsems, 6 + offset)
    arrived(shard(0, 1, 1), wsems, 10)
    arrived(shard(3, 1, 1), wsems, 11)
    arrived(xall_ref.at[beside, 1 - core], xsems, 7)
    for step in y_steps:
        origin = (r + rows - 2 * step) % rows
        arrived(xall_ref.at[origin, 1 - core], xsems, 7 + step)
        origin = origin + 1 - 2 * (origin % 2)
        arrived(xall_ref.at[origin, 1 - core], xsems, 10 + step)
    remote(first_ref, first_ref, (msend, mrecv), 0, mirror).wait_recv()
    for copy in started:
        copy.wait_send()
    for copy in outs + [own_w, own_x]:
        copy.wait()


def gather_parts(x_factor, shard, amp4, core, early, split):
    rows = lax.axis_size("row")
    cols = lax.axis_size("col")
    width = amp4.shape[1]
    hbm = pl.BlockSpec(memory_space=pl.ANY)
    bf16 = jnp.bfloat16
    dma = pltpu.SemaphoreType.DMA
    shapes = [(rows,) + x_factor.shape, (cols,) + shard.shape, (2,) + shard.shape, (width, early), core.shape]
    shapes += [(width, 2 * width - early), (width, width)]
    shapes += [(width, split), (width, width - split)]
    return pl.pallas_call(
        gather_kernel,
        out_shape=[jax.ShapeDtypeStruct(shape, bf16) for shape in shapes],
        in_specs=[hbm] * 4,
        out_specs=[hbm] * len(shapes),
        scratch_shapes=[
            pltpu.VMEM(amp4.shape, bf16),
            pltpu.VMEM(amp4.shape, bf16),
            pltpu.VMEM((2,) + core.shape, bf16),
            dma((12,)),
            dma((12,)),
            dma((14,)),
            dma((14,)),
            dma((1,)),
            dma((1,)),
            dma((8,)),
            dma((5,)),
        ],
        compiler_params=pltpu.CompilerParams(
            collective_id=0, has_side_effects=True, vmem_limit_bytes=VMEM_LIMIT
        ),
        name="gather_parts",
    )(x_factor, shard, amp4, core)


def own_ladder_kernel(
    tiles_ref, count_ref, slot_ref, xall_ref, amps_ref, core_ref, x_ref, xt_ref, wt_ref, gathered, proj, sem
):
    @pl.when(pl.program_id(0) == 0)
    def _():
        tile = xall_ref.shape[1]
        copies = []
        for s in range(tiles_ref.shape[0]):
            copy = pltpu.make_async_copy(
                xall_ref.at[slot_ref[tiles_ref[s]]], gathered.at[pl.ds(s * tile, tile), :], sem.at[s]
            )
            copy.start()
            copies.append(copy)
        for copy in copies:
            copy.wait()
        live = lax.broadcasted_iota(jnp.int32, (x_ref.shape[0], 1), 0) < count_ref[0, 0] * tile
        x_ref[...] = jnp.where(live, gathered[...].astype(jnp.float32), 0.0).astype(x_ref.dtype)
        for cut in strips(x_ref.shape[0], 256):
            xt_ref[:, cut] = x_ref[cut, :].T

    proj[...] = dot(xt_ref[...], amps_ref[0]).astype(proj.dtype)
    inner = dot(proj[...], x_ref[...])
    wt_ref[0] = (core_ref[...].astype(jnp.float32) * inner).astype(wt_ref.dtype)


def own_ladder(tiles, count, tile_slot, xall, amp4, core):
    width = amp4.shape[1]
    points = core.shape[0]
    smem = pl.BlockSpec(memory_space=pltpu.SMEM)
    bf16 = jnp.bfloat16

    def whole(shape):
        return pl.BlockSpec(shape, lambda p: (0, 0))

    return pl.pallas_call(
        own_ladder_kernel,
        out_shape=(
            jax.ShapeDtypeStruct((width, points), bf16),
            jax.ShapeDtypeStruct((points, width), bf16),
            jax.ShapeDtypeStruct((4, points, points), bf16),
        ),
        grid=(4,),
        in_specs=[
            smem, smem, smem, pl.BlockSpec(memory_space=pl.ANY),
            pl.BlockSpec((1, width, width), lambda p: (p, 0, 0)), whole((points, points)),
        ],
        out_specs=(
            whole((width, points)), whole((points, width)),
            pl.BlockSpec((1, points, points), lambda p: (p, 0, 0)),
        ),
        scratch_shapes=[
            pltpu.VMEM((width, points), bf16),
            pltpu.VMEM((points, width), bf16),
            pltpu.SemaphoreType.DMA((tiles.shape[0],)),
        ],
        compiler_params=pltpu.CompilerParams(vmem_limit_bytes=VMEM_LIMIT),
        name="own_ladder",
    )(tiles, count, tile_slot, xall, amp4, core)


def window_index(tiles_ref, count_ref, tile, shape, axis):
    at = lax.broadcasted_iota(jnp.int32, shape, axis)
    index = jnp.full(shape, -1, jnp.int32)
    for s in range(tiles_ref.shape[0]):
        inside = (at >= s * tile) & (at < (s + 1) * tile) & (s < count_ref[0, 0])
        index = jnp.where(inside, at + (tiles_ref[s] - s) * tile, index)
    return index


def own_cycle_kernel(
    tiles_ref, count_ref, virt_ref, wall_ref, far_ref, side_ref, twin_ref, a0_ref, a1_ref,
    wd_ref, cyc_ref, vcol_ref, vrow_ref, wsel, pick, sem,
):
    p = pl.program_id(0)
    tile = wall_ref.shape[2]
    slots = tiles_ref.shape[0]
    width = wd_ref.shape[1]
    window = virt_ref.shape[1]

    @pl.when(p == 0)
    def _():
        me = lax.axis_index("col")
        for first in range(2):
            for s in range(slots):
                number = tiles_ref[s]
                offset = ((number >> 2) + 4 - (me >> 2)) & 3
                plane = ((number >> 1) + (me >> 1)) & 1
                side = (number + me) & 1
                apart = (offset == 1) | (offset == 2)
                dst = wsel.at[pl.ds(2 * first, 2), pl.ds(s * tile, tile), :]

                def fetch(source, at, dst=dst, done=sem.at[first, s], first=first):
                    pltpu.make_async_copy(source.at[at, pl.ds(2 * first, 2)], dst, done).start()

                @pl.when(jnp.logical_not(apart) | ((plane == 0) & (side == 1)))
                def _(number=number, fetch=fetch):
                    fetch(wall_ref, number)

                for source, at_plane, at_side in ((far_ref, 0, 0), (side_ref, 1, 0), (twin_ref, 1, 1)):

                    @pl.when(apart & (plane == at_plane) & (side == at_side))
                    def _(source=source, offset=offset, fetch=fetch):
                        fetch(source, offset - 1)

        along = lax.broadcasted_iota(jnp.int32, pick.shape, 0)
        picked = window_index(tiles_ref, count_ref, tile, (1, width), 1)
        pick[...] = jnp.where(along == picked, 1.0, 0.0).astype(pick.dtype)
        picked = window_index(tiles_ref, count_ref, tile, (width, 1), 0)
        along = lax.broadcasted_iota(jnp.int32, (width, window), 1)
        levels = jnp.sum(jnp.where(along == picked, virt_ref[...], 0.0), axis=1, keepdims=True)
        vcol_ref[...] = levels
        vrow_ref[...] = jnp.broadcast_to(levels, (width, 128)).T[:1, :]

    for first in range(2):

        @pl.when(p == 2 * first)
        def _(first=first):
            for s in range(slots):
                pltpu.make_async_copy(
                    wall_ref.at[0, pl.ds(0, 2)],
                    wsel.at[pl.ds(2 * first, 2), pl.ds(s * tile, tile), :],
                    sem.at[first, s],
                ).wait()
            for k in range(2):
                wd_ref[k] = dot(wsel[2 * first + k], pick[...]).astype(wd_ref.dtype)

    cyc_ref[0] = dot(wd_ref[0], a0_ref[0]) + dot(wd_ref[1], a1_ref[0])


def own_cycle(tiles, count, virt, wall, far, side, twin, amp4):
    width = amp4.shape[1]
    slots, window = tiles.shape[0], wall.shape[3]
    smem = pl.BlockSpec(memory_space=pltpu.SMEM)
    hbm = pl.BlockSpec(memory_space=pl.ANY)
    f32, bf16 = jnp.float32, jnp.bfloat16
    return pl.pallas_call(
        own_cycle_kernel,
        out_shape=(
            jax.ShapeDtypeStruct((4, width, width), bf16),
            jax.ShapeDtypeStruct((4, width, width), f32),
            jax.ShapeDtypeStruct((width, 1), f32),
            jax.ShapeDtypeStruct((1, width), f32),
        ),
        grid=(4,),
        in_specs=[
            smem,
            smem,
            pl.BlockSpec((1, window), lambda p: (0, 0)),
            hbm,
            hbm,
            hbm,
            hbm,
            pl.BlockSpec((1, width, width), lambda p: (p % 2, 0, 0)),
            pl.BlockSpec((1, width, width), lambda p: (2 + p % 2, 0, 0)),
        ],
        out_specs=(
            pl.BlockSpec((2, width, width), lambda p: (p // 2, 0, 0)),
            pl.BlockSpec((1, width, width), lambda p: (p, 0, 0)),
            pl.BlockSpec((width, 1), lambda p: (0, 0)),
            pl.BlockSpec((1, width), lambda p: (0, 0)),
        ),
        scratch_shapes=[
            pltpu.VMEM((4, width, window), bf16),
            pltpu.VMEM((window, width), bf16),
            pltpu.SemaphoreType.DMA((2, slots)),
        ],
        compiler_params=pltpu.CompilerParams(vmem_limit_bytes=VMEM_LIMIT),
        name="own_cycle",
    )(tiles, count, virt, wall, far, side, twin, amp4, amp4)


class Mover:
    def __init__(self, stages, in_sem, out_sem):
        self.in_sem = in_sem
        self.out_sem = out_sem
        self.outs = []
        self.stages = stages
        self.waiting = {}
        self.begun = 0
        self.count = 0
        self.advance(2)

    def advance(self, upto):
        while self.begun < min(upto, len(self.stages)):
            for name, (src, dst) in self.stages[self.begun].items():
                copy = pltpu.make_async_copy(src, dst, self.in_sem.at[self.count])
                copy.start()
                self.waiting[name] = (copy, self.begun)
                self.count += 1
            self.begun += 1

    def need(self, *names):
        for name in names:
            if name in self.waiting:
                copy, stage = self.waiting.pop(name)
                copy.wait()
                self.advance(stage + 3)

    def put(self, src, dst):
        copy = pltpu.make_async_copy(src, dst, self.out_sem.at[len(self.outs)])
        copy.start()
        self.outs.append(copy)

    def drain(self):
        for copy in self.outs:
            copy.wait()


def emit(mover, last, pair, j, rows, raw, count_ref, occ_ref, vcol_ref, vrow_ref, part, amps, upd, res_hbm, upd_hbm):
    raw = raw + part[j, rows, :]
    if last:
        count = count_ref[0, 0] * 64
        height, width = raw.shape
        live = (lax.broadcasted_iota(jnp.int32, (height, 1), 0) + rows.start < count) & (
            lax.broadcasted_iota(jnp.int32, (1, width), 1) < count
        )
        raw = jnp.where(live, raw, 0.0)
        own = jnp.where(live, amps[j, rows, :].astype(jnp.float32), 0.0)
        gap = (occ_ref[0, pair // 2] + occ_ref[1, pair % 2]) - vcol_ref[rows, :] - vrow_ref[...]
        upd[j, rows, :] = (own + raw / gap).astype(upd.dtype)
        mover.put(upd.at[j, rows, :], upd_hbm.at[pair, rows, :])
    part[j, rows, :] = raw
    mover.put(part.at[j, rows, :], res_hbm.at[pair, rows, :])


def row_kernel(
    i, count_ref, occ_ref, vcol_ref, vrow_ref, b0_hbm, b1_hbm, xt_hbm, x_hbm, coret_hbm, wt_hbm, wd_hbm,
    amps_hbm, part_hbm, res_hbm, upd_hbm, xt, coret, wt, right, left, part, amps, proj, total, upd, sem, osem,
):
    width, points = x_hbm.shape
    early = b0_hbm.shape[1]
    head = pl.ds(0, points)
    blocks = [pl.ds(points + k * width, width) for k in range(2)]
    ends = []
    for j in range(2):
        stage = {"w%d%d" % (j, k): (wd_hbm.at[2 * j + k], right.at[j, :, blocks[k]]) for k in range(2)}
        stage["part%d" % j] = (part_hbm.at[2 * i + j], part.at[j])
        stage["amps%d" % j] = (amps_hbm.at[2 * i + j], amps.at[j])
        if j == 1:
            stage["x1"] = (x_hbm, right.at[1, :, head])
        ends.append(stage)
    stages = [
        {
            "xt": (xt_hbm, xt),
            "b0": (b0_hbm, left.at[:, pl.ds(points, early)]),
            "b1": (b1_hbm, left.at[:, pl.ds(points + early, 2 * width - early)]),
        },
        {
            "x0": (x_hbm, right.at[0, :, head]),
            "coret": (coret_hbm, coret),
            "wt": (wt_hbm.at[pl.ds(2 * i, 2)], wt),
        },
    ]
    mover = Mover(stages + ends, sem, osem)
    for j in range(2):
        mover.need("b0", "b1", "xt")
        proj[...] = dot(xt[...], left[:, blocks[j]]).astype(proj.dtype)
        mover.need("x0", "coret", "wt")
        inner = dot(proj[...], right[0, :, head])
        total[j] = (
            wt[j].astype(jnp.float32) + coret[...].astype(jnp.float32) * inner
        ).astype(total.dtype)
    for j in range(2):
        left[:, head] = dot(right[0, :, head], total[j]).astype(left.dtype)
        mover.need("x%d" % j, "w%d0" % j, "w%d1" % j, "part%d" % j, "amps%d" % j)
        for rows in strips(width, STRIP):
            raw = dot_nt(left[rows, :], right[j])
            emit(
                mover, True, 2 * i + j, j, rows, raw, count_ref, occ_ref, vcol_ref, vrow_ref,
                part, amps, upd, res_hbm, upd_hbm,
            )
    mover.drain()


def row(i, count, occ, vcol, vrow, b0, b1, xt, x, coret, wt, wd, amp4, part):
    width, points = x.shape
    vmem = pl.BlockSpec(memory_space=pltpu.VMEM)
    smem = pl.BlockSpec(memory_space=pltpu.SMEM)
    hbm = pl.BlockSpec(memory_space=pl.ANY)
    f32, bf16 = jnp.float32, jnp.bfloat16
    depth = points + 2 * width
    return pl.pallas_call(
        functools.partial(row_kernel, i),
        out_shape=[jax.ShapeDtypeStruct(part.shape, f32), jax.ShapeDtypeStruct(part.shape, bf16)],
        in_specs=[smem, smem, vmem, vmem] + [hbm] * 9,
        out_specs=[hbm] * 2,
        scratch_shapes=[
            pltpu.VMEM((points, width), bf16),
            pltpu.VMEM((points, points), bf16),
            pltpu.VMEM((2, points, points), bf16),
            pltpu.VMEM((2, width, depth), bf16),
            pltpu.VMEM((width, depth), bf16),
            pltpu.VMEM((2, width, width), f32),
            pltpu.VMEM((2, width, width), bf16),
            pltpu.VMEM((points, width), bf16),
            pltpu.VMEM((2, points, points), bf16),
            pltpu.VMEM((2, width, width), bf16),
            pltpu.SemaphoreType.DMA((15,)),
            pltpu.SemaphoreType.DMA((4 * (width // STRIP),)),
        ],
        input_output_aliases={12: 0},
        compiler_params=pltpu.CompilerParams(vmem_limit_bytes=VMEM_LIMIT),
        name="row_%d" % i,
    )(count, occ, vcol, vrow, b0, b1, xt, x, coret, wt, wd, amp4, part)


def piece_kernel(i, k, low, high, end, count_ref, occ_ref, vcol_ref, vrow_ref, *refs):
    last = k == 1 and end
    scratch = 13
    refs, (xt, coret, wt, right, left, part, amps, acc, proj, total, upd, sem, osem) = (
        refs[:-scratch], refs[-scratch:]
    )
    (b_hbm, xt_hbm, x_hbm, coret_hbm, wt_hbm, wd_hbm, amps_hbm, part_hbm) = refs[:8]
    refs = list(refs[8:])
    acc_in = refs.pop(0) if low > 0 else None
    upd_hbm = refs.pop() if last else None
    acc_out = None if end else refs.pop()
    res_hbm = refs.pop()
    width, points = x_hbm.shape
    head, rest = pl.ds(0, points), pl.ds(points, high - low)
    cut = pl.ds(low, high - low)
    stages = [{"b": (b_hbm, left.at[:, rest]), "xt": (xt_hbm, xt)}, {"x": (x_hbm, right.at[k, :, head])}]
    stages.append({"coret": (coret_hbm, coret)})
    if low > 0:
        stages[2]["acc"] = (acc_in, acc)
    else:
        stages[2]["wt"] = (wt_hbm.at[2 * i + k], wt)
    for j in (1 - k, k):
        stages.append({
            "w%d" % j: (wd_hbm.at[2 * j + k, :, cut], right.at[j, :, rest]),
            "part%d" % j: (part_hbm.at[2 * i + j], part.at[j]),
        })
        if last:
            stages[-1]["amps%d" % j] = (amps_hbm.at[2 * i + j], amps.at[j])
    mover = Mover(stages, sem, osem)

    def products(j, columns):
        mover.need("w%d" % j, "part%d" % j, "amps%d" % j)
        for rows in strips(width, STRIP):
            raw = dot_nt(left[rows, columns], right[j, :, columns])
            emit(
                mover, last, 2 * i + j, j, rows, raw, count_ref, occ_ref, vcol_ref, vrow_ref,
                part, amps, upd, res_hbm, upd_hbm,
            )

    mover.need("b", "xt")
    proj[...] = dot(xt[...], left[:, rest]).astype(proj.dtype)
    mover.need("x")
    inner = dot(proj[...], right[k, cut, head])
    mover.need("coret", "wt", "acc")
    before = acc[...] if low > 0 else wt[...].astype(jnp.float32)
    inner = before + coret[...].astype(jnp.float32) * inner
    if end:
        total[...] = inner.astype(total.dtype)
        left[:, head] = dot(right[k, :, head], total[...]).astype(left.dtype)
        products(1 - k, rest)
        products(k, pl.ds(0, points + high - low))
    else:
        acc[...] = inner
        mover.put(acc, acc_out)
        for j in (1 - k, k):
            products(j, rest)
    mover.drain()


def piece(i, k, low, high, count, occ, vcol, vrow, b, xt, x, coret, wt, wd, amp4, part, acc, updated):
    width, points = x.shape
    end = high == width
    last = k == 1 and end
    vmem = pl.BlockSpec(memory_space=pltpu.VMEM)
    smem = pl.BlockSpec(memory_space=pltpu.SMEM)
    hbm = pl.BlockSpec(memory_space=pl.ANY)
    f32, bf16 = jnp.float32, jnp.bfloat16
    operands = [count, occ, vcol, vrow, b, xt, x, coret, wt, wd, amp4, part]
    out_shape = [jax.ShapeDtypeStruct(part.shape, f32)]
    alias = {len(operands) - 1: 0}
    if low > 0:
        operands.append(acc)
    if not end:
        out_shape.append(jax.ShapeDtypeStruct((points, points), f32))
    if last:
        out_shape.append(jax.ShapeDtypeStruct(part.shape, bf16))
        alias[len(operands)] = 1
        operands.append(updated)
    return pl.pallas_call(
        functools.partial(piece_kernel, i, k, low, high, end),
        out_shape=out_shape,
        in_specs=[smem, smem, vmem, vmem] + [hbm] * (len(operands) - 4),
        out_specs=[hbm] * len(out_shape),
        scratch_shapes=[
            pltpu.VMEM((points, width), bf16),
            pltpu.VMEM((points, points), bf16),
            pltpu.VMEM((points, points), bf16),
            pltpu.VMEM((2, width, points + high - low), bf16),
            pltpu.VMEM((width, points + high - low), bf16),
            pltpu.VMEM((2, width, width), f32),
            pltpu.VMEM((2, width, width), bf16),
            pltpu.VMEM((points, points), f32),
            pltpu.VMEM((points, high - low), bf16),
            pltpu.VMEM((points, points), bf16),
            pltpu.VMEM((2, width, width), bf16),
            pltpu.SemaphoreType.DMA((12,)),
            pltpu.SemaphoreType.DMA((9,)),
        ],
        input_output_aliases=alias,
        compiler_params=pltpu.CompilerParams(vmem_limit_bytes=VMEM_LIMIT),
        name="piece_%d%d_%d" % (i, k, low),
    )(*operands)


def per_device(
    amps, x_factor, core, cycle_w, domain_tiles, domain_count, tile_slot, occ_energy, virt_energy
):
    occ = amps.shape[2]
    width = amps.shape[4]
    tile_width = x_factor.shape[1]
    grid_points = x_factor.shape[2]
    window = cycle_w.shape[4]
    cols = lax.axis_size("col")
    amp4 = amps[0, 0].reshape(occ * occ, width, width)
    shard = cycle_w[0].reshape(occ * occ, tile_width, window)

    early, split = width // 2, 512
    xall, wall, far, first, coret, *turned = gather_parts(x_factor, shard, amp4, core, early, split)
    xall = xall.reshape(-1, tile_width, grid_points)
    mirror = [(i, (i + cols // 2) % cols) for i in range(cols)]
    second, third, fourth = [lax.ppermute(part, "col", mirror) for part in turned[:3]]
    side = lax.ppermute(far, "col", [(i, i ^ 2) for i in range(cols)])

    tiles, count = domain_tiles[0, 0], domain_count
    x, xt, wt = own_ladder(tiles, count, tile_slot, xall, amp4, core)
    side, tail, wt = lax.optimization_barrier((side, turned[3], wt))
    fifth = lax.ppermute(tail, "col", mirror)
    twin = lax.ppermute(side, "col", [(i, i ^ 1) for i in range(cols)])
    wd, part, vcol, vrow = own_cycle(tiles, count, virt_energy[None, :], wall, far, side, twin, amp4)
    energies = (count, occ_energy[0, 0], vcol, vrow)
    part, updated = row(0, *energies, first, second, xt, x, coret, wt, wd, amp4, part)
    fixed = (xt, x, coret, wt, wd, amp4)
    part, = piece(1, 0, 0, width, *energies, third, *fixed, part, None, None)
    part, acc = piece(1, 1, 0, split, *energies, fourth, *fixed, part, None, None)
    part, updated = piece(1, 1, split, width, *energies, fifth, *fixed, part, acc, updated)
    return part.reshape(amps.shape), updated.reshape(amps.shape)


def solution(mesh):
    in_specs = (
        P("row", "col", None, None, None, None),
        P("row", None, None),
        P(),
        P("row", None, None, "col", None),
        P("row", "col", None),
        P("row", "col"),
        P(),
        P("row", "col", None, None),
        P(),
    )
    out_specs = (P("row", "col", None, None, None, None), P("row", "col", None, None, None, None))
    return jax.shard_map(
        per_device, mesh=mesh, in_specs=in_specs, out_specs=out_specs, check_vma=False
    )
```

```python
import functools

import jax
import jax.numpy as jnp
from jax import lax
from jax.experimental import pallas as pl
from jax.experimental.pallas import tpu as pltpu
from jax.sharding import PartitionSpec as P

MESH = pl.DeviceIdType.MESH
VMEM_LIMIT = 65300 * 1024
STRIP = 384


def dot(a, b):
    return jnp.dot(a, b, preferred_element_type=jnp.float32)


def dot_nt(a, b):
    return lax.dot_general(a, b, (((1,), (1,)), ((), ())), preferred_element_type=jnp.float32)


def strips(width, step):
    return [pl.ds(start, step) for start in range(0, width, step)]


def remote(src, dst, sems, index, device):
    return pltpu.make_async_remote_copy(
        src_ref=src, dst_ref=dst, send_sem=sems[0].at[index], recv_sem=sems[1].at[index],
        device_id=device, device_id_type=MESH,
    )


def greet(devices):
    barrier = pltpu.get_barrier_semaphore()
    for device in devices:
        pl.semaphore_signal(barrier, inc=1, device_id=device, device_id_type=MESH)
    pl.semaphore_wait(barrier, len(devices))


def gather_kernel(
    count_ref, x_ref, w_ref, amps_ref, core_ref,
    xall_ref, wall_ref, far_ref, first_ref, coret_ref, live_ref, *refs
):
    cuts, (plain, turned, fixed, wsend, wrecv, xsend, xrecv, msend, mrecv, local, tsem) = refs[:-11], refs[-11:]
    r = lax.axis_index("row")
    c = lax.axis_index("col")
    rows = lax.axis_size("row")
    cols = lax.axis_size("col")
    forth = (r, (c + 4) % cols)
    back = (r, (c + cols - 4) % cols)
    mirror = (r, (c + cols // 2) % cols)
    zside = (r, c + 2 - 4 * ((c // 2) % 2))
    twin = (r, c + 1 - 2 * (c % 2))
    beside = r + 1 - 2 * (r % 2)
    core = c % 2
    half = w_ref.shape[0] // 2
    width = plain.shape[1]
    y_steps = range(1, rows // 2)

    amps_in = [pltpu.make_async_copy(amps_ref.at[q], plain.at[q], tsem.at[q]) for q in range(4)]
    core_in = pltpu.make_async_copy(core_ref, fixed.at[0], tsem.at[4])
    for copy in amps_in + [core_in]:
        copy.start()
    greet(
        [forth, back, mirror, zside, twin, (beside, c)]
        + [((r + 2 * step) % rows, c) for step in y_steps]
    )
    wsems, xsems = (wsend, wrecv), (xsend, xrecv)
    started = []

    def send(*args):
        copy = remote(*args)
        copy.start()
        started.append(copy)

    def arrived(part, sems, index):
        remote(part, part, sems, index, twin).wait_recv()

    def shard(offset, plane, side):
        if offset in (1, 2) and plane + side == 0:
            return far_ref.at[offset - 1]
        x = (c // 4 + offset) % (cols // 4)
        z = (c // 2) % 2
        z = z + plane * (1 - 2 * z)
        k = core + side * (1 - 2 * core)
        return wall_ref.at[x * 4 + z * 2 + k]

    def to_twin(offset):
        x = (c // 4 + offset) % (cols // 4)
        send(shard(offset, 0, 0), wall_ref.at[x * 4 + c % 4], wsems, 6 + offset, twin)

    def live(shape, axis):
        at = lax.broadcasted_iota(jnp.int32, shape, axis)
        return jnp.where(at < count_ref[0, 0] * x_ref.shape[1], 1.0, 0.0)

    live_rows, live_cols = live((width, 1), 0), live((1, width), 1)

    def transpose(q, p):
        amps_in[q].wait()
        for cut in strips(width, 256):
            mask = live_rows[cut.start:cut.start + cut.size] * live_cols
            plain[q, cut, :] = (plain[q, cut, :].astype(jnp.float32) * mask).astype(plain.dtype)
            turned[p, :, cut] = plain[q, cut, :].T

    own = wall_ref.at[c]
    send(w_ref, own, wsems, 0, forth)
    send(w_ref, far_ref.at[0], wsems, 1, back)
    send(x_ref.at[core], xall_ref.at[r, core], xsems, 0, (beside, c))
    send(w_ref, own, wsems, 4, zside)
    for step in y_steps:
        send(x_ref.at[core], xall_ref.at[r, core], xsems, step, ((r + 2 * step) % rows, c))
    send(w_ref, own, wsems, 6, twin)
    own_w = pltpu.make_async_copy(w_ref, own, local.at[0])
    own_x = pltpu.make_async_copy(x_ref, xall_ref.at[r], local.at[1])
    own_w.start()
    own_x.start()
    transpose(0, 0)

    part = xall_ref.at[beside, core]
    arrived(part, xsems, 0)
    for step in y_steps:
        send(part, part, xsems, 3 + step, ((r + 2 * step) % rows, c))
    send(part, part, xsems, 7, twin)

    part = shard(3, 0, 0)
    arrived(part, wsems, 0)
    send(part.at[:half], far_ref.at[1, :half], wsems, 2, forth)
    send(part, part, wsems, 5, zside)
    arrived(far_ref.at[0], wsems, 1)
    send(far_ref.at[0, half:], far_ref.at[1, half:], wsems, 3, back)
    send(turned.at[0, :, pl.ds(0, first_ref.shape[1])], first_ref, (msend, mrecv), 0, mirror)
    to_twin(3)
    to_twin(1)
    transpose(2, 1)
    for step in y_steps:
        origin = (r + rows - 2 * step) % rows
        arrived(xall_ref.at[origin, core], xsems, step)
        send(xall_ref.at[origin, core], xall_ref.at[origin, core], xsems, 7 + step, twin)
    transpose(1, 2)
    part = shard(0, 1, 0)
    arrived(part, wsems, 4)
    send(part, part, wsems, 10, twin)
    for step in y_steps:
        origin = (r + rows - 2 * step) % rows
        origin = origin + 1 - 2 * (origin % 2)
        arrived(xall_ref.at[origin, core], xsems, 3 + step)
        send(xall_ref.at[origin, core], xall_ref.at[origin, core], xsems, 10 + step, twin)
    arrived(far_ref.at[1, :half], wsems, 2)
    arrived(far_ref.at[1, half:], wsems, 3)
    to_twin(2)
    transpose(3, 3)
    early, split = first_ref.shape[1], cuts[2].shape[1]
    moves = (
        (0, pl.ds(early, width - early), 0, pl.ds(0, width - early)),
        (1, pl.ds(0, width), 0, pl.ds(width - early, width)),
        (2, pl.ds(0, width), 1, pl.ds(0, width)),
        (3, pl.ds(0, split), 2, pl.ds(0, split)),
        (3, pl.ds(split, width - split), 3, pl.ds(0, width - split)),
    )
    outs = [
        pltpu.make_async_copy(turned.at[p, :, source], cuts[q].at[:, target], local.at[3 + at])
        for at, (p, source, q, target) in enumerate(moves)
    ]
    core_in.wait()
    for cut in strips(width, 256):
        fixed[1, :, cut] = fixed[0, cut, :].T
    outs.append(pltpu.make_async_copy(fixed.at[1], coret_ref, local.at[2]))
    outs.append(pltpu.make_async_copy(plain, live_ref, local.at[8]))
    for copy in outs:
        copy.start()
    part = shard(3, 1, 0)
    arrived(part, wsems, 5)
    send(part, part, wsems, 11, twin)

    for offset in range(4):
        arrived(shard(offset, 0, 1), wsems, 6 + offset)
    arrived(shard(0, 1, 1), wsems, 10)
    arrived(shard(3, 1, 1), wsems, 11)
    arrived(xall_ref.at[beside, 1 - core], xsems, 7)
    for step in y_steps:
        origin = (r + rows - 2 * step) % rows
        arrived(xall_ref.at[origin, 1 - core], xsems, 7 + step)
        origin = origin + 1 - 2 * (origin % 2)
        arrived(xall_ref.at[origin, 1 - core], xsems, 10 + step)
    remote(first_ref, first_ref, (msend, mrecv), 0, mirror).wait_recv()
    for copy in started:
        copy.wait_send()
    for copy in outs + [own_w, own_x]:
        copy.wait()


def gather_parts(count, x_factor, shard, amp4, core, early, split):
    rows = lax.axis_size("row")
    cols = lax.axis_size("col")
    width = amp4.shape[1]
    hbm = pl.BlockSpec(memory_space=pl.ANY)
    bf16 = jnp.bfloat16
    dma = pltpu.SemaphoreType.DMA
    shapes = [(rows,) + x_factor.shape, (cols,) + shard.shape, (2,) + shard.shape, (width, early), core.shape, amp4.shape]
    shapes += [(width, 2 * width - early), (width, width)]
    shapes += [(width, split), (width, width - split)]
    return pl.pallas_call(
        gather_kernel,
        out_shape=[jax.ShapeDtypeStruct(shape, bf16) for shape in shapes],
        in_specs=[pl.BlockSpec(memory_space=pltpu.SMEM)] + [hbm] * 4,
        out_specs=[hbm] * len(shapes),
        scratch_shapes=[
            pltpu.VMEM(amp4.shape, bf16),
            pltpu.VMEM(amp4.shape, bf16),
            pltpu.VMEM((2,) + core.shape, bf16),
            dma((12,)),
            dma((12,)),
            dma((14,)),
            dma((14,)),
            dma((1,)),
            dma((1,)),
            dma((9,)),
            dma((5,)),
        ],
        compiler_params=pltpu.CompilerParams(
            collective_id=0, has_side_effects=True, vmem_limit_bytes=VMEM_LIMIT
        ),
        name="gather_parts",
    )(count, x_factor, shard, amp4, core)


def own_ladder_kernel(
    tiles_ref, count_ref, slot_ref, xall_ref, amps_ref, core_ref, x_ref, xt_ref, wt_ref, gathered, proj, sem
):
    @pl.when(pl.program_id(0) == 0)
    def _():
        tile = xall_ref.shape[1]
        copies = []
        for s in range(tiles_ref.shape[0]):
            copy = pltpu.make_async_copy(
                xall_ref.at[slot_ref[tiles_ref[s]]], gathered.at[pl.ds(s * tile, tile), :], sem.at[s]
            )
            copy.start()
            copies.append(copy)
        for copy in copies:
            copy.wait()
        live = lax.broadcasted_iota(jnp.int32, (x_ref.shape[0], 1), 0) < count_ref[0, 0] * tile
        x_ref[...] = jnp.where(live, gathered[...].astype(jnp.float32), 0.0).astype(x_ref.dtype)
        for cut in strips(x_ref.shape[0], 256):
            xt_ref[:, cut] = x_ref[cut, :].T

    proj[...] = dot(xt_ref[...], amps_ref[0]).astype(proj.dtype)
    inner = dot(proj[...], x_ref[...])
    wt_ref[0] = (core_ref[...].astype(jnp.float32) * inner).astype(wt_ref.dtype)


def own_ladder(tiles, count, tile_slot, xall, amp4, core):
    width = amp4.shape[1]
    points = core.shape[0]
    smem = pl.BlockSpec(memory_space=pltpu.SMEM)
    bf16 = jnp.bfloat16

    def whole(shape):
        return pl.BlockSpec(shape, lambda p: (0, 0))

    return pl.pallas_call(
        own_ladder_kernel,
        out_shape=(
            jax.ShapeDtypeStruct((width, points), bf16),
            jax.ShapeDtypeStruct((points, width), bf16),
            jax.ShapeDtypeStruct((4, points, points), bf16),
        ),
        grid=(4,),
        in_specs=[
            smem, smem, smem, pl.BlockSpec(memory_space=pl.ANY),
            pl.BlockSpec((1, width, width), lambda p: (p, 0, 0)), whole((points, points)),
        ],
        out_specs=(
            whole((width, points)), whole((points, width)),
            pl.BlockSpec((1, points, points), lambda p: (p, 0, 0)),
        ),
        scratch_shapes=[
            pltpu.VMEM((width, points), bf16),
            pltpu.VMEM((points, width), bf16),
            pltpu.SemaphoreType.DMA((tiles.shape[0],)),
        ],
        compiler_params=pltpu.CompilerParams(vmem_limit_bytes=VMEM_LIMIT),
        name="own_ladder",
    )(tiles, count, tile_slot, xall, amp4, core)


def window_index(tiles_ref, count_ref, tile, shape, axis):
    at = lax.broadcasted_iota(jnp.int32, shape, axis)
    index = jnp.full(shape, -1, jnp.int32)
    for s in range(tiles_ref.shape[0]):
        inside = (at >= s * tile) & (at < (s + 1) * tile) & (s < count_ref[0, 0])
        index = jnp.where(inside, at + (tiles_ref[s] - s) * tile, index)
    return index


def own_cycle_kernel(
    tiles_ref, count_ref, virt_ref, wall_ref, far_ref, side_ref, twin_ref, a0_ref, a1_ref,
    wd_ref, cyc_ref, vcol_ref, vrow_ref, wsel, pick, sem,
):
    p = pl.program_id(0)
    tile = wall_ref.shape[2]
    slots = tiles_ref.shape[0]
    width = wd_ref.shape[1]
    window = virt_ref.shape[1]

    @pl.when(p == 0)
    def _():
        me = lax.axis_index("col")
        for first in range(2):
            for s in range(slots):
                number = tiles_ref[s]
                offset = ((number >> 2) + 4 - (me >> 2)) & 3
                plane = ((number >> 1) + (me >> 1)) & 1
                side = (number + me) & 1
                apart = (offset == 1) | (offset == 2)
                dst = wsel.at[pl.ds(2 * first, 2), pl.ds(s * tile, tile), :]

                def fetch(source, at, dst=dst, done=sem.at[first, s], first=first):
                    pltpu.make_async_copy(source.at[at, pl.ds(2 * first, 2)], dst, done).start()

                @pl.when(jnp.logical_not(apart) | ((plane == 0) & (side == 1)))
                def _(number=number, fetch=fetch):
                    fetch(wall_ref, number)

                for source, at_plane, at_side in ((far_ref, 0, 0), (side_ref, 1, 0), (twin_ref, 1, 1)):

                    @pl.when(apart & (plane == at_plane) & (side == at_side))
                    def _(source=source, offset=offset, fetch=fetch):
                        fetch(source, offset - 1)

        along = lax.broadcasted_iota(jnp.int32, pick.shape, 0)
        picked = window_index(tiles_ref, count_ref, tile, (1, width), 1)
        pick[...] = jnp.where(along == picked, 1.0, 0.0).astype(pick.dtype)
        picked = window_index(tiles_ref, count_ref, tile, (width, 1), 0)
        along = lax.broadcasted_iota(jnp.int32, (width, window), 1)
        levels = jnp.sum(jnp.where(along == picked, virt_ref[...], 0.0), axis=1, keepdims=True)
        vcol_ref[...] = levels
        vrow_ref[...] = jnp.broadcast_to(levels, (width, 128)).T[:1, :]

    for first in range(2):

        @pl.when(p == 2 * first)
        def _(first=first):
            for s in range(slots):
                pltpu.make_async_copy(
                    wall_ref.at[0, pl.ds(0, 2)],
                    wsel.at[pl.ds(2 * first, 2), pl.ds(s * tile, tile), :],
                    sem.at[first, s],
                ).wait()
            live = lax.broadcasted_iota(jnp.int32, (width, 1), 0) < count_ref[0, 0] * tile
            for k in range(2):
                picked = dot(wsel[2 * first + k], pick[...])
                wd_ref[k] = jnp.where(live, picked, 0.0).astype(wd_ref.dtype)

    cyc_ref[0] = dot(wd_ref[0], a0_ref[0]) + dot(wd_ref[1], a1_ref[0])


def own_cycle(tiles, count, virt, wall, far, side, twin, amp4):
    width = amp4.shape[1]
    slots, window = tiles.shape[0], wall.shape[3]
    smem = pl.BlockSpec(memory_space=pltpu.SMEM)
    hbm = pl.BlockSpec(memory_space=pl.ANY)
    f32, bf16 = jnp.float32, jnp.bfloat16
    return pl.pallas_call(
        own_cycle_kernel,
        out_shape=(
            jax.ShapeDtypeStruct((4, width, width), bf16),
            jax.ShapeDtypeStruct((4, width, width), f32),
            jax.ShapeDtypeStruct((width, 1), f32),
            jax.ShapeDtypeStruct((1, width), f32),
        ),
        grid=(4,),
        in_specs=[
            smem,
            smem,
            pl.BlockSpec((1, window), lambda p: (0, 0)),
            hbm,
            hbm,
            hbm,
            hbm,
            pl.BlockSpec((1, width, width), lambda p: (p % 2, 0, 0)),
            pl.BlockSpec((1, width, width), lambda p: (2 + p % 2, 0, 0)),
        ],
        out_specs=(
            pl.BlockSpec((2, width, width), lambda p: (p // 2, 0, 0)),
            pl.BlockSpec((1, width, width), lambda p: (p, 0, 0)),
            pl.BlockSpec((width, 1), lambda p: (0, 0)),
            pl.BlockSpec((1, width), lambda p: (0, 0)),
        ),
        scratch_shapes=[
            pltpu.VMEM((4, width, window), bf16),
            pltpu.VMEM((window, width), bf16),
            pltpu.SemaphoreType.DMA((2, slots)),
        ],
        compiler_params=pltpu.CompilerParams(vmem_limit_bytes=VMEM_LIMIT),
        name="own_cycle",
    )(tiles, count, virt, wall, far, side, twin, amp4, amp4)


class Mover:
    def __init__(self, plan, in_sem, out_sem):
        self.out_sem = out_sem
        self.outs = []
        self.loads = {}
        for at, (name, (src, dst)) in enumerate(plan.items()):
            self.loads[name] = pltpu.make_async_copy(src, dst, in_sem.at[at])
            self.loads[name].start()

    def need(self, *names):
        for name in names:
            if name in self.loads:
                self.loads.pop(name).wait()

    def put(self, src, dst):
        copy = pltpu.make_async_copy(src, dst, self.out_sem.at[len(self.outs)])
        copy.start()
        self.outs.append(copy)

    def drain(self):
        for copy in self.outs:
            copy.wait()


def emit(mover, last, pair, j, rows, raw, occ_ref, vcol_ref, vrow_ref, part, amps, upd, res_hbm, upd_hbm):
    raw = raw + part[j, rows, :]
    part[j, rows, :] = raw
    mover.put(part.at[j, rows, :], res_hbm.at[pair, rows, :])
    if last:
        gap = (occ_ref[0, pair // 2] + occ_ref[1, pair % 2]) - vcol_ref[rows, :] - vrow_ref[...]
        inverse = pl.reciprocal(gap, approx=True)
        inverse = inverse * (2.0 - gap * inverse)
        own = amps[j, rows, :].astype(jnp.float32)
        upd[j, rows, :] = (own + raw * inverse).astype(upd.dtype)
        mover.put(upd.at[j, rows, :], upd_hbm.at[pair, rows, :])


def emit_behind(products, emit_one):
    waiting = None
    for j, rows, product in products:
        raw = product()
        if waiting is not None:
            emit_one(*waiting)
        waiting = (j, rows, raw)
    emit_one(*waiting)


def row_kernel(
    i, occ_ref, vcol_ref, vrow_ref, b0_hbm, b1_hbm, xt_hbm, x_hbm, coret_hbm, wt_hbm, wd_hbm,
    amps_hbm, part_hbm, res_hbm, upd_hbm, xt, coret, wt, right, left, part, amps, proj, total, upd, sem, osem,
):
    width, points = x_hbm.shape
    early = b0_hbm.shape[1]
    head = pl.ds(0, points)
    blocks = [pl.ds(points + k * width, width) for k in range(2)]
    plan = {
        "b0": (b0_hbm, left.at[:, pl.ds(points, early)]),
        "b1": (b1_hbm, left.at[:, pl.ds(points + early, 2 * width - early)]),
        "xt": (xt_hbm, xt),
        "x0": (x_hbm, right.at[0, :, head]),
        "wt": (wt_hbm.at[pl.ds(2 * i, 2)], wt),
        "coret": (coret_hbm, coret),
    }
    for j in range(2):
        for k in range(2):
            plan["w%d%d" % (j, k)] = (wd_hbm.at[2 * j + k], right.at[j, :, blocks[k]])
        plan["part%d" % j] = (part_hbm.at[2 * i + j], part.at[j])
        plan["amps%d" % j] = (amps_hbm.at[2 * i + j], amps.at[j])
        if j == 0:
            plan["x1"] = (x_hbm, right.at[1, :, head])
    mover = Mover(plan, sem, osem)
    for j in range(2):
        mover.need("b0", "b1", "xt")
        proj[...] = dot(xt[...], left[:, blocks[j]]).astype(proj.dtype)
        mover.need("x0", "coret", "wt")
        inner = dot(proj[...], right[0, :, head])
        total[j] = (
            wt[j].astype(jnp.float32) + coret[...].astype(jnp.float32) * inner
        ).astype(total.dtype)
    def products():
        for j in range(2):
            for at, rows in enumerate(strips(width, STRIP)):

                def product(j=j, at=at, rows=rows):
                    if at == 0:
                        left[:, head] = dot(right[0, :, head], total[j]).astype(left.dtype)
                        mover.need("x%d" % j, "w%d0" % j, "w%d1" % j, "part%d" % j, "amps%d" % j)
                    return dot_nt(left[rows, :], right[j])

                yield j, rows, product

    def emit_one(j, rows, raw):
        emit(
            mover, True, 2 * i + j, j, rows, raw, occ_ref, vcol_ref, vrow_ref,
            part, amps, upd, res_hbm, upd_hbm,
        )

    emit_behind(products(), emit_one)
    mover.drain()


def row(i, occ, vcol, vrow, b0, b1, xt, x, coret, wt, wd, amp4, part):
    width, points = x.shape
    vmem = pl.BlockSpec(memory_space=pltpu.VMEM)
    smem = pl.BlockSpec(memory_space=pltpu.SMEM)
    hbm = pl.BlockSpec(memory_space=pl.ANY)
    f32, bf16 = jnp.float32, jnp.bfloat16
    depth = points + 2 * width
    return pl.pallas_call(
        functools.partial(row_kernel, i),
        out_shape=[jax.ShapeDtypeStruct(part.shape, f32), jax.ShapeDtypeStruct(part.shape, bf16)],
        in_specs=[smem, vmem, vmem] + [hbm] * 9,
        out_specs=[hbm] * 2,
        scratch_shapes=[
            pltpu.VMEM((points, width), bf16),
            pltpu.VMEM((points, points), bf16),
            pltpu.VMEM((2, points, points), bf16),
            pltpu.VMEM((2, width, depth), bf16),
            pltpu.VMEM((width, depth), bf16),
            pltpu.VMEM((2, width, width), f32),
            pltpu.VMEM((2, width, width), bf16),
            pltpu.VMEM((points, width), bf16),
            pltpu.VMEM((2, points, points), bf16),
            pltpu.VMEM((2, width, width), bf16),
            pltpu.SemaphoreType.DMA((15,)),
            pltpu.SemaphoreType.DMA((4 * (width // STRIP),)),
        ],
        input_output_aliases={11: 0},
        compiler_params=pltpu.CompilerParams(vmem_limit_bytes=VMEM_LIMIT),
        name="row_%d" % i,
    )(occ, vcol, vrow, b0, b1, xt, x, coret, wt, wd, amp4, part)


def piece_kernel(i, k, low, high, end, occ_ref, vcol_ref, vrow_ref, *refs):
    last = k == 1 and end
    scratch = 13
    refs, (xt, coret, wt, right, left, part, amps, acc, proj, total, upd, sem, osem) = (
        refs[:-scratch], refs[-scratch:]
    )
    (b_hbm, xt_hbm, x_hbm, coret_hbm, wt_hbm, wd_hbm, amps_hbm, part_hbm) = refs[:8]
    refs = list(refs[8:])
    acc_in = refs.pop(0) if low > 0 else None
    upd_hbm = refs.pop() if last else None
    acc_out = None if end else refs.pop()
    res_hbm = refs.pop()
    width, points = x_hbm.shape
    head, rest = pl.ds(0, points), pl.ds(points, high - low)
    cut = pl.ds(low, high - low)
    plan = {
        "b": (b_hbm, left.at[:, rest]),
        "xt": (xt_hbm, xt),
        "x": (x_hbm, right.at[k, :, head]),
    }
    if low > 0:
        plan["acc"] = (acc_in, acc)
    if end:
        plan["wt"] = (wt_hbm.at[2 * i + k], wt)
        plan["coret"] = (coret_hbm, coret)
    for j in (1 - k, k):
        plan["w%d" % j] = (wd_hbm.at[2 * j + k, :, cut], right.at[j, :, rest])
        plan["part%d" % j] = (part_hbm.at[2 * i + j], part.at[j])
        if last:
            plan["amps%d" % j] = (amps_hbm.at[2 * i + j], amps.at[j])
    mover = Mover(plan, sem, osem)

    def products(plan):
        for j, columns in plan:
            for rows in strips(width, STRIP):

                def product(j=j, columns=columns, rows=rows):
                    mover.need("w%d" % j, "part%d" % j, "amps%d" % j)
                    return dot_nt(left[rows, columns], right[j, :, columns])

                yield j, rows, product

    def emit_one(j, rows, raw):
        emit(
            mover, last, 2 * i + j, j, rows, raw, occ_ref, vcol_ref, vrow_ref,
            part, amps, upd, res_hbm, upd_hbm,
        )

    mover.need("b", "xt")
    proj[...] = dot(xt[...], left[:, rest]).astype(proj.dtype)
    mover.need("x")
    inner = dot(proj[...], right[k, cut, head])
    if low > 0:
        mover.need("acc")
        inner = inner + acc[...]
    if end:
        mover.need("wt", "coret")
        total[...] = (
            wt[...].astype(jnp.float32) + coret[...].astype(jnp.float32) * inner
        ).astype(total.dtype)
        left[:, head] = dot(right[k, :, head], total[...]).astype(left.dtype)
        emit_behind(products([(1 - k, rest), (k, pl.ds(0, points + high - low))]), emit_one)
    else:
        acc[...] = inner
        mover.put(acc, acc_out)
        emit_behind(products([(1 - k, rest), (k, rest)]), emit_one)
    mover.drain()


def piece(i, k, low, high, occ, vcol, vrow, b, xt, x, coret, wt, wd, amp4, part, acc, updated):
    width, points = x.shape
    end = high == width
    last = k == 1 and end
    vmem = pl.BlockSpec(memory_space=pltpu.VMEM)
    smem = pl.BlockSpec(memory_space=pltpu.SMEM)
    hbm = pl.BlockSpec(memory_space=pl.ANY)
    f32, bf16 = jnp.float32, jnp.bfloat16
    operands = [occ, vcol, vrow, b, xt, x, coret, wt, wd, amp4, part]
    out_shape = [jax.ShapeDtypeStruct(part.shape, f32)]
    alias = {len(operands) - 1: 0}
    if low > 0:
        operands.append(acc)
    if not end:
        out_shape.append(jax.ShapeDtypeStruct((points, points), f32))
    if last:
        out_shape.append(jax.ShapeDtypeStruct(part.shape, bf16))
        alias[len(operands)] = 1
        operands.append(updated)
    return pl.pallas_call(
        functools.partial(piece_kernel, i, k, low, high, end),
        out_shape=out_shape,
        in_specs=[smem, vmem, vmem] + [hbm] * (len(operands) - 3),
        out_specs=[hbm] * len(out_shape),
        scratch_shapes=[
            pltpu.VMEM((points, width), bf16),
            pltpu.VMEM((points, points), bf16),
            pltpu.VMEM((points, points), bf16),
            pltpu.VMEM((2, width, points + high - low), bf16),
            pltpu.VMEM((width, points + high - low), bf16),
            pltpu.VMEM((2, width, width), f32),
            pltpu.VMEM((2, width, width), bf16),
            pltpu.VMEM((points, points), f32),
            pltpu.VMEM((points, high - low), bf16),
            pltpu.VMEM((points, points), bf16),
            pltpu.VMEM((2, width, width), bf16),
            pltpu.SemaphoreType.DMA((12,)),
            pltpu.SemaphoreType.DMA((9,)),
        ],
        input_output_aliases=alias,
        compiler_params=pltpu.CompilerParams(vmem_limit_bytes=VMEM_LIMIT),
        name="piece_%d%d_%d" % (i, k, low),
    )(*operands)


def per_device(
    amps, x_factor, core, cycle_w, domain_tiles, domain_count, tile_slot, occ_energy, virt_energy
):
    occ = amps.shape[2]
    width = amps.shape[4]
    tile_width = x_factor.shape[1]
    grid_points = x_factor.shape[2]
    window = cycle_w.shape[4]
    cols = lax.axis_size("col")
    amp4 = amps[0, 0].reshape(occ * occ, width, width)
    shard = cycle_w[0].reshape(occ * occ, tile_width, window)

    early, split = width // 2, 512
    tiles, count = domain_tiles[0, 0], domain_count
    xall, wall, far, first, coret, amp4, *turned = gather_parts(
        count, x_factor, shard, amp4, core, early, split
    )
    xall = xall.reshape(-1, tile_width, grid_points)
    mirror = [(i, (i + cols // 2) % cols) for i in range(cols)]
    second, third, fourth = [lax.ppermute(part, "col", mirror) for part in turned[:3]]
    side = lax.ppermute(far, "col", [(i, i ^ 2) for i in range(cols)])

    x, xt, wt = own_ladder(tiles, count, tile_slot, xall, amp4, core)
    side, tail, wt = lax.optimization_barrier((side, turned[3], wt))
    fifth = lax.ppermute(tail, "col", mirror)
    twin = lax.ppermute(side, "col", [(i, i ^ 1) for i in range(cols)])
    wd, part, vcol, vrow = own_cycle(tiles, count, virt_energy[None, :], wall, far, side, twin, amp4)
    energies = (occ_energy[0, 0], vcol, vrow)
    part, updated = row(0, *energies, first, second, xt, x, coret, wt, wd, amp4, part)
    fixed = (xt, x, coret, wt, wd, amp4)
    part, = piece(1, 0, 0, width, *energies, third, *fixed, part, None, None)
    part, acc = piece(1, 1, 0, split, *energies, fourth, *fixed, part, None, None)
    part, updated = piece(1, 1, split, width, *energies, fifth, *fixed, part, acc, updated)
    return part.reshape(amps.shape), updated.reshape(amps.shape)


def solution(mesh):
    in_specs = (
        P("row", "col", None, None, None, None),
        P("row", None, None),
        P(),
        P("row", None, None, "col", None),
        P("row", "col", None),
        P("row", "col"),
        P(),
        P("row", "col", None, None),
        P(),
    )
    out_specs = (P("row", "col", None, None, None, None), P("row", "col", None, None, None, None))
    return jax.shard_map(
        per_device, mesh=mesh, in_specs=in_specs, out_specs=out_specs, check_vma=False
    )
```

```python
import functools

import jax
import jax.numpy as jnp
from jax import lax
from jax.experimental import pallas as pl
from jax.experimental.pallas import tpu as pltpu
from jax.sharding import PartitionSpec as P

MESH = pl.DeviceIdType.MESH
VMEM_LIMIT = 65300 * 1024
STRIP = 384


def dot(a, b):
    return jnp.dot(a, b, preferred_element_type=jnp.float32)


def dot_nt(a, b):
    return lax.dot_general(a, b, (((1,), (1,)), ((), ())), preferred_element_type=jnp.float32)


def strips(width, step):
    return [pl.ds(start, step) for start in range(0, width, step)]


def remote(src, dst, sems, index, device):
    return pltpu.make_async_remote_copy(
        src_ref=src, dst_ref=dst, send_sem=sems[0].at[index], recv_sem=sems[1].at[index],
        device_id=device, device_id_type=MESH,
    )


def greet(devices):
    barrier = pltpu.get_barrier_semaphore()
    for device in devices:
        pl.semaphore_signal(barrier, inc=1, device_id=device, device_id_type=MESH)
    pl.semaphore_wait(barrier, len(devices))


def gather_kernel(
    x_ref, w_ref, amps_ref, core_ref, xall_ref, wall_ref, far_ref, first_ref, coret_ref, *refs
):
    cuts, (plain, turned, fixed, wsend, wrecv, xsend, xrecv, msend, mrecv, local, tsem) = refs[:-11], refs[-11:]
    r = lax.axis_index("row")
    c = lax.axis_index("col")
    rows = lax.axis_size("row")
    cols = lax.axis_size("col")
    forth = (r, (c + 4) % cols)
    back = (r, (c + cols - 4) % cols)
    mirror = (r, (c + cols // 2) % cols)
    zside = (r, c + 2 - 4 * ((c // 2) % 2))
    twin = (r, c + 1 - 2 * (c % 2))
    beside = r + 1 - 2 * (r % 2)
    core = c % 2
    half = w_ref.shape[0] // 2
    width = plain.shape[1]
    y_steps = range(1, rows // 2)

    amps_in = [pltpu.make_async_copy(amps_ref.at[q], plain.at[q], tsem.at[q]) for q in range(4)]
    core_in = pltpu.make_async_copy(core_ref, fixed.at[0], tsem.at[4])
    for copy in amps_in + [core_in]:
        copy.start()
    greet(
        [forth, back, mirror, zside, twin, (beside, c)]
        + [((r + 2 * step) % rows, c) for step in y_steps]
    )
    wsems, xsems = (wsend, wrecv), (xsend, xrecv)
    started = []

    def send(*args):
        copy = remote(*args)
        copy.start()
        started.append(copy)

    def arrived(part, sems, index):
        remote(part, part, sems, index, twin).wait_recv()

    def shard(offset, plane, side):
        if offset in (1, 2) and plane + side == 0:
            return far_ref.at[offset - 1]
        x = (c // 4 + offset) % (cols // 4)
        z = (c // 2) % 2
        z = z + plane * (1 - 2 * z)
        k = core + side * (1 - 2 * core)
        return wall_ref.at[x * 4 + z * 2 + k]

    def to_twin(offset):
        x = (c // 4 + offset) % (cols // 4)
        send(shard(offset, 0, 0), wall_ref.at[x * 4 + c % 4], wsems, 6 + offset, twin)

    def transpose(q, p):
        amps_in[q].wait()
        for cut in strips(width, 256):
            turned[p, :, cut] = plain[q, cut, :].T

    own = wall_ref.at[c]
    send(w_ref, own, wsems, 0, forth)
    send(w_ref, far_ref.at[0], wsems, 1, back)
    send(x_ref.at[core], xall_ref.at[r, core], xsems, 0, (beside, c))
    send(w_ref, own, wsems, 4, zside)
    for step in y_steps:
        send(x_ref.at[core], xall_ref.at[r, core], xsems, step, ((r + 2 * step) % rows, c))
    send(w_ref, own, wsems, 6, twin)
    own_w = pltpu.make_async_copy(w_ref, own, local.at[0])
    own_x = pltpu.make_async_copy(x_ref, xall_ref.at[r], local.at[1])
    own_w.start()
    own_x.start()
    transpose(0, 0)

    part = xall_ref.at[beside, core]
    arrived(part, xsems, 0)
    for step in y_steps:
        send(part, part, xsems, 3 + step, ((r + 2 * step) % rows, c))
    send(part, part, xsems, 7, twin)

    part = shard(3, 0, 0)
    arrived(part, wsems, 0)
    send(part.at[:half], far_ref.at[1, :half], wsems, 2, forth)
    send(part, part, wsems, 5, zside)
    arrived(far_ref.at[0], wsems, 1)
    send(far_ref.at[0, half:], far_ref.at[1, half:], wsems, 3, back)
    send(turned.at[0, :, pl.ds(0, first_ref.shape[1])], first_ref, (msend, mrecv), 0, mirror)
    to_twin(3)
    to_twin(1)
    transpose(2, 1)
    for step in y_steps:
        origin = (r + rows - 2 * step) % rows
        arrived(xall_ref.at[origin, core], xsems, step)
        send(xall_ref.at[origin, core], xall_ref.at[origin, core], xsems, 7 + step, twin)
    transpose(1, 2)
    part = shard(0, 1, 0)
    arrived(part, wsems, 4)
    send(part, part, wsems, 10, twin)
    for step in y_steps:
        origin = (r + rows - 2 * step) % rows
        origin = origin + 1 - 2 * (origin % 2)
        arrived(xall_ref.at[origin, core], xsems, 3 + step)
        send(xall_ref.at[origin, core], xall_ref.at[origin, core], xsems, 10 + step, twin)
    arrived(far_ref.at[1, :half], wsems, 2)
    arrived(far_ref.at[1, half:], wsems, 3)
    to_twin(2)
    transpose(3, 3)
    early, split = first_ref.shape[1], cuts[2].shape[1]
    moves = (
        (0, pl.ds(early, width - early), 0, pl.ds(0, width - early)),
        (1, pl.ds(0, width), 0, pl.ds(width - early, width)),
        (2, pl.ds(0, width), 1, pl.ds(0, width)),
        (3, pl.ds(0, split), 2, pl.ds(0, split)),
        (3, pl.ds(split, width - split), 3, pl.ds(0, width - split)),
    )
    outs = [
        pltpu.make_async_copy(turned.at[p, :, source], cuts[q].at[:, target], local.at[3 + at])
        for at, (p, source, q, target) in enumerate(moves)
    ]
    core_in.wait()
    for cut in strips(width, 256):
        fixed[1, :, cut] = fixed[0, cut, :].T
    outs.append(pltpu.make_async_copy(fixed.at[1], coret_ref, local.at[2]))
    for copy in outs:
        copy.start()
    part = shard(3, 1, 0)
    arrived(part, wsems, 5)
    send(part, part, wsems, 11, twin)

    for offset in range(4):
        arrived(shard(offset, 0, 1), wsems, 6 + offset)
    arrived(shard(0, 1, 1), wsems, 10)
    arrived(shard(3, 1, 1), wsems, 11)
    arrived(xall_ref.at[beside, 1 - core], xsems, 7)
    for step in y_steps:
        origin = (r + rows - 2 * step) % rows
        arrived(xall_ref.at[origin, 1 - core], xsems, 7 + step)
        origin = origin + 1 - 2 * (origin % 2)
        arrived(xall_ref.at[origin, 1 - core], xsems, 10 + step)
    remote(first_ref, first_ref, (msend, mrecv), 0, mirror).wait_recv()
    for copy in started:
        copy.wait_send()
    for copy in outs + [own_w, own_x]:
        copy.wait()


def gather_parts(x_factor, shard, amp4, core, early, split):
    rows = lax.axis_size("row")
    cols = lax.axis_size("col")
    width = amp4.shape[1]
    hbm = pl.BlockSpec(memory_space=pl.ANY)
    bf16 = jnp.bfloat16
    dma = pltpu.SemaphoreType.DMA
    shapes = [(rows,) + x_factor.shape, (cols,) + shard.shape, (2,) + shard.shape, (width, early), core.shape]
    shapes += [(width, 2 * width - early), (width, width)]
    shapes += [(width, split), (width, width - split)]
    return pl.pallas_call(
        gather_kernel,
        out_shape=[jax.ShapeDtypeStruct(shape, bf16) for shape in shapes],
        in_specs=[hbm] * 4,
        out_specs=[hbm] * len(shapes),
        scratch_shapes=[
            pltpu.VMEM(amp4.shape, bf16),
            pltpu.VMEM(amp4.shape, bf16),
            pltpu.VMEM((2,) + core.shape, bf16),
            dma((12,)),
            dma((12,)),
            dma((14,)),
            dma((14,)),
            dma((1,)),
            dma((1,)),
            dma((8,)),
            dma((5,)),
        ],
        compiler_params=pltpu.CompilerParams(
            collective_id=0, has_side_effects=True, vmem_limit_bytes=VMEM_LIMIT
        ),
        name="gather_parts",
    )(x_factor, shard, amp4, core)


def own_ladder_kernel(
    tiles_ref, count_ref, slot_ref, xall_ref, amps_ref, core_ref, x_ref, xt_ref, wt_ref, gathered, proj, sem
):
    @pl.when(pl.program_id(0) == 0)
    def _():
        tile = xall_ref.shape[1]
        copies = []
        for s in range(tiles_ref.shape[0]):
            copy = pltpu.make_async_copy(
                xall_ref.at[slot_ref[tiles_ref[s]]], gathered.at[pl.ds(s * tile, tile), :], sem.at[s]
            )
            copy.start()
            copies.append(copy)
        for copy in copies:
            copy.wait()
        live = lax.broadcasted_iota(jnp.int32, (x_ref.shape[0], 1), 0) < count_ref[0, 0] * tile
        x_ref[...] = jnp.where(live, gathered[...].astype(jnp.float32), 0.0).astype(x_ref.dtype)
        for cut in strips(x_ref.shape[0], 256):
            xt_ref[:, cut] = x_ref[cut, :].T

    proj[...] = dot(xt_ref[...], amps_ref[0]).astype(proj.dtype)
    inner = dot(proj[...], x_ref[...])
    wt_ref[0] = (core_ref[...].astype(jnp.float32) * inner).astype(wt_ref.dtype)


def own_ladder(tiles, count, tile_slot, xall, amp4, core):
    width = amp4.shape[1]
    points = core.shape[0]
    smem = pl.BlockSpec(memory_space=pltpu.SMEM)
    bf16 = jnp.bfloat16

    def whole(shape):
        return pl.BlockSpec(shape, lambda p: (0, 0))

    return pl.pallas_call(
        own_ladder_kernel,
        out_shape=(
            jax.ShapeDtypeStruct((width, points), bf16),
            jax.ShapeDtypeStruct((points, width), bf16),
            jax.ShapeDtypeStruct((4, points, points), bf16),
        ),
        grid=(4,),
        in_specs=[
            smem, smem, smem, pl.BlockSpec(memory_space=pl.ANY),
            pl.BlockSpec((1, width, width), lambda p: (p, 0, 0)), whole((points, points)),
        ],
        out_specs=(
            whole((width, points)), whole((points, width)),
            pl.BlockSpec((1, points, points), lambda p: (p, 0, 0)),
        ),
        scratch_shapes=[
            pltpu.VMEM((width, points), bf16),
            pltpu.VMEM((points, width), bf16),
            pltpu.SemaphoreType.DMA((tiles.shape[0],)),
        ],
        compiler_params=pltpu.CompilerParams(vmem_limit_bytes=VMEM_LIMIT),
        name="own_ladder",
    )(tiles, count, tile_slot, xall, amp4, core)


def window_index(tiles_ref, count_ref, tile, shape, axis):
    at = lax.broadcasted_iota(jnp.int32, shape, axis)
    index = jnp.full(shape, -1, jnp.int32)
    for s in range(tiles_ref.shape[0]):
        inside = (at >= s * tile) & (at < (s + 1) * tile) & (s < count_ref[0, 0])
        index = jnp.where(inside, at + (tiles_ref[s] - s) * tile, index)
    return index


def own_cycle_kernel(
    tiles_ref, count_ref, virt_ref, wall_ref, far_ref, side_ref, twin_ref, a0_ref, a1_ref,
    wd_ref, cyc_ref, vcol_ref, vrow_ref, wsel, pick, sem,
):
    p = pl.program_id(0)
    tile = wall_ref.shape[2]
    slots = tiles_ref.shape[0]
    width = wd_ref.shape[1]
    window = virt_ref.shape[1]

    @pl.when(p == 0)
    def _():
        me = lax.axis_index("col")
        for first in range(2):
            for s in range(slots):
                number = tiles_ref[s]
                offset = ((number >> 2) + 4 - (me >> 2)) & 3
                plane = ((number >> 1) + (me >> 1)) & 1
                side = (number + me) & 1
                apart = (offset == 1) | (offset == 2)
                dst = wsel.at[pl.ds(2 * first, 2), pl.ds(s * tile, tile), :]

                def fetch(source, at, dst=dst, done=sem.at[first, s], first=first):
                    pltpu.make_async_copy(source.at[at, pl.ds(2 * first, 2)], dst, done).start()

                @pl.when(jnp.logical_not(apart) | ((plane == 0) & (side == 1)))
                def _(number=number, fetch=fetch):
                    fetch(wall_ref, number)

                for source, at_plane, at_side in ((far_ref, 0, 0), (side_ref, 1, 0), (twin_ref, 1, 1)):

                    @pl.when(apart & (plane == at_plane) & (side == at_side))
                    def _(source=source, offset=offset, fetch=fetch):
                        fetch(source, offset - 1)

        along = lax.broadcasted_iota(jnp.int32, pick.shape, 0)
        picked = window_index(tiles_ref, count_ref, tile, (1, width), 1)
        pick[...] = jnp.where(along == picked, 1.0, 0.0).astype(pick.dtype)
        picked = window_index(tiles_ref, count_ref, tile, (width, 1), 0)
        along = lax.broadcasted_iota(jnp.int32, (width, window), 1)
        levels = jnp.sum(jnp.where(along == picked, virt_ref[...], 0.0), axis=1, keepdims=True)
        vcol_ref[...] = levels
        vrow_ref[...] = jnp.broadcast_to(levels, (width, 128)).T[:1, :]

    for first in range(2):

        @pl.when(p == 2 * first)
        def _(first=first):
            for s in range(slots):
                pltpu.make_async_copy(
                    wall_ref.at[0, pl.ds(0, 2)],
                    wsel.at[pl.ds(2 * first, 2), pl.ds(s * tile, tile), :],
                    sem.at[first, s],
                ).wait()
            for k in range(2):
                wd_ref[k] = dot(wsel[2 * first + k], pick[...]).astype(wd_ref.dtype)

    cyc_ref[0] = (dot(wd_ref[0], a0_ref[0]) + dot(wd_ref[1], a1_ref[0])).astype(cyc_ref.dtype)


def own_cycle(tiles, count, virt, wall, far, side, twin, amp4):
    width = amp4.shape[1]
    slots, window = tiles.shape[0], wall.shape[3]
    smem = pl.BlockSpec(memory_space=pltpu.SMEM)
    hbm = pl.BlockSpec(memory_space=pl.ANY)
    f32, bf16 = jnp.float32, jnp.bfloat16
    return pl.pallas_call(
        own_cycle_kernel,
        out_shape=(
            jax.ShapeDtypeStruct((4, width, width), bf16),
            jax.ShapeDtypeStruct((4, width, width), bf16),
            jax.ShapeDtypeStruct((width, 1), f32),
            jax.ShapeDtypeStruct((1, width), f32),
        ),
        grid=(4,),
        in_specs=[
            smem,
            smem,
            pl.BlockSpec((1, window), lambda p: (0, 0)),
            hbm,
            hbm,
            hbm,
            hbm,
            pl.BlockSpec((1, width, width), lambda p: (p % 2, 0, 0)),
            pl.BlockSpec((1, width, width), lambda p: (2 + p % 2, 0, 0)),
        ],
        out_specs=(
            pl.BlockSpec((2, width, width), lambda p: (p // 2, 0, 0)),
            pl.BlockSpec((1, width, width), lambda p: (p, 0, 0)),
            pl.BlockSpec((width, 1), lambda p: (0, 0)),
            pl.BlockSpec((1, width), lambda p: (0, 0)),
        ),
        scratch_shapes=[
            pltpu.VMEM((4, width, window), bf16),
            pltpu.VMEM((window, width), bf16),
            pltpu.SemaphoreType.DMA((2, slots)),
        ],
        compiler_params=pltpu.CompilerParams(vmem_limit_bytes=VMEM_LIMIT),
        name="own_cycle",
    )(tiles, count, virt, wall, far, side, twin, amp4, amp4)


class Mover:
    def __init__(self, plan, in_sem, out_sem):
        self.out_sem = out_sem
        self.outs = []
        self.loads = {}
        for at, (name, (src, dst)) in enumerate(plan.items()):
            self.loads[name] = pltpu.make_async_copy(src, dst, in_sem.at[at])
            self.loads[name].start()

    def need(self, *names):
        for name in names:
            if name in self.loads:
                self.loads.pop(name).wait()

    def put(self, src, dst):
        copy = pltpu.make_async_copy(src, dst, self.out_sem.at[len(self.outs)])
        copy.start()
        self.outs.append(copy)

    def drain(self):
        for copy in self.outs:
            copy.wait()


def emit(mover, pair, j, rows, raw, count_ref, occ_ref, vcol_ref, vrow_ref, part, amps, res, upd, res_hbm, upd_hbm):
    height, width = raw.shape
    count = count_ref[0, 0] * 64
    live = (lax.broadcasted_iota(jnp.int32, (height, 1), 0) + rows.start < count) & (
        lax.broadcasted_iota(jnp.int32, (1, width), 1) < count
    )
    raw = jnp.where(live, raw + part[j, rows, :].astype(jnp.float32), 0.0)
    own = jnp.where(live, amps[j, rows, :].astype(jnp.float32), 0.0)
    gap = (occ_ref[0, pair // 2] + occ_ref[1, pair % 2]) - vcol_ref[rows, :] - vrow_ref[...]
    inverse = pl.reciprocal(gap, approx=True)
    inverse = inverse * (2.0 - gap * inverse)
    res[j, rows, :] = raw
    mover.put(res.at[j, rows, :], res_hbm.at[pair, rows, :])
    upd[j, rows, :] = (own + raw * inverse).astype(upd.dtype)
    mover.put(upd.at[j, rows, :], upd_hbm.at[pair, rows, :])


def emit_behind(products, emit_one):
    waiting = None
    for j, rows, product in products:
        raw = product()
        if waiting is not None:
            emit_one(*waiting)
        waiting = (j, rows, raw)
    emit_one(*waiting)


def row_kernel(
    i, count_ref, occ_ref, vcol_ref, vrow_ref, b0_hbm, b1_hbm, xt_hbm, x_hbm, coret_hbm, wt_hbm, wd_hbm,
    amps_hbm, part_hbm, res_hbm, upd_hbm, xt, coret, wt, right, left, part, amps, proj, total, res, upd, sem, osem,
):
    width, points = x_hbm.shape
    early = b0_hbm.shape[1]
    head = pl.ds(0, points)
    blocks = [pl.ds(points + k * width, width) for k in range(2)]
    plan = {
        "b0": (b0_hbm, left.at[:, pl.ds(points, early)]),
        "b1": (b1_hbm, left.at[:, pl.ds(points + early, 2 * width - early)]),
        "xt": (xt_hbm, xt),
        "x0": (x_hbm, right.at[0, :, head]),
        "wt": (wt_hbm.at[pl.ds(2 * i, 2)], wt),
        "coret": (coret_hbm, coret),
    }
    for j in range(2):
        for k in range(2):
            plan["w%d%d" % (j, k)] = (wd_hbm.at[2 * j + k], right.at[j, :, blocks[k]])
        plan["part%d" % j] = (part_hbm.at[2 * i + j], part.at[j])
        plan["amps%d" % j] = (amps_hbm.at[2 * i + j], amps.at[j])
        if j == 0:
            plan["x1"] = (x_hbm, right.at[1, :, head])
    mover = Mover(plan, sem, osem)
    for j in range(2):
        mover.need("b0", "b1", "xt")
        proj[...] = dot(xt[...], left[:, blocks[j]]).astype(proj.dtype)
        mover.need("x0", "coret", "wt")
        inner = dot(proj[...], right[0, :, head])
        total[j] = (
            wt[j].astype(jnp.float32) + coret[...].astype(jnp.float32) * inner
        ).astype(total.dtype)
    def products():
        for j in range(2):
            for at, rows in enumerate(strips(width, STRIP)):

                def product(j=j, at=at, rows=rows):
                    if at == 0:
                        left[:, head] = dot(right[0, :, head], total[j]).astype(left.dtype)
                        mover.need("x%d" % j, "w%d0" % j, "w%d1" % j, "part%d" % j, "amps%d" % j)
                    return dot_nt(left[rows, :], right[j])

                yield j, rows, product

    def emit_one(j, rows, raw):
        emit(
            mover, 2 * i + j, j, rows, raw, count_ref, occ_ref, vcol_ref, vrow_ref,
            part, amps, res, upd, res_hbm, upd_hbm,
        )

    emit_behind(products(), emit_one)
    mover.drain()


def row(i, count, occ, vcol, vrow, b0, b1, xt, x, coret, wt, wd, amp4, part):
    width, points = x.shape
    vmem = pl.BlockSpec(memory_space=pltpu.VMEM)
    smem = pl.BlockSpec(memory_space=pltpu.SMEM)
    hbm = pl.BlockSpec(memory_space=pl.ANY)
    f32, bf16 = jnp.float32, jnp.bfloat16
    depth = points + 2 * width
    return pl.pallas_call(
        functools.partial(row_kernel, i),
        out_shape=[jax.ShapeDtypeStruct(part.shape, f32), jax.ShapeDtypeStruct(part.shape, bf16)],
        in_specs=[smem, smem, vmem, vmem] + [hbm] * 9,
        out_specs=[hbm] * 2,
        scratch_shapes=[
            pltpu.VMEM((points, width), bf16),
            pltpu.VMEM((points, points), bf16),
            pltpu.VMEM((2, points, points), bf16),
            pltpu.VMEM((2, width, depth), bf16),
            pltpu.VMEM((width, depth), bf16),
            pltpu.VMEM((2, width, width), bf16),
            pltpu.VMEM((2, width, width), bf16),
            pltpu.VMEM((points, width), bf16),
            pltpu.VMEM((2, points, points), bf16),
            pltpu.VMEM((2, width, width), f32),
            pltpu.VMEM((2, width, width), bf16),
            pltpu.SemaphoreType.DMA((15,)),
            pltpu.SemaphoreType.DMA((4 * (width // STRIP),)),
        ],
        compiler_params=pltpu.CompilerParams(vmem_limit_bytes=VMEM_LIMIT),
        name="row_%d" % i,
    )(count, occ, vcol, vrow, b0, b1, xt, x, coret, wt, wd, amp4, part)


def piece_kernel(i, k, low, high, end, count_ref, occ_ref, vcol_ref, vrow_ref, *refs):
    last = k == 1 and end
    scratch = 13
    refs, (xt, coret, before, right, left, part, amps, proj, total, res, upd, sem, osem) = (
        refs[:-scratch], refs[-scratch:]
    )
    (b_hbm, xt_hbm, x_hbm, coret_hbm, before_hbm, wd_hbm, amps_hbm, part_hbm) = refs[:8]
    outs = refs[8:]
    width, points = x_hbm.shape
    head, rest = pl.ds(0, points), pl.ds(points, high - low)
    cut = pl.ds(low, high - low)
    plan = {
        "b": (b_hbm, left.at[:, rest]),
        "xt": (xt_hbm, xt),
        "x": (x_hbm, right.at[k, :, head]) if end else (x_hbm.at[cut], right.at[k, cut, head]),
        "coret": (coret_hbm, coret),
        "before": (before_hbm if low > 0 else before_hbm.at[2 * i + k], before),
    }
    for j in (1 - k, k):
        plan["w%d" % j] = (wd_hbm.at[2 * j + k, :, cut], right.at[j, :, rest])
        plan["part%d" % j] = (part_hbm.at[2 * i + j], part.at[j])
        if last:
            plan["amps%d" % j] = (amps_hbm.at[2 * i + j], amps.at[j])
    mover = Mover(plan, sem, osem)

    def products(plan):
        for j, columns in plan:
            for rows in strips(width, STRIP):

                def product(j=j, columns=columns, rows=rows):
                    mover.need("w%d" % j, "part%d" % j, "amps%d" % j)
                    return dot_nt(left[rows, columns], right[j, :, columns])

                yield j, rows, product

    def emit_one(j, rows, raw):
        if last:
            emit(
                mover, 2 * i + j, j, rows, raw, count_ref, occ_ref, vcol_ref, vrow_ref,
                part, amps, res, upd, outs[-2], outs[-1],
            )
        else:
            part[j, rows, :] = (raw + part[j, rows, :].astype(jnp.float32)).astype(part.dtype)
            mover.put(part.at[j, rows, :], outs[0].at[2 * i + j, rows, :])

    mover.need("b", "xt")
    proj[...] = dot(xt[...], left[:, rest]).astype(proj.dtype)
    mover.need("x")
    inner = dot(proj[...], right[k, cut, head])
    mover.need("coret", "before")
    total[...] = (
        before[...].astype(jnp.float32) + coret[...].astype(jnp.float32) * inner
    ).astype(total.dtype)
    if end:
        left[:, head] = dot(right[k, :, head], total[...]).astype(left.dtype)
        emit_behind(products([(1 - k, rest), (k, pl.ds(0, points + high - low))]), emit_one)
    else:
        mover.put(total, outs[1])
        emit_behind(products([(1 - k, rest), (k, rest)]), emit_one)
    mover.drain()


def piece(i, k, low, high, count, occ, vcol, vrow, b, xt, x, coret, before, wd, amp4, part, residual, updated):
    width, points = x.shape
    end = high == width
    last = k == 1 and end
    vmem = pl.BlockSpec(memory_space=pltpu.VMEM)
    smem = pl.BlockSpec(memory_space=pltpu.SMEM)
    hbm = pl.BlockSpec(memory_space=pl.ANY)
    f32, bf16 = jnp.float32, jnp.bfloat16
    operands = [count, occ, vcol, vrow, b, xt, x, coret, before, wd, amp4, part]
    if last:
        out_shape = [jax.ShapeDtypeStruct(part.shape, f32), jax.ShapeDtypeStruct(part.shape, bf16)]
        alias = {len(operands): 0, len(operands) + 1: 1}
        operands += [residual, updated]
    else:
        out_shape = [jax.ShapeDtypeStruct(part.shape, bf16)]
        alias = {len(operands) - 1: 0}
        if not end:
            out_shape.append(jax.ShapeDtypeStruct((points, points), bf16))
    return pl.pallas_call(
        functools.partial(piece_kernel, i, k, low, high, end),
        out_shape=out_shape,
        in_specs=[smem, smem, vmem, vmem] + [hbm] * (len(operands) - 4),
        out_specs=[hbm] * len(out_shape),
        scratch_shapes=[
            pltpu.VMEM((points, width), bf16),
            pltpu.VMEM((points, points), bf16),
            pltpu.VMEM((points, points), bf16),
            pltpu.VMEM((2, width, points + high - low), bf16),
            pltpu.VMEM((width, points + high - low), bf16),
            pltpu.VMEM((2, width, width), bf16),
            pltpu.VMEM((2, width, width), bf16),
            pltpu.VMEM((points, high - low), bf16),
            pltpu.VMEM((points, points), bf16),
            pltpu.VMEM((2, width, width), f32),
            pltpu.VMEM((2, width, width), bf16),
            pltpu.SemaphoreType.DMA((11,)),
            pltpu.SemaphoreType.DMA((8,)),
        ],
        input_output_aliases=alias,
        compiler_params=pltpu.CompilerParams(vmem_limit_bytes=VMEM_LIMIT),
        name="piece_%d%d_%d" % (i, k, low),
    )(*operands)


def per_device(
    amps, x_factor, core, cycle_w, domain_tiles, domain_count, tile_slot, occ_energy, virt_energy
):
    occ = amps.shape[2]
    width = amps.shape[4]
    tile_width = x_factor.shape[1]
    grid_points = x_factor.shape[2]
    window = cycle_w.shape[4]
    cols = lax.axis_size("col")
    amp4 = amps[0, 0].reshape(occ * occ, width, width)
    shard = cycle_w[0].reshape(occ * occ, tile_width, window)

    early, split = width // 2, 512
    tiles, count = domain_tiles[0, 0], domain_count
    xall, wall, far, first, coret, *turned = gather_parts(x_factor, shard, amp4, core, early, split)
    xall = xall.reshape(-1, tile_width, grid_points)
    mirror = [(i, (i + cols // 2) % cols) for i in range(cols)]
    second, third, fourth = [lax.ppermute(part, "col", mirror) for part in turned[:3]]
    side = lax.ppermute(far, "col", [(i, i ^ 2) for i in range(cols)])

    x, xt, wt = own_ladder(tiles, count, tile_slot, xall, amp4, core)
    side, tail, wt = lax.optimization_barrier((side, turned[3], wt))
    fifth = lax.ppermute(tail, "col", mirror)
    twin = lax.ppermute(side, "col", [(i, i ^ 1) for i in range(cols)])
    wd, part, vcol, vrow = own_cycle(tiles, count, virt_energy[None, :], wall, far, side, twin, amp4)
    energies = (count, occ_energy[0, 0], vcol, vrow)
    residual, updated = row(0, *energies, first, second, xt, x, coret, wt, wd, amp4, part)
    fixed = (xt, x, coret)
    part, = piece(1, 0, 0, width, *energies, third, *fixed, wt, wd, amp4, part, None, None)
    part, total = piece(1, 1, 0, split, *energies, fourth, *fixed, wt, wd, amp4, part, None, None)
    residual, updated = piece(
        1, 1, split, width, *energies, fifth, *fixed, total, wd, amp4, part, residual, updated
    )
    return residual.reshape(amps.shape), updated.reshape(amps.shape)


def solution(mesh):
    in_specs = (
        P("row", "col", None, None, None, None),
        P("row", None, None),
        P(),
        P("row", None, None, "col", None),
        P("row", "col", None),
        P("row", "col"),
        P(),
        P("row", "col", None, None),
        P(),
    )
    out_specs = (P("row", "col", None, None, None, None), P("row", "col", None, None, None, None))
    return jax.shard_map(
        per_device, mesh=mesh, in_specs=in_specs, out_specs=out_specs, check_vma=False
    )
```

```python
import functools

import jax
import jax.numpy as jnp
from jax import lax
from jax.experimental import pallas as pl
from jax.experimental.pallas import tpu as pltpu
from jax.sharding import PartitionSpec as P

MESH = pl.DeviceIdType.MESH
VMEM_LIMIT = 65300 * 1024
STRIP = 384


def dot(a, b):
    return jnp.dot(a, b, preferred_element_type=jnp.float32)


def strips(width, step):
    return [pl.ds(start, step) for start in range(0, width, step)]


def remote(src, dst, sems, index, device):
    return pltpu.make_async_remote_copy(
        src_ref=src, dst_ref=dst, send_sem=sems[0].at[index], recv_sem=sems[1].at[index],
        device_id=device, device_id_type=MESH,
    )


def greet(devices):
    barrier = pltpu.get_barrier_semaphore()
    for device in devices:
        pl.semaphore_signal(barrier, inc=1, device_id=device, device_id_type=MESH)
    pl.semaphore_wait(barrier, len(devices))


def gather_kernel(
    x_ref, w_ref, amps_ref, core_ref, xall_ref, wall_ref, far_ref, first_ref, coret_ref, *refs
):
    cuts, (plain, turned, fixed, wsend, wrecv, xsend, xrecv, msend, mrecv, local, tsem) = refs[:-11], refs[-11:]
    r = lax.axis_index("row")
    c = lax.axis_index("col")
    rows = lax.axis_size("row")
    cols = lax.axis_size("col")
    forth = (r, (c + 4) % cols)
    back = (r, (c + cols - 4) % cols)
    mirror = (r, (c + cols // 2) % cols)
    zside = (r, c + 2 - 4 * ((c // 2) % 2))
    twin = (r, c + 1 - 2 * (c % 2))
    beside = r + 1 - 2 * (r % 2)
    core = c % 2
    half = w_ref.shape[0] // 2
    width = plain.shape[1]
    y_steps = range(1, rows // 2)

    amps_in = [pltpu.make_async_copy(amps_ref.at[q], plain.at[q], tsem.at[q]) for q in range(4)]
    core_in = pltpu.make_async_copy(core_ref, fixed.at[0], tsem.at[4])
    for copy in amps_in + [core_in]:
        copy.start()
    greet(
        [forth, back, mirror, zside, twin, (beside, c)]
        + [((r + 2 * step) % rows, c) for step in y_steps]
    )
    wsems, xsems = (wsend, wrecv), (xsend, xrecv)
    started = []

    def send(*args):
        copy = remote(*args)
        copy.start()
        started.append(copy)

    def arrived(part, sems, index):
        remote(part, part, sems, index, twin).wait_recv()

    def shard(offset, plane, side):
        if offset in (1, 2) and plane + side == 0:
            return far_ref.at[offset - 1]
        x = (c // 4 + offset) % (cols // 4)
        z = (c // 2) % 2
        z = z + plane * (1 - 2 * z)
        k = core + side * (1 - 2 * core)
        return wall_ref.at[x * 4 + z * 2 + k]

    def to_twin(offset):
        x = (c // 4 + offset) % (cols // 4)
        send(shard(offset, 0, 0), wall_ref.at[x * 4 + c % 4], wsems, 6 + offset, twin)

    def transpose(q, p):
        amps_in[q].wait()
        for cut in strips(width, 256):
            turned[p, :, cut] = plain[q, cut, :].T

    own = wall_ref.at[c]
    send(w_ref, own, wsems, 0, forth)
    send(w_ref, far_ref.at[0], wsems, 1, back)
    send(x_ref.at[core], xall_ref.at[r, core], xsems, 0, (beside, c))
    send(w_ref, own, wsems, 4, zside)
    for step in y_steps:
        send(x_ref.at[core], xall_ref.at[r, core], xsems, step, ((r + 2 * step) % rows, c))
    send(w_ref, own, wsems, 6, twin)
    own_w = pltpu.make_async_copy(w_ref, own, local.at[0])
    own_x = pltpu.make_async_copy(x_ref, xall_ref.at[r], local.at[1])
    own_w.start()
    own_x.start()
    transpose(0, 0)

    part = xall_ref.at[beside, core]
    arrived(part, xsems, 0)
    for step in y_steps:
        send(part, part, xsems, 3 + step, ((r + 2 * step) % rows, c))
    send(part, part, xsems, 7, twin)

    part = shard(3, 0, 0)
    arrived(part, wsems, 0)
    send(part.at[:half], far_ref.at[1, :half], wsems, 2, forth)
    send(part, part, wsems, 5, zside)
    arrived(far_ref.at[0], wsems, 1)
    send(far_ref.at[0, half:], far_ref.at[1, half:], wsems, 3, back)
    send(turned.at[0, :, pl.ds(0, first_ref.shape[1])], first_ref, (msend, mrecv), 0, mirror)
    to_twin(3)
    to_twin(1)
    transpose(2, 1)
    for step in y_steps:
        origin = (r + rows - 2 * step) % rows
        arrived(xall_ref.at[origin, core], xsems, step)
        send(xall_ref.at[origin, core], xall_ref.at[origin, core], xsems, 7 + step, twin)
    transpose(1, 2)
    part = shard(0, 1, 0)
    arrived(part, wsems, 4)
    send(part, part, wsems, 10, twin)
    for step in y_steps:
        origin = (r + rows - 2 * step) % rows
        origin = origin + 1 - 2 * (origin % 2)
        arrived(xall_ref.at[origin, core], xsems, 3 + step)
        send(xall_ref.at[origin, core], xall_ref.at[origin, core], xsems, 10 + step, twin)
    arrived(far_ref.at[1, :half], wsems, 2)
    arrived(far_ref.at[1, half:], wsems, 3)
    to_twin(2)
    transpose(3, 3)
    early, split = first_ref.shape[1], cuts[2].shape[1]
    moves = (
        (0, pl.ds(early, width - early), 0, pl.ds(0, width - early)),
        (1, pl.ds(0, width), 0, pl.ds(width - early, width)),
        (2, pl.ds(0, width), 1, pl.ds(0, width)),
        (3, pl.ds(0, split), 2, pl.ds(0, split)),
        (3, pl.ds(split, width - split), 3, pl.ds(0, width - split)),
    )
    outs = [
        pltpu.make_async_copy(turned.at[p, :, source], cuts[q].at[:, target], local.at[3 + at])
        for at, (p, source, q, target) in enumerate(moves)
    ]
    core_in.wait()
    for cut in strips(width, 256):
        fixed[1, :, cut] = fixed[0, cut, :].T
    outs.append(pltpu.make_async_copy(fixed.at[1], coret_ref, local.at[2]))
    for copy in outs:
        copy.start()
    part = shard(3, 1, 0)
    arrived(part, wsems, 5)
    send(part, part, wsems, 11, twin)

    for offset in range(4):
        arrived(shard(offset, 0, 1), wsems, 6 + offset)
    arrived(shard(0, 1, 1), wsems, 10)
    arrived(shard(3, 1, 1), wsems, 11)
    arrived(xall_ref.at[beside, 1 - core], xsems, 7)
    for step in y_steps:
        origin = (r + rows - 2 * step) % rows
        arrived(xall_ref.at[origin, 1 - core], xsems, 7 + step)
        origin = origin + 1 - 2 * (origin % 2)
        arrived(xall_ref.at[origin, 1 - core], xsems, 10 + step)
    remote(first_ref, first_ref, (msend, mrecv), 0, mirror).wait_recv()
    for copy in started:
        copy.wait_send()
    for copy in outs + [own_w, own_x]:
        copy.wait()


def gather_parts(x_factor, shard, amp4, core, early, split):
    rows = lax.axis_size("row")
    cols = lax.axis_size("col")
    width = amp4.shape[1]
    hbm = pl.BlockSpec(memory_space=pl.ANY)
    bf16 = jnp.bfloat16
    dma = pltpu.SemaphoreType.DMA
    shapes = [(rows,) + x_factor.shape, (cols,) + shard.shape, (2,) + shard.shape, (width, early), core.shape]
    shapes += [(width, 2 * width - early), (width, width)]
    shapes += [(width, split), (width, width - split)]
    return pl.pallas_call(
        gather_kernel,
        out_shape=[jax.ShapeDtypeStruct(shape, bf16) for shape in shapes],
        in_specs=[hbm] * 4,
        out_specs=[hbm] * len(shapes),
        scratch_shapes=[
            pltpu.VMEM(amp4.shape, bf16),
            pltpu.VMEM(amp4.shape, bf16),
            pltpu.VMEM((2,) + core.shape, bf16),
            dma((12,)),
            dma((12,)),
            dma((14,)),
            dma((14,)),
            dma((1,)),
            dma((1,)),
            dma((8,)),
            dma((5,)),
        ],
        compiler_params=pltpu.CompilerParams(
            collective_id=0, has_side_effects=True, vmem_limit_bytes=VMEM_LIMIT
        ),
        name="gather_parts",
    )(x_factor, shard, amp4, core)


def own_ladder_kernel(
    tiles_ref, count_ref, slot_ref, xall_ref, amps_ref, core_ref, x_ref, xt_ref, wt_ref, gathered, proj, sem
):
    @pl.when(pl.program_id(0) == 0)
    def _():
        tile = xall_ref.shape[1]
        copies = []
        for s in range(tiles_ref.shape[0]):
            copy = pltpu.make_async_copy(
                xall_ref.at[slot_ref[tiles_ref[s]]], gathered.at[pl.ds(s * tile, tile), :], sem.at[s]
            )
            copy.start()
            copies.append(copy)
        for copy in copies:
            copy.wait()
        live = lax.broadcasted_iota(jnp.int32, (x_ref.shape[0], 1), 0) < count_ref[0, 0] * tile
        x_ref[...] = jnp.where(live, gathered[...].astype(jnp.float32), 0.0).astype(x_ref.dtype)
        for cut in strips(x_ref.shape[0], 256):
            xt_ref[:, cut] = x_ref[cut, :].T

    proj[...] = dot(xt_ref[...], amps_ref[0]).astype(proj.dtype)
    inner = dot(proj[...], x_ref[...])
    wt_ref[0] = (core_ref[...].astype(jnp.float32) * inner).astype(wt_ref.dtype)


def own_ladder(tiles, count, tile_slot, xall, amp4, core):
    width = amp4.shape[1]
    points = core.shape[0]
    smem = pl.BlockSpec(memory_space=pltpu.SMEM)
    bf16 = jnp.bfloat16

    def whole(shape):
        return pl.BlockSpec(shape, lambda p: (0, 0))

    return pl.pallas_call(
        own_ladder_kernel,
        out_shape=(
            jax.ShapeDtypeStruct((width, points), bf16),
            jax.ShapeDtypeStruct((points, width), bf16),
            jax.ShapeDtypeStruct((4, points, points), bf16),
        ),
        grid=(4,),
        in_specs=[
            smem, smem, smem, pl.BlockSpec(memory_space=pl.ANY),
            pl.BlockSpec((1, width, width), lambda p: (p, 0, 0)), whole((points, points)),
        ],
        out_specs=(
            whole((width, points)), whole((points, width)),
            pl.BlockSpec((1, points, points), lambda p: (p, 0, 0)),
        ),
        scratch_shapes=[
            pltpu.VMEM((width, points), bf16),
            pltpu.VMEM((points, width), bf16),
            pltpu.SemaphoreType.DMA((tiles.shape[0],)),
        ],
        compiler_params=pltpu.CompilerParams(vmem_limit_bytes=VMEM_LIMIT),
        name="own_ladder",
    )(tiles, count, tile_slot, xall, amp4, core)


def window_index(tiles_ref, count_ref, tile, shape, axis):
    at = lax.broadcasted_iota(jnp.int32, shape, axis)
    index = jnp.full(shape, -1, jnp.int32)
    for s in range(tiles_ref.shape[0]):
        inside = (at >= s * tile) & (at < (s + 1) * tile) & (s < count_ref[0, 0])
        index = jnp.where(inside, at + (tiles_ref[s] - s) * tile, index)
    return index


def own_cycle_kernel(
    tiles_ref, count_ref, virt_ref, wall_ref, far_ref, side_ref, twin_ref, a0_ref, a1_ref,
    wdt_ref, cyc_ref, vcol_ref, vrow_ref, wsel, wd, pick, sem,
):
    p = pl.program_id(0)
    tile = wall_ref.shape[2]
    slots = tiles_ref.shape[0]
    width = wd.shape[1]
    window = virt_ref.shape[1]

    @pl.when(p == 0)
    def _():
        me = lax.axis_index("col")
        for first in range(2):
            for s in range(slots):
                number = tiles_ref[s]
                offset = ((number >> 2) + 4 - (me >> 2)) & 3
                plane = ((number >> 1) + (me >> 1)) & 1
                side = (number + me) & 1
                apart = (offset == 1) | (offset == 2)
                dst = wsel.at[pl.ds(2 * first, 2), pl.ds(s * tile, tile), :]

                def fetch(source, at, dst=dst, done=sem.at[first, s], first=first):
                    pltpu.make_async_copy(source.at[at, pl.ds(2 * first, 2)], dst, done).start()

                @pl.when(jnp.logical_not(apart) | ((plane == 0) & (side == 1)))
                def _(number=number, fetch=fetch):
                    fetch(wall_ref, number)

                for source, at_plane, at_side in ((far_ref, 0, 0), (side_ref, 1, 0), (twin_ref, 1, 1)):

                    @pl.when(apart & (plane == at_plane) & (side == at_side))
                    def _(source=source, offset=offset, fetch=fetch):
                        fetch(source, offset - 1)

        along = lax.broadcasted_iota(jnp.int32, pick.shape, 0)
        picked = window_index(tiles_ref, count_ref, tile, (1, width), 1)
        pick[...] = jnp.where(along == picked, 1.0, 0.0).astype(pick.dtype)
        picked = window_index(tiles_ref, count_ref, tile, (width, 1), 0)
        along = lax.broadcasted_iota(jnp.int32, (width, window), 1)
        levels = jnp.sum(jnp.where(along == picked, virt_ref[...], 0.0), axis=1, keepdims=True)
        vcol_ref[...] = levels
        vrow_ref[...] = jnp.broadcast_to(levels, (width, 128)).T[:1, :]

    for first in range(2):

        @pl.when(p == 2 * first)
        def _(first=first):
            for s in range(slots):
                pltpu.make_async_copy(
                    wall_ref.at[0, pl.ds(0, 2)],
                    wsel.at[pl.ds(2 * first, 2), pl.ds(s * tile, tile), :],
                    sem.at[first, s],
                ).wait()
            for k in range(2):
                wd[k] = dot(wsel[2 * first + k], pick[...]).astype(wd.dtype)
                for cut in strips(width, 256):
                    wdt_ref[k, :, cut] = wd[k, cut, :].T

    cyc_ref[0] = (dot(wd[0], a0_ref[0]) + dot(wd[1], a1_ref[0])).astype(cyc_ref.dtype)


def own_cycle(tiles, count, virt, wall, far, side, twin, amp4):
    width = amp4.shape[1]
    slots, window = tiles.shape[0], wall.shape[3]
    smem = pl.BlockSpec(memory_space=pltpu.SMEM)
    hbm = pl.BlockSpec(memory_space=pl.ANY)
    f32, bf16 = jnp.float32, jnp.bfloat16
    return pl.pallas_call(
        own_cycle_kernel,
        out_shape=(
            jax.ShapeDtypeStruct((4, width, width), bf16),
            jax.ShapeDtypeStruct((4, width, width), bf16),
            jax.ShapeDtypeStruct((width, 1), f32),
            jax.ShapeDtypeStruct((1, width), f32),
        ),
        grid=(4,),
        in_specs=[
            smem,
            smem,
            pl.BlockSpec((1, window), lambda p: (0, 0)),
            hbm,
            hbm,
            hbm,
            hbm,
            pl.BlockSpec((1, width, width), lambda p: (p % 2, 0, 0)),
            pl.BlockSpec((1, width, width), lambda p: (2 + p % 2, 0, 0)),
        ],
        out_specs=(
            pl.BlockSpec((2, width, width), lambda p: (p // 2, 0, 0)),
            pl.BlockSpec((1, width, width), lambda p: (p, 0, 0)),
            pl.BlockSpec((width, 1), lambda p: (0, 0)),
            pl.BlockSpec((1, width), lambda p: (0, 0)),
        ),
        scratch_shapes=[
            pltpu.VMEM((4, width, window), bf16),
            pltpu.VMEM((2, width, width), bf16),
            pltpu.VMEM((window, width), bf16),
            pltpu.SemaphoreType.DMA((2, slots)),
        ],
        compiler_params=pltpu.CompilerParams(vmem_limit_bytes=VMEM_LIMIT),
        name="own_cycle",
    )(tiles, count, virt, wall, far, side, twin, amp4, amp4)


class Mover:
    def __init__(self, plan, in_sem, out_sem):
        self.out_sem = out_sem
        self.outs = []
        self.loads = {}
        for at, (name, (src, dst)) in enumerate(plan.items()):
            self.loads[name] = pltpu.make_async_copy(src, dst, in_sem.at[at])
            self.loads[name].start()

    def need(self, *names):
        for name in names:
            if name in self.loads:
                self.loads.pop(name).wait()

    def put(self, src, dst):
        copy = pltpu.make_async_copy(src, dst, self.out_sem.at[len(self.outs)])
        copy.start()
        self.outs.append(copy)

    def drain(self):
        for copy in self.outs:
            copy.wait()


def emit(mover, pair, j, rows, raw, count_ref, occ_ref, vcol_ref, vrow_ref, part, amps, res, upd, res_hbm, upd_hbm):
    height, width = raw.shape
    count = count_ref[0, 0] * 64
    live = (lax.broadcasted_iota(jnp.int32, (height, 1), 0) + rows.start < count) & (
        lax.broadcasted_iota(jnp.int32, (1, width), 1) < count
    )
    raw = jnp.where(live, raw + part[j, rows, :].astype(jnp.float32), 0.0)
    own = jnp.where(live, amps[j, rows, :].astype(jnp.float32), 0.0)
    gap = (occ_ref[0, pair // 2] + occ_ref[1, pair % 2]) - vcol_ref[rows, :] - vrow_ref[...]
    inverse = pl.reciprocal(gap, approx=True)
    inverse = inverse * (2.0 - gap * inverse)
    res[j, rows, :] = raw
    mover.put(res.at[j, rows, :], res_hbm.at[pair, rows, :])
    upd[j, rows, :] = (own + raw * inverse).astype(upd.dtype)
    mover.put(upd.at[j, rows, :], upd_hbm.at[pair, rows, :])


def emit_behind(products, emit_one):
    waiting = None
    for j, rows, product in products:
        raw = product()
        if waiting is not None:
            emit_one(*waiting)
        waiting = (j, rows, raw)
    emit_one(*waiting)


def row_kernel(
    i, count_ref, occ_ref, vcol_ref, vrow_ref, b0_hbm, b1_hbm, xt_hbm, x_hbm, coret_hbm, wt_hbm, wdt_hbm,
    amps_hbm, part_hbm, res_hbm, upd_hbm, x, coret, wt, right, left, part, amps, proj, total, res, upd, sem, osem,
):
    width, points = x_hbm.shape
    early = b0_hbm.shape[1]
    head = pl.ds(0, points)
    blocks = [pl.ds(points + k * width, width) for k in range(2)]
    plan = {
        "b0": (b0_hbm, left.at[:, pl.ds(points, early)]),
        "b1": (b1_hbm, left.at[:, pl.ds(points + early, 2 * width - early)]),
        "xt0": (xt_hbm, right.at[0, head, :]),
        "x": (x_hbm, x),
        "wt": (wt_hbm.at[pl.ds(2 * i, 2)], wt),
        "coret": (coret_hbm, coret),
    }
    for j in range(2):
        for k in range(2):
            plan["w%d%d" % (j, k)] = (wdt_hbm.at[2 * j + k], right.at[j, blocks[k], :])
        plan["part%d" % j] = (part_hbm.at[2 * i + j], part.at[j])
        plan["amps%d" % j] = (amps_hbm.at[2 * i + j], amps.at[j])
        if j == 0:
            plan["xt1"] = (xt_hbm, right.at[1, head, :])
    mover = Mover(plan, sem, osem)
    for j in range(2):
        mover.need("b0", "b1", "xt0")
        proj[...] = dot(right[0, head, :], left[:, blocks[j]]).astype(proj.dtype)
        mover.need("x", "coret", "wt")
        inner = dot(proj[...], x[...])
        total[j] = (
            wt[j].astype(jnp.float32) + coret[...].astype(jnp.float32) * inner
        ).astype(total.dtype)
    def products():
        for j in range(2):
            for at, rows in enumerate(strips(width, STRIP)):

                def product(j=j, at=at, rows=rows):
                    if at == 0:
                        left[:, head] = dot(x[...], total[j]).astype(left.dtype)
                        mover.need("xt%d" % j, "w%d0" % j, "w%d1" % j, "part%d" % j, "amps%d" % j)
                    return dot(left[rows, :], right[j])

                yield j, rows, product

    def emit_one(j, rows, raw):
        emit(
            mover, 2 * i + j, j, rows, raw, count_ref, occ_ref, vcol_ref, vrow_ref,
            part, amps, res, upd, res_hbm, upd_hbm,
        )

    emit_behind(products(), emit_one)
    mover.drain()


def row(i, count, occ, vcol, vrow, b0, b1, xt, x, coret, wt, wdt, amp4, part):
    width, points = x.shape
    vmem = pl.BlockSpec(memory_space=pltpu.VMEM)
    smem = pl.BlockSpec(memory_space=pltpu.SMEM)
    hbm = pl.BlockSpec(memory_space=pl.ANY)
    f32, bf16 = jnp.float32, jnp.bfloat16
    depth = points + 2 * width
    return pl.pallas_call(
        functools.partial(row_kernel, i),
        out_shape=[jax.ShapeDtypeStruct(part.shape, f32), jax.ShapeDtypeStruct(part.shape, bf16)],
        in_specs=[smem, smem, vmem, vmem] + [hbm] * 9,
        out_specs=[hbm] * 2,
        scratch_shapes=[
            pltpu.VMEM((points, width), bf16),
            pltpu.VMEM((points, points), bf16),
            pltpu.VMEM((2, points, points), bf16),
            pltpu.VMEM((2, depth, width), bf16),
            pltpu.VMEM((width, depth), bf16),
            pltpu.VMEM((2, width, width), bf16),
            pltpu.VMEM((2, width, width), bf16),
            pltpu.VMEM((points, width), bf16),
            pltpu.VMEM((2, points, points), bf16),
            pltpu.VMEM((2, width, width), f32),
            pltpu.VMEM((2, width, width), bf16),
            pltpu.SemaphoreType.DMA((15,)),
            pltpu.SemaphoreType.DMA((4 * (width // STRIP),)),
        ],
        compiler_params=pltpu.CompilerParams(vmem_limit_bytes=VMEM_LIMIT),
        name="row_%d" % i,
    )(count, occ, vcol, vrow, b0, b1, xt, x, coret, wt, wdt, amp4, part)


def piece_kernel(i, k, low, high, end, count_ref, occ_ref, vcol_ref, vrow_ref, *refs):
    last = k == 1 and end
    scratch = 13
    refs, (x, coret, before, right, left, part, amps, proj, total, res, upd, sem, osem) = (
        refs[:-scratch], refs[-scratch:]
    )
    (b_hbm, xt_hbm, x_hbm, coret_hbm, before_hbm, wdt_hbm, amps_hbm, part_hbm) = refs[:8]
    outs = refs[8:]
    width, points = x_hbm.shape
    head, rest = pl.ds(0, points), pl.ds(points, high - low)
    cut = pl.ds(low, high - low)
    plan = {
        "b": (b_hbm, left.at[:, rest]),
        "xt": (xt_hbm, right.at[k, head, :]),
        "x": (x_hbm, x) if end else (x_hbm.at[cut], x.at[cut]),
        "coret": (coret_hbm, coret),
        "before": (before_hbm if low > 0 else before_hbm.at[2 * i + k], before),
    }
    for j in (1 - k, k):
        plan["w%d" % j] = (wdt_hbm.at[2 * j + k, cut, :], right.at[j, rest, :])
        plan["part%d" % j] = (part_hbm.at[2 * i + j], part.at[j])
        if last:
            plan["amps%d" % j] = (amps_hbm.at[2 * i + j], amps.at[j])
    mover = Mover(plan, sem, osem)

    def products(plan):
        for j, columns in plan:
            for rows in strips(width, STRIP):

                def product(j=j, columns=columns, rows=rows):
                    mover.need("w%d" % j, "part%d" % j, "amps%d" % j)
                    return dot(left[rows, columns], right[j, columns, :])

                yield j, rows, product

    def emit_one(j, rows, raw):
        if last:
            emit(
                mover, 2 * i + j, j, rows, raw, count_ref, occ_ref, vcol_ref, vrow_ref,
                part, amps, res, upd, outs[-2], outs[-1],
            )
        else:
            part[j, rows, :] = (raw + part[j, rows, :].astype(jnp.float32)).astype(part.dtype)
            mover.put(part.at[j, rows, :], outs[0].at[2 * i + j, rows, :])

    mover.need("b", "xt")
    proj[...] = dot(right[k, head, :], left[:, rest]).astype(proj.dtype)
    mover.need("x")
    inner = dot(proj[...], x[cut, :])
    mover.need("coret", "before")
    total[...] = (
        before[...].astype(jnp.float32) + coret[...].astype(jnp.float32) * inner
    ).astype(total.dtype)
    if end:
        left[:, head] = dot(x[...], total[...]).astype(left.dtype)
        emit_behind(products([(1 - k, rest), (k, pl.ds(0, points + high - low))]), emit_one)
    else:
        mover.put(total, outs[1])
        emit_behind(products([(1 - k, rest), (k, rest)]), emit_one)
    mover.drain()


def piece(i, k, low, high, count, occ, vcol, vrow, b, xt, x, coret, before, wdt, amp4, part, residual, updated):
    width, points = x.shape
    end = high == width
    last = k == 1 and end
    vmem = pl.BlockSpec(memory_space=pltpu.VMEM)
    smem = pl.BlockSpec(memory_space=pltpu.SMEM)
    hbm = pl.BlockSpec(memory_space=pl.ANY)
    f32, bf16 = jnp.float32, jnp.bfloat16
    operands = [count, occ, vcol, vrow, b, xt, x, coret, before, wdt, amp4, part]
    if last:
        out_shape = [jax.ShapeDtypeStruct(part.shape, f32), jax.ShapeDtypeStruct(part.shape, bf16)]
        alias = {len(operands): 0, len(operands) + 1: 1}
        operands += [residual, updated]
    else:
        out_shape = [jax.ShapeDtypeStruct(part.shape, bf16)]
        alias = {len(operands) - 1: 0}
        if not end:
            out_shape.append(jax.ShapeDtypeStruct((points, points), bf16))
    return pl.pallas_call(
        functools.partial(piece_kernel, i, k, low, high, end),
        out_shape=out_shape,
        in_specs=[smem, smem, vmem, vmem] + [hbm] * (len(operands) - 4),
        out_specs=[hbm] * len(out_shape),
        scratch_shapes=[
            pltpu.VMEM((points, width), bf16),
            pltpu.VMEM((points, points), bf16),
            pltpu.VMEM((points, points), bf16),
            pltpu.VMEM((2, points + high - low, width), bf16),
            pltpu.VMEM((width, points + high - low), bf16),
            pltpu.VMEM((2, width, width), bf16),
            pltpu.VMEM((2, width, width), bf16),
            pltpu.VMEM((points, high - low), bf16),
            pltpu.VMEM((points, points), bf16),
            pltpu.VMEM((2, width, width), f32),
            pltpu.VMEM((2, width, width), bf16),
            pltpu.SemaphoreType.DMA((11,)),
            pltpu.SemaphoreType.DMA((8,)),
        ],
        input_output_aliases=alias,
        compiler_params=pltpu.CompilerParams(vmem_limit_bytes=VMEM_LIMIT),
        name="piece_%d%d_%d" % (i, k, low),
    )(*operands)


def per_device(
    amps, x_factor, core, cycle_w, domain_tiles, domain_count, tile_slot, occ_energy, virt_energy
):
    occ = amps.shape[2]
    width = amps.shape[4]
    tile_width = x_factor.shape[1]
    grid_points = x_factor.shape[2]
    window = cycle_w.shape[4]
    cols = lax.axis_size("col")
    amp4 = amps[0, 0].reshape(occ * occ, width, width)
    shard = cycle_w[0].reshape(occ * occ, tile_width, window)

    early, split = width // 2, 512
    tiles, count = domain_tiles[0, 0], domain_count
    xall, wall, far, first, coret, *turned = gather_parts(x_factor, shard, amp4, core, early, split)
    xall = xall.reshape(-1, tile_width, grid_points)
    mirror = [(i, (i + cols // 2) % cols) for i in range(cols)]
    second, third, fourth = [lax.ppermute(part, "col", mirror) for part in turned[:3]]
    side = lax.ppermute(far, "col", [(i, i ^ 2) for i in range(cols)])

    x, xt, wt = own_ladder(tiles, count, tile_slot, xall, amp4, core)
    side, tail, wt = lax.optimization_barrier((side, turned[3], wt))
    fifth = lax.ppermute(tail, "col", mirror)
    twin = lax.ppermute(side, "col", [(i, i ^ 1) for i in range(cols)])
    wdt, part, vcol, vrow = own_cycle(tiles, count, virt_energy[None, :], wall, far, side, twin, amp4)
    energies = (count, occ_energy[0, 0], vcol, vrow)
    residual, updated = row(0, *energies, first, second, xt, x, coret, wt, wdt, amp4, part)
    fixed = (xt, x, coret)
    part, = piece(1, 0, 0, width, *energies, third, *fixed, wt, wdt, amp4, part, None, None)
    part, total = piece(1, 1, 0, split, *energies, fourth, *fixed, wt, wdt, amp4, part, None, None)
    residual, updated = piece(
        1, 1, split, width, *energies, fifth, *fixed, total, wdt, amp4, part, residual, updated
    )
    return residual.reshape(amps.shape), updated.reshape(amps.shape)


def solution(mesh):
    in_specs = (
        P("row", "col", None, None, None, None),
        P("row", None, None),
        P(),
        P("row", None, None, "col", None),
        P("row", "col", None),
        P("row", "col"),
        P(),
        P("row", "col", None, None),
        P(),
    )
    out_specs = (P("row", "col", None, None, None, None), P("row", "col", None, None, None, None))
    return jax.shard_map(
        per_device, mesh=mesh, in_specs=in_specs, out_specs=out_specs, check_vma=False
    )
```

```python
import functools

import jax
import jax.numpy as jnp
from jax import lax
from jax.experimental import pallas as pl
from jax.experimental.pallas import tpu as pltpu
from jax.sharding import PartitionSpec as P

MESH = pl.DeviceIdType.MESH
VMEM_LIMIT = 65300 * 1024
STRIP = 384


def dot(a, b):
    return jnp.dot(a, b, preferred_element_type=jnp.float32)


def tapered(width):
    return [pl.ds(0, width // 2), pl.ds(width // 2, width // 3), pl.ds(width // 2 + width // 3, width // 6)]


def strips(width, step):
    return [pl.ds(start, step) for start in range(0, width, step)]


def remote(src, dst, sems, index, device):
    return pltpu.make_async_remote_copy(
        src_ref=src, dst_ref=dst, send_sem=sems[0].at[index], recv_sem=sems[1].at[index],
        device_id=device, device_id_type=MESH,
    )


def greet(devices):
    barrier = pltpu.get_barrier_semaphore()
    for device in devices:
        pl.semaphore_signal(barrier, inc=1, device_id=device, device_id_type=MESH)
    pl.semaphore_wait(barrier, len(devices))


def gather_kernel(
    x_ref, w_ref, amps_ref, core_ref, xall_ref, wall_ref, far_ref, first_ref, coret_ref, *refs
):
    cuts, (plain, turned, fixed, wsend, wrecv, xsend, xrecv, msend, mrecv, local, tsem) = refs[:-11], refs[-11:]
    r = lax.axis_index("row")
    c = lax.axis_index("col")
    rows = lax.axis_size("row")
    cols = lax.axis_size("col")
    forth = (r, (c + 4) % cols)
    back = (r, (c + cols - 4) % cols)
    mirror = (r, (c + cols // 2) % cols)
    zside = (r, c + 2 - 4 * ((c // 2) % 2))
    twin = (r, c + 1 - 2 * (c % 2))
    beside = r + 1 - 2 * (r % 2)
    core = c % 2
    half = w_ref.shape[0] // 2
    width = plain.shape[1]
    y_steps = range(1, rows // 2)

    amps_in = [pltpu.make_async_copy(amps_ref.at[q], plain.at[q], tsem.at[q]) for q in range(4)]
    core_in = pltpu.make_async_copy(core_ref, fixed.at[0], tsem.at[4])
    for copy in amps_in + [core_in]:
        copy.start()
    greet(
        [forth, back, mirror, zside, twin, (beside, c)]
        + [((r + 2 * step) % rows, c) for step in y_steps]
    )
    wsems, xsems = (wsend, wrecv), (xsend, xrecv)
    started = []

    def send(*args):
        copy = remote(*args)
        copy.start()
        started.append(copy)

    def arrived(part, sems, index):
        remote(part, part, sems, index, twin).wait_recv()

    def shard(offset, plane, side):
        if offset in (1, 2) and plane + side == 0:
            return far_ref.at[offset - 1]
        x = (c // 4 + offset) % (cols // 4)
        z = (c // 2) % 2
        z = z + plane * (1 - 2 * z)
        k = core + side * (1 - 2 * core)
        return wall_ref.at[x * 4 + z * 2 + k]

    def to_twin(offset):
        x = (c // 4 + offset) % (cols // 4)
        send(shard(offset, 0, 0), wall_ref.at[x * 4 + c % 4], wsems, 6 + offset, twin)

    def transpose(q, p):
        amps_in[q].wait()
        for cut in strips(width, 256):
            turned[p, :, cut] = plain[q, cut, :].T

    own = wall_ref.at[c]
    send(w_ref, own, wsems, 0, forth)
    send(w_ref, far_ref.at[0], wsems, 1, back)
    send(x_ref.at[core], xall_ref.at[r, core], xsems, 0, (beside, c))
    send(w_ref, own, wsems, 4, zside)
    for step in y_steps:
        send(x_ref.at[core], xall_ref.at[r, core], xsems, step, ((r + 2 * step) % rows, c))
    send(w_ref, own, wsems, 6, twin)
    own_w = pltpu.make_async_copy(w_ref, own, local.at[0])
    own_x = pltpu.make_async_copy(x_ref, xall_ref.at[r], local.at[1])
    own_w.start()
    own_x.start()
    transpose(0, 0)

    part = xall_ref.at[beside, core]
    arrived(part, xsems, 0)
    for step in y_steps:
        send(part, part, xsems, 3 + step, ((r + 2 * step) % rows, c))
    send(part, part, xsems, 7, twin)

    part = shard(3, 0, 0)
    arrived(part, wsems, 0)
    send(part.at[:half], far_ref.at[1, :half], wsems, 2, forth)
    send(part, part, wsems, 5, zside)
    arrived(far_ref.at[0], wsems, 1)
    send(far_ref.at[0, half:], far_ref.at[1, half:], wsems, 3, back)
    send(turned.at[0, :, pl.ds(0, first_ref.shape[1])], first_ref, (msend, mrecv), 0, mirror)
    to_twin(3)
    to_twin(1)
    transpose(2, 1)
    for step in y_steps:
        origin = (r + rows - 2 * step) % rows
        arrived(xall_ref.at[origin, core], xsems, step)
        send(xall_ref.at[origin, core], xall_ref.at[origin, core], xsems, 7 + step, twin)
    transpose(1, 2)
    part = shard(0, 1, 0)
    arrived(part, wsems, 4)
    send(part, part, wsems, 10, twin)
    for step in y_steps:
        origin = (r + rows - 2 * step) % rows
        origin = origin + 1 - 2 * (origin % 2)
        arrived(xall_ref.at[origin, core], xsems, 3 + step)
        send(xall_ref.at[origin, core], xall_ref.at[origin, core], xsems, 10 + step, twin)
    arrived(far_ref.at[1, :half], wsems, 2)
    arrived(far_ref.at[1, half:], wsems, 3)
    to_twin(2)
    transpose(3, 3)
    early, split = first_ref.shape[1], cuts[2].shape[1]
    moves = (
        (0, pl.ds(early, width - early), 0, pl.ds(0, width - early)),
        (1, pl.ds(0, width), 0, pl.ds(width - early, width)),
        (2, pl.ds(0, width), 1, pl.ds(0, width)),
        (3, pl.ds(0, split), 2, pl.ds(0, split)),
        (3, pl.ds(split, width - split), 3, pl.ds(0, width - split)),
    )
    outs = [
        pltpu.make_async_copy(turned.at[p, :, source], cuts[q].at[:, target], local.at[3 + at])
        for at, (p, source, q, target) in enumerate(moves)
    ]
    core_in.wait()
    for cut in strips(width, 256):
        fixed[1, :, cut] = fixed[0, cut, :].T
    outs.append(pltpu.make_async_copy(fixed.at[1], coret_ref, local.at[2]))
    for copy in outs:
        copy.start()
    part = shard(3, 1, 0)
    arrived(part, wsems, 5)
    send(part, part, wsems, 11, twin)

    for offset in range(4):
        arrived(shard(offset, 0, 1), wsems, 6 + offset)
    arrived(shard(0, 1, 1), wsems, 10)
    arrived(shard(3, 1, 1), wsems, 11)
    arrived(xall_ref.at[beside, 1 - core], xsems, 7)
    for step in y_steps:
        origin = (r + rows - 2 * step) % rows
        arrived(xall_ref.at[origin, 1 - core], xsems, 7 + step)
        origin = origin + 1 - 2 * (origin % 2)
        arrived(xall_ref.at[origin, 1 - core], xsems, 10 + step)
    remote(first_ref, first_ref, (msend, mrecv), 0, mirror).wait_recv()
    for copy in started:
        copy.wait_send()
    for copy in outs + [own_w, own_x]:
        copy.wait()


def gather_parts(x_factor, shard, amp4, core, early, split):
    rows = lax.axis_size("row")
    cols = lax.axis_size("col")
    width = amp4.shape[1]
    hbm = pl.BlockSpec(memory_space=pl.ANY)
    bf16 = jnp.bfloat16
    dma = pltpu.SemaphoreType.DMA
    shapes = [(rows,) + x_factor.shape, (cols,) + shard.shape, (2,) + shard.shape, (width, early), core.shape]
    shapes += [(width, 2 * width - early), (width, width)]
    shapes += [(width, split), (width, width - split)]
    return pl.pallas_call(
        gather_kernel,
        out_shape=[jax.ShapeDtypeStruct(shape, bf16) for shape in shapes],
        in_specs=[hbm] * 4,
        out_specs=[hbm] * len(shapes),
        scratch_shapes=[
            pltpu.VMEM(amp4.shape, bf16),
            pltpu.VMEM(amp4.shape, bf16),
            pltpu.VMEM((2,) + core.shape, bf16),
            dma((12,)),
            dma((12,)),
            dma((14,)),
            dma((14,)),
            dma((1,)),
            dma((1,)),
            dma((8,)),
            dma((5,)),
        ],
        compiler_params=pltpu.CompilerParams(
            collective_id=0, has_side_effects=True, vmem_limit_bytes=VMEM_LIMIT
        ),
        name="gather_parts",
    )(x_factor, shard, amp4, core)


def own_ladder_kernel(
    tiles_ref, count_ref, slot_ref, xall_ref, amps_ref, core_ref, x_ref, xt_ref, wt_ref, gathered, proj, sem
):
    @pl.when(pl.program_id(0) == 0)
    def _():
        tile = xall_ref.shape[1]
        copies = []
        for s in range(tiles_ref.shape[0]):
            copy = pltpu.make_async_copy(
                xall_ref.at[slot_ref[tiles_ref[s]]], gathered.at[pl.ds(s * tile, tile), :], sem.at[s]
            )
            copy.start()
            copies.append(copy)
        for copy in copies:
            copy.wait()
        live = lax.broadcasted_iota(jnp.int32, (x_ref.shape[0], 1), 0) < count_ref[0, 0] * tile
        x_ref[...] = jnp.where(live, gathered[...].astype(jnp.float32), 0.0).astype(x_ref.dtype)
        for cut in strips(x_ref.shape[0], 256):
            xt_ref[:, cut] = x_ref[cut, :].T

    proj[...] = dot(xt_ref[...], amps_ref[0]).astype(proj.dtype)
    inner = dot(proj[...], x_ref[...])
    wt_ref[0] = (core_ref[...].astype(jnp.float32) * inner).astype(wt_ref.dtype)


def own_ladder(tiles, count, tile_slot, xall, amp4, core):
    width = amp4.shape[1]
    points = core.shape[0]
    smem = pl.BlockSpec(memory_space=pltpu.SMEM)
    bf16 = jnp.bfloat16

    def whole(shape):
        return pl.BlockSpec(shape, lambda p: (0, 0))

    return pl.pallas_call(
        own_ladder_kernel,
        out_shape=(
            jax.ShapeDtypeStruct((width, points), bf16),
            jax.ShapeDtypeStruct((points, width), bf16),
            jax.ShapeDtypeStruct((4, points, points), bf16),
        ),
        grid=(4,),
        in_specs=[
            smem, smem, smem, pl.BlockSpec(memory_space=pl.ANY),
            pl.BlockSpec((1, width, width), lambda p: (p, 0, 0)), whole((points, points)),
        ],
        out_specs=(
            whole((width, points)), whole((points, width)),
            pl.BlockSpec((1, points, points), lambda p: (p, 0, 0)),
        ),
        scratch_shapes=[
            pltpu.VMEM((width, points), bf16),
            pltpu.VMEM((points, width), bf16),
            pltpu.SemaphoreType.DMA((tiles.shape[0],)),
        ],
        compiler_params=pltpu.CompilerParams(vmem_limit_bytes=VMEM_LIMIT),
        name="own_ladder",
    )(tiles, count, tile_slot, xall, amp4, core)


def window_index(tiles_ref, count_ref, tile, shape, axis):
    at = lax.broadcasted_iota(jnp.int32, shape, axis)
    index = jnp.full(shape, -1, jnp.int32)
    for s in range(tiles_ref.shape[0]):
        inside = (at >= s * tile) & (at < (s + 1) * tile) & (s < count_ref[0, 0])
        index = jnp.where(inside, at + (tiles_ref[s] - s) * tile, index)
    return index


def own_cycle_kernel(
    tiles_ref, count_ref, occ_ref, virt_ref, wall_ref, far_ref, side_ref, twin_ref, a0_ref, a1_ref,
    wdt_ref, cyc_ref, down_ref, along_ref, wsel, wd, pick, sem,
):
    p = pl.program_id(0)
    tile = wall_ref.shape[2]
    slots = tiles_ref.shape[0]
    width = wd.shape[1]
    window = virt_ref.shape[1]

    @pl.when(p == 0)
    def _():
        me = lax.axis_index("col")
        for first in range(2):
            for s in range(slots):
                number = tiles_ref[s]
                offset = ((number >> 2) + 4 - (me >> 2)) & 3
                plane = ((number >> 1) + (me >> 1)) & 1
                side = (number + me) & 1
                apart = (offset == 1) | (offset == 2)
                dst = wsel.at[pl.ds(2 * first, 2), pl.ds(s * tile, tile), :]

                def fetch(source, at, dst=dst, done=sem.at[first, s], first=first):
                    pltpu.make_async_copy(source.at[at, pl.ds(2 * first, 2)], dst, done).start()

                @pl.when(jnp.logical_not(apart) | ((plane == 0) & (side == 1)))
                def _(number=number, fetch=fetch):
                    fetch(wall_ref, number)

                for source, at_plane, at_side in ((far_ref, 0, 0), (side_ref, 1, 0), (twin_ref, 1, 1)):

                    @pl.when(apart & (plane == at_plane) & (side == at_side))
                    def _(source=source, offset=offset, fetch=fetch):
                        fetch(source, offset - 1)

        along = lax.broadcasted_iota(jnp.int32, pick.shape, 0)
        picked = window_index(tiles_ref, count_ref, tile, (1, width), 1)
        pick[...] = jnp.where(along == picked, 1.0, 0.0).astype(pick.dtype)
        picked = window_index(tiles_ref, count_ref, tile, (width, 1), 0)
        along = lax.broadcasted_iota(jnp.int32, (width, window), 1)
        levels = jnp.sum(jnp.where(along == picked, virt_ref[...], 0.0), axis=1, keepdims=True)
        lane = lax.broadcasted_iota(jnp.int32, (1, 128), 1)
        sums = jnp.zeros((1, 128), jnp.float32)
        for i in range(2):
            for j in range(2):
                sums = jnp.where(lane == 2 * i + j, occ_ref[0, i] + occ_ref[1, j], sums)
        live = jnp.where(picked >= 0, 1.0, 0.0)
        down_ref[...] = jnp.where(lane < 4, sums - levels, live)
        line = lax.broadcasted_iota(jnp.int32, (8, 1), 0)
        wide_levels = jnp.broadcast_to(levels, (width, 128)).T[:8, :]
        wide_live = jnp.broadcast_to(live, (width, 128)).T[:8, :]
        along_ref[...] = jnp.where(line == 0, wide_levels, wide_live)

    for first in range(2):

        @pl.when(p == 2 * first)
        def _(first=first):
            for s in range(slots):
                pltpu.make_async_copy(
                    wall_ref.at[0, pl.ds(0, 2)],
                    wsel.at[pl.ds(2 * first, 2), pl.ds(s * tile, tile), :],
                    sem.at[first, s],
                ).wait()
            for k in range(2):
                wd[k] = dot(wsel[2 * first + k], pick[...]).astype(wd.dtype)
                for cut in strips(width, 256):
                    wdt_ref[k, :, cut] = wd[k, cut, :].T

    cyc_ref[0] = (dot(wd[0], a0_ref[0]) + dot(wd[1], a1_ref[0])).astype(cyc_ref.dtype)


def own_cycle(tiles, count, occ, virt, wall, far, side, twin, amp4):
    width = amp4.shape[1]
    slots, window = tiles.shape[0], wall.shape[3]
    smem = pl.BlockSpec(memory_space=pltpu.SMEM)
    hbm = pl.BlockSpec(memory_space=pl.ANY)
    f32, bf16 = jnp.float32, jnp.bfloat16
    return pl.pallas_call(
        own_cycle_kernel,
        out_shape=(
            jax.ShapeDtypeStruct((4, width, width), bf16),
            jax.ShapeDtypeStruct((4, width, width), bf16),
            jax.ShapeDtypeStruct((width, 128), f32),
            jax.ShapeDtypeStruct((8, width), f32),
        ),
        grid=(4,),
        in_specs=[
            smem,
            smem,
            smem,
            pl.BlockSpec((1, window), lambda p: (0, 0)),
            hbm,
            hbm,
            hbm,
            hbm,
            pl.BlockSpec((1, width, width), lambda p: (p % 2, 0, 0)),
            pl.BlockSpec((1, width, width), lambda p: (2 + p % 2, 0, 0)),
        ],
        out_specs=(
            pl.BlockSpec((2, width, width), lambda p: (p // 2, 0, 0)),
            pl.BlockSpec((1, width, width), lambda p: (p, 0, 0)),
            pl.BlockSpec((width, 128), lambda p: (0, 0)),
            pl.BlockSpec((8, width), lambda p: (0, 0)),
        ),
        scratch_shapes=[
            pltpu.VMEM((4, width, window), bf16),
            pltpu.VMEM((2, width, width), bf16),
            pltpu.VMEM((window, width), bf16),
            pltpu.SemaphoreType.DMA((2, slots)),
        ],
        compiler_params=pltpu.CompilerParams(vmem_limit_bytes=VMEM_LIMIT),
        name="own_cycle",
    )(tiles, count, occ, virt, wall, far, side, twin, amp4, amp4)


class Mover:
    def __init__(self, plan, in_sem, out_sem):
        self.out_sem = out_sem
        self.outs = []
        self.loads = {}
        for at, (name, (src, dst)) in enumerate(plan.items()):
            self.loads[name] = pltpu.make_async_copy(src, dst, in_sem.at[at])
            self.loads[name].start()

    def need(self, *names):
        for name in names:
            if name in self.loads:
                self.loads.pop(name).wait()

    def put(self, src, dst):
        copy = pltpu.make_async_copy(src, dst, self.out_sem.at[len(self.outs)])
        copy.start()
        self.outs.append(copy)

    def drain(self):
        for copy in self.outs:
            copy.wait()


def emit(mover, pair, j, rows, raw, down, along, part, amps, res, upd, res_hbm, upd_hbm):
    mask = down[rows, 4:5] * along[1:2, :]
    raw = (raw + part[j, rows, :].astype(jnp.float32)) * mask
    own = amps[j, rows, :].astype(jnp.float32) * mask
    gap = down[rows, pair:pair + 1] - along[0:1, :]
    inverse = pl.reciprocal(gap, approx=True)
    inverse = inverse * (2.0 - gap * inverse)
    res[j, rows, :] = raw
    mover.put(res.at[j, rows, :], res_hbm.at[pair, rows, :])
    upd[j, rows, :] = (own + raw * inverse).astype(upd.dtype)
    mover.put(upd.at[j, rows, :], upd_hbm.at[pair, rows, :])


def emit_behind(products, emit_one):
    waiting = None
    for j, rows, product in products:
        raw = product()
        if waiting is not None:
            emit_one(*waiting)
        waiting = (j, rows, raw)
    emit_one(*waiting)


def row_kernel(
    i, down_hbm, along_hbm, b0_hbm, b1_hbm, xt_hbm, x_hbm, coret_hbm, wt_hbm, wdt_hbm,
    amps_hbm, part_hbm, res_hbm, upd_hbm, x, coret, wt, right, left, part, amps, proj, total, res, upd, down, along,
    sem, osem,
):
    width, points = x_hbm.shape
    early = b0_hbm.shape[1]
    head = pl.ds(0, points)
    blocks = [pl.ds(points + k * width, width) for k in range(2)]
    plan = {
        "b0": (b0_hbm, left.at[:, pl.ds(points, early)]),
        "b1": (b1_hbm, left.at[:, pl.ds(points + early, 2 * width - early)]),
        "xt0": (xt_hbm, right.at[0, head, :]),
        "x": (x_hbm, x),
        "wt": (wt_hbm.at[pl.ds(2 * i, 2)], wt),
        "coret": (coret_hbm, coret),
        "down": (down_hbm, down),
        "along": (along_hbm, along),
    }
    for j in range(2):
        for k in range(2):
            plan["w%d%d" % (j, k)] = (wdt_hbm.at[2 * j + k], right.at[j, blocks[k], :])
        plan["part%d" % j] = (part_hbm.at[2 * i + j], part.at[j])
        plan["amps%d" % j] = (amps_hbm.at[2 * i + j], amps.at[j])
        if j == 0:
            plan["xt1"] = (xt_hbm, right.at[1, head, :])
    mover = Mover(plan, sem, osem)
    for j in range(2):
        mover.need("b0", "b1", "xt0")
        proj[...] = dot(right[0, head, :], left[:, blocks[j]]).astype(proj.dtype)
        mover.need("x", "coret", "wt")
        inner = dot(proj[...], x[...])
        total[j] = (
            wt[j].astype(jnp.float32) + coret[...].astype(jnp.float32) * inner
        ).astype(total.dtype)
    def products():
        for j in range(2):
            for at, rows in enumerate(strips(width, STRIP)):

                def product(j=j, at=at, rows=rows):
                    if at == 0:
                        left[:, head] = dot(x[...], total[j]).astype(left.dtype)
                        mover.need("down", "along", "xt%d" % j, "w%d0" % j, "w%d1" % j, "part%d" % j, "amps%d" % j)
                    return dot(left[rows, :], right[j])

                yield j, rows, product

    def emit_one(j, rows, raw):
        emit(
            mover, 2 * i + j, j, rows, raw, down, along, part, amps, res, upd, res_hbm, upd_hbm,
        )

    emit_behind(products(), emit_one)
    mover.drain()


def row(i, down, along, b0, b1, xt, x, coret, wt, wdt, amp4, part):
    width, points = x.shape
    hbm = pl.BlockSpec(memory_space=pl.ANY)
    f32, bf16 = jnp.float32, jnp.bfloat16
    depth = points + 2 * width
    return pl.pallas_call(
        functools.partial(row_kernel, i),
        out_shape=[jax.ShapeDtypeStruct(part.shape, f32), jax.ShapeDtypeStruct(part.shape, bf16)],
        in_specs=[hbm] * 11,
        out_specs=[hbm] * 2,
        scratch_shapes=[
            pltpu.VMEM((points, width), bf16),
            pltpu.VMEM((points, points), bf16),
            pltpu.VMEM((2, points, points), bf16),
            pltpu.VMEM((2, depth, width), bf16),
            pltpu.VMEM((width, depth), bf16),
            pltpu.VMEM((2, width, width), bf16),
            pltpu.VMEM((2, width, width), bf16),
            pltpu.VMEM((points, width), bf16),
            pltpu.VMEM((2, points, points), bf16),
            pltpu.VMEM((2, width, width), f32),
            pltpu.VMEM((2, width, width), bf16),
            pltpu.VMEM((width, 128), f32),
            pltpu.VMEM((8, width), f32),
            pltpu.SemaphoreType.DMA((17,)),
            pltpu.SemaphoreType.DMA((4 * (width // STRIP),)),
        ],
        compiler_params=pltpu.CompilerParams(vmem_limit_bytes=VMEM_LIMIT),
        name="row_%d" % i,
    )(down, along, b0, b1, xt, x, coret, wt, wdt, amp4, part)


def piece_kernel(i, k, low, high, end, down_hbm, along_hbm, *refs):
    last = k == 1 and end
    scratch = 15
    refs, (x, coret, before, right, left, part, amps, proj, total, res, upd, down, along, sem, osem) = (
        refs[:-scratch], refs[-scratch:]
    )
    (b_hbm, xt_hbm, x_hbm, coret_hbm, before_hbm, wdt_hbm, amps_hbm, part_hbm) = refs[:8]
    outs = refs[8:]
    width, points = x_hbm.shape
    head, rest = pl.ds(0, points), pl.ds(points, high - low)
    cut = pl.ds(low, high - low)
    plan = {
        "b": (b_hbm, left.at[:, rest]),
        "xt": (xt_hbm, right.at[k, head, :]),
        "x": (x_hbm, x) if end else (x_hbm.at[cut], x.at[cut]),
        "coret": (coret_hbm, coret),
        "before": (before_hbm if low > 0 else before_hbm.at[2 * i + k], before),
    }
    if last:
        plan["down"] = (down_hbm, down)
        plan["along"] = (along_hbm, along)
    for j in (1 - k, k):
        plan["w%d" % j] = (wdt_hbm.at[2 * j + k, cut, :], right.at[j, rest, :])
        plan["part%d" % j] = (part_hbm.at[2 * i + j], part.at[j])
        if last:
            plan["amps%d" % j] = (amps_hbm.at[2 * i + j], amps.at[j])
    mover = Mover(plan, sem, osem)

    def products(plan):
        for j, columns in plan:
            for rows in tapered(width) if last and j == k else strips(width, STRIP):

                def product(j=j, columns=columns, rows=rows):
                    mover.need("down", "along", "w%d" % j, "part%d" % j, "amps%d" % j)
                    return dot(left[rows, columns], right[j, columns, :])

                yield j, rows, product

    def emit_one(j, rows, raw):
        if last:
            emit(
                mover, 2 * i + j, j, rows, raw, down, along, part, amps, res, upd, outs[-2], outs[-1],
            )
        else:
            part[j, rows, :] = (raw + part[j, rows, :].astype(jnp.float32)).astype(part.dtype)
            mover.put(part.at[j, rows, :], outs[0].at[2 * i + j, rows, :])

    mover.need("b", "xt")
    proj[...] = dot(right[k, head, :], left[:, rest]).astype(proj.dtype)
    mover.need("x")
    inner = dot(proj[...], x[cut, :])
    mover.need("coret", "before")
    total[...] = (
        before[...].astype(jnp.float32) + coret[...].astype(jnp.float32) * inner
    ).astype(total.dtype)
    if end:
        left[:, head] = dot(x[...], total[...]).astype(left.dtype)
        emit_behind(products([(1 - k, rest), (k, pl.ds(0, points + high - low))]), emit_one)
    else:
        mover.put(total, outs[1])
        emit_behind(products([(1 - k, rest), (k, rest)]), emit_one)
    mover.drain()


def piece(i, k, low, high, down, along, b, xt, x, coret, before, wdt, amp4, part, residual, updated):
    width, points = x.shape
    end = high == width
    last = k == 1 and end
    hbm = pl.BlockSpec(memory_space=pl.ANY)
    f32, bf16 = jnp.float32, jnp.bfloat16
    operands = [down, along, b, xt, x, coret, before, wdt, amp4, part]
    if last:
        out_shape = [jax.ShapeDtypeStruct(part.shape, f32), jax.ShapeDtypeStruct(part.shape, bf16)]
        alias = {len(operands): 0, len(operands) + 1: 1}
        operands += [residual, updated]
    else:
        out_shape = [jax.ShapeDtypeStruct(part.shape, bf16)]
        alias = {len(operands) - 1: 0}
        if not end:
            out_shape.append(jax.ShapeDtypeStruct((points, points), bf16))
    return pl.pallas_call(
        functools.partial(piece_kernel, i, k, low, high, end),
        out_shape=out_shape,
        in_specs=[hbm] * len(operands),
        out_specs=[hbm] * len(out_shape),
        scratch_shapes=[
            pltpu.VMEM((points, width), bf16),
            pltpu.VMEM((points, points), bf16),
            pltpu.VMEM((points, points), bf16),
            pltpu.VMEM((2, points + high - low, width), bf16),
            pltpu.VMEM((width, points + high - low), bf16),
            pltpu.VMEM((2, width, width), bf16),
            pltpu.VMEM((2, width, width), bf16),
            pltpu.VMEM((points, high - low), bf16),
            pltpu.VMEM((points, points), bf16),
            pltpu.VMEM((2, width, width), f32),
            pltpu.VMEM((2, width, width), bf16),
            pltpu.VMEM((width, 128), f32),
            pltpu.VMEM((8, width), f32),
            pltpu.SemaphoreType.DMA((13,)),
            pltpu.SemaphoreType.DMA((10,)),
        ],
        input_output_aliases=alias,
        compiler_params=pltpu.CompilerParams(vmem_limit_bytes=VMEM_LIMIT),
        name="piece_%d%d_%d" % (i, k, low),
    )(*operands)


def per_device(
    amps, x_factor, core, cycle_w, domain_tiles, domain_count, tile_slot, occ_energy, virt_energy
):
    occ = amps.shape[2]
    width = amps.shape[4]
    tile_width = x_factor.shape[1]
    grid_points = x_factor.shape[2]
    window = cycle_w.shape[4]
    cols = lax.axis_size("col")
    amp4 = amps[0, 0].reshape(occ * occ, width, width)
    shard = cycle_w[0].reshape(occ * occ, tile_width, window)

    early, split = 256, 512
    tiles, count = domain_tiles[0, 0], domain_count
    xall, wall, far, first, coret, *turned = gather_parts(x_factor, shard, amp4, core, early, split)
    xall = xall.reshape(-1, tile_width, grid_points)
    mirror = [(i, (i + cols // 2) % cols) for i in range(cols)]
    second, third, fourth = [lax.ppermute(part, "col", mirror) for part in turned[:3]]
    side = lax.ppermute(far, "col", [(i, i ^ 2) for i in range(cols)])

    x, xt, wt = own_ladder(tiles, count, tile_slot, xall, amp4, core)
    side, tail, wt = lax.optimization_barrier((side, turned[3], wt))
    fifth = lax.ppermute(tail, "col", mirror)
    twin = lax.ppermute(side, "col", [(i, i ^ 1) for i in range(cols)])
    wdt, part, down, along = own_cycle(tiles, count, occ_energy[0, 0], virt_energy[None, :], wall, far, side, twin, amp4)
    energies = (down, along)
    residual, updated = row(0, *energies, first, second, xt, x, coret, wt, wdt, amp4, part)
    fixed = (xt, x, coret)
    part, = piece(1, 0, 0, width, *energies, third, *fixed, wt, wdt, amp4, part, None, None)
    part, total = piece(1, 1, 0, split, *energies, fourth, *fixed, wt, wdt, amp4, part, None, None)
    residual, updated = piece(
        1, 1, split, width, *energies, fifth, *fixed, total, wdt, amp4, part, residual, updated
    )
    return residual.reshape(amps.shape), updated.reshape(amps.shape)


def solution(mesh):
    in_specs = (
        P("row", "col", None, None, None, None),
        P("row", None, None),
        P(),
        P("row", None, None, "col", None),
        P("row", "col", None),
        P("row", "col"),
        P(),
        P("row", "col", None, None),
        P(),
    )
    out_specs = (P("row", "col", None, None, None, None), P("row", "col", None, None, None, None))
    return jax.shard_map(
        per_device, mesh=mesh, in_specs=in_specs, out_specs=out_specs, check_vma=False
    )
```

```python
import functools

import jax
import jax.numpy as jnp
from jax import lax
from jax.experimental import pallas as pl
from jax.experimental.pallas import tpu as pltpu
from jax.sharding import PartitionSpec as P

MESH = pl.DeviceIdType.MESH
VMEM_LIMIT = 65300 * 1024
STRIP = 384


def dot(a, b):
    return jnp.dot(a, b, preferred_element_type=jnp.float32)


def tapered(width):
    return [pl.ds(0, width // 2), pl.ds(width // 2, width // 3), pl.ds(width // 2 + width // 3, width // 6)]


def strips(width, step):
    return [pl.ds(start, step) for start in range(0, width, step)]


def remote(src, dst, sems, index, device):
    return pltpu.make_async_remote_copy(
        src_ref=src, dst_ref=dst, send_sem=sems[0].at[index], recv_sem=sems[1].at[index],
        device_id=device, device_id_type=MESH,
    )


def greet(devices):
    barrier = pltpu.get_barrier_semaphore()
    for device in devices:
        pl.semaphore_signal(barrier, inc=1, device_id=device, device_id_type=MESH)
    pl.semaphore_wait(barrier, len(devices))


def gather_kernel(
    x_ref, w_ref, amps_ref, core_ref, xall_ref, wall_ref, far_ref, first_ref, coret_ref, *refs
):
    cuts, (plain, turned, fixed, wsend, wrecv, xsend, xrecv, msend, mrecv, local, tsem) = refs[:-11], refs[-11:]
    r = lax.axis_index("row")
    c = lax.axis_index("col")
    rows = lax.axis_size("row")
    cols = lax.axis_size("col")
    forth = (r, (c + 4) % cols)
    back = (r, (c + cols - 4) % cols)
    mirror = (r, (c + cols // 2) % cols)
    zside = (r, c + 2 - 4 * ((c // 2) % 2))
    twin = (r, c + 1 - 2 * (c % 2))
    beside = r + 1 - 2 * (r % 2)
    core = c % 2
    half = w_ref.shape[0] // 2
    width = plain.shape[1]
    y_steps = range(1, rows // 2)

    amps_in = [pltpu.make_async_copy(amps_ref.at[q], plain.at[q], tsem.at[q]) for q in range(4)]
    core_in = pltpu.make_async_copy(core_ref, fixed.at[0], tsem.at[4])
    for copy in amps_in + [core_in]:
        copy.start()
    greet(
        [forth, back, mirror, zside, twin, (beside, c)]
        + [((r + 2 * step) % rows, c) for step in y_steps]
    )
    wsems, xsems = (wsend, wrecv), (xsend, xrecv)
    started = []

    def send(*args):
        copy = remote(*args)
        copy.start()
        started.append(copy)

    def arrived(part, sems, index):
        remote(part, part, sems, index, twin).wait_recv()

    def shard(offset, plane, side):
        if offset in (1, 2) and plane + side == 0:
            return far_ref.at[offset - 1]
        x = (c // 4 + offset) % (cols // 4)
        z = (c // 2) % 2
        z = z + plane * (1 - 2 * z)
        k = core + side * (1 - 2 * core)
        return wall_ref.at[x * 4 + z * 2 + k]

    def to_twin(offset):
        x = (c // 4 + offset) % (cols // 4)
        send(shard(offset, 0, 0), wall_ref.at[x * 4 + c % 4], wsems, 6 + offset, twin)

    def transpose(q, p):
        amps_in[q].wait()
        for cut in strips(width, 256):
            turned[p, :, cut] = plain[q, cut, :].T

    own = wall_ref.at[c]
    send(w_ref, own, wsems, 0, forth)
    send(w_ref, far_ref.at[0], wsems, 1, back)
    send(x_ref.at[core], xall_ref.at[r, core], xsems, 0, (beside, c))
    send(w_ref, own, wsems, 4, zside)
    for step in y_steps:
        send(x_ref.at[core], xall_ref.at[r, core], xsems, step, ((r + 2 * step) % rows, c))
    send(w_ref, own, wsems, 6, twin)
    own_w = pltpu.make_async_copy(w_ref, own, local.at[0])
    own_x = pltpu.make_async_copy(x_ref, xall_ref.at[r], local.at[1])
    own_w.start()
    own_x.start()
    transpose(0, 0)

    def send_first(at):
        columns = pl.ds(at * (first_ref.shape[1] // 2), first_ref.shape[1] // 2)
        send(turned.at[0, :, columns], first_ref.at[:, columns], (msend, mrecv), at, mirror)

    send_first(0)

    part = xall_ref.at[beside, core]
    arrived(part, xsems, 0)
    for step in y_steps:
        send(part, part, xsems, 3 + step, ((r + 2 * step) % rows, c))
    send(part, part, xsems, 7, twin)

    part = shard(3, 0, 0)
    arrived(part, wsems, 0)
    send(part.at[:half], far_ref.at[1, :half], wsems, 2, forth)
    send(part, part, wsems, 5, zside)
    arrived(far_ref.at[0], wsems, 1)
    send(far_ref.at[0, half:], far_ref.at[1, half:], wsems, 3, back)
    send_first(1)
    to_twin(3)
    to_twin(1)
    transpose(2, 1)
    for step in y_steps:
        origin = (r + rows - 2 * step) % rows
        arrived(xall_ref.at[origin, core], xsems, step)
        send(xall_ref.at[origin, core], xall_ref.at[origin, core], xsems, 7 + step, twin)
    transpose(1, 2)
    part = shard(0, 1, 0)
    arrived(part, wsems, 4)
    send(part, part, wsems, 10, twin)
    for step in y_steps:
        origin = (r + rows - 2 * step) % rows
        origin = origin + 1 - 2 * (origin % 2)
        arrived(xall_ref.at[origin, core], xsems, 3 + step)
        send(xall_ref.at[origin, core], xall_ref.at[origin, core], xsems, 10 + step, twin)
    arrived(far_ref.at[1, :half], wsems, 2)
    arrived(far_ref.at[1, half:], wsems, 3)
    to_twin(2)
    transpose(3, 3)
    early, split = first_ref.shape[1], cuts[2].shape[1]
    moves = (
        (0, pl.ds(early, width - early), 0, pl.ds(0, width - early)),
        (1, pl.ds(0, width), 0, pl.ds(width - early, width)),
        (2, pl.ds(0, width), 1, pl.ds(0, width)),
        (3, pl.ds(0, split), 2, pl.ds(0, split)),
        (3, pl.ds(split, width - split), 3, pl.ds(0, width - split)),
    )
    outs = [
        pltpu.make_async_copy(turned.at[p, :, source], cuts[q].at[:, target], local.at[3 + at])
        for at, (p, source, q, target) in enumerate(moves)
    ]
    core_in.wait()
    for cut in strips(width, 256):
        fixed[1, :, cut] = fixed[0, cut, :].T
    outs.append(pltpu.make_async_copy(fixed.at[1], coret_ref, local.at[2]))
    for copy in outs:
        copy.start()
    part = shard(3, 1, 0)
    arrived(part, wsems, 5)
    send(part, part, wsems, 11, twin)

    for offset in range(4):
        arrived(shard(offset, 0, 1), wsems, 6 + offset)
    arrived(shard(0, 1, 1), wsems, 10)
    arrived(shard(3, 1, 1), wsems, 11)
    arrived(xall_ref.at[beside, 1 - core], xsems, 7)
    for step in y_steps:
        origin = (r + rows - 2 * step) % rows
        arrived(xall_ref.at[origin, 1 - core], xsems, 7 + step)
        origin = origin + 1 - 2 * (origin % 2)
        arrived(xall_ref.at[origin, 1 - core], xsems, 10 + step)
    for at in range(2):
        part = first_ref.at[:, pl.ds(at * (first_ref.shape[1] // 2), first_ref.shape[1] // 2)]
        arrived(part, (msend, mrecv), at)
    for copy in started:
        copy.wait_send()
    for copy in outs + [own_w, own_x]:
        copy.wait()


def gather_parts(x_factor, shard, amp4, core, early, split):
    rows = lax.axis_size("row")
    cols = lax.axis_size("col")
    width = amp4.shape[1]
    hbm = pl.BlockSpec(memory_space=pl.ANY)
    bf16 = jnp.bfloat16
    dma = pltpu.SemaphoreType.DMA
    shapes = [(rows,) + x_factor.shape, (cols,) + shard.shape, (2,) + shard.shape, (width, early), core.shape]
    shapes += [(width, 2 * width - early), (width, width)]
    shapes += [(width, split), (width, width - split)]
    return pl.pallas_call(
        gather_kernel,
        out_shape=[jax.ShapeDtypeStruct(shape, bf16) for shape in shapes],
        in_specs=[hbm] * 4,
        out_specs=[hbm] * len(shapes),
        scratch_shapes=[
            pltpu.VMEM(amp4.shape, bf16),
            pltpu.VMEM(amp4.shape, bf16),
            pltpu.VMEM((2,) + core.shape, bf16),
            dma((12,)),
            dma((12,)),
            dma((14,)),
            dma((14,)),
            dma((2,)),
            dma((2,)),
            dma((8,)),
            dma((5,)),
        ],
        compiler_params=pltpu.CompilerParams(
            collective_id=0, has_side_effects=True, vmem_limit_bytes=VMEM_LIMIT
        ),
        name="gather_parts",
    )(x_factor, shard, amp4, core)


def own_ladder_kernel(
    tiles_ref, count_ref, slot_ref, xall_ref, amps_ref, core_ref, x_ref, xt_ref, wt_ref, gathered, proj, sem
):
    @pl.when(pl.program_id(0) == 0)
    def _():
        tile = xall_ref.shape[1]
        copies = []
        for s in range(tiles_ref.shape[0]):
            copy = pltpu.make_async_copy(
                xall_ref.at[slot_ref[tiles_ref[s]]], gathered.at[pl.ds(s * tile, tile), :], sem.at[s]
            )
            copy.start()
            copies.append(copy)
        for copy in copies:
            copy.wait()
        live = lax.broadcasted_iota(jnp.int32, (x_ref.shape[0], 1), 0) < count_ref[0, 0] * tile
        x_ref[...] = jnp.where(live, gathered[...].astype(jnp.float32), 0.0).astype(x_ref.dtype)
        for cut in strips(x_ref.shape[0], 256):
            xt_ref[:, cut] = x_ref[cut, :].T

    proj[...] = dot(xt_ref[...], amps_ref[0]).astype(proj.dtype)
    inner = dot(proj[...], x_ref[...])
    wt_ref[0] = (core_ref[...].astype(jnp.float32) * inner).astype(wt_ref.dtype)


def own_ladder(tiles, count, tile_slot, xall, amp4, core):
    width = amp4.shape[1]
    points = core.shape[0]
    smem = pl.BlockSpec(memory_space=pltpu.SMEM)
    bf16 = jnp.bfloat16

    def whole(shape):
        return pl.BlockSpec(shape, lambda p: (0, 0))

    return pl.pallas_call(
        own_ladder_kernel,
        out_shape=(
            jax.ShapeDtypeStruct((width, points), bf16),
            jax.ShapeDtypeStruct((points, width), bf16),
            jax.ShapeDtypeStruct((4, points, points), bf16),
        ),
        grid=(4,),
        in_specs=[
            smem, smem, smem, pl.BlockSpec(memory_space=pl.ANY),
            pl.BlockSpec((1, width, width), lambda p: (p, 0, 0)), whole((points, points)),
        ],
        out_specs=(
            whole((width, points)), whole((points, width)),
            pl.BlockSpec((1, points, points), lambda p: (p, 0, 0)),
        ),
        scratch_shapes=[
            pltpu.VMEM((width, points), bf16),
            pltpu.VMEM((points, width), bf16),
            pltpu.SemaphoreType.DMA((tiles.shape[0],)),
        ],
        compiler_params=pltpu.CompilerParams(vmem_limit_bytes=VMEM_LIMIT),
        name="own_ladder",
    )(tiles, count, tile_slot, xall, amp4, core)


def window_index(tiles_ref, count_ref, tile, shape, axis):
    at = lax.broadcasted_iota(jnp.int32, shape, axis)
    index = jnp.full(shape, -1, jnp.int32)
    for s in range(tiles_ref.shape[0]):
        inside = (at >= s * tile) & (at < (s + 1) * tile) & (s < count_ref[0, 0])
        index = jnp.where(inside, at + (tiles_ref[s] - s) * tile, index)
    return index


def own_cycle_kernel(
    tiles_ref, count_ref, occ_ref, virt_ref, wall_ref, far_ref, side_ref, twin_ref, a0_ref, a1_ref,
    wdt_ref, cyc_ref, down_ref, along_ref, wsel, wd, pick, sem,
):
    p = pl.program_id(0)
    tile = wall_ref.shape[2]
    slots = tiles_ref.shape[0]
    width = wd.shape[1]
    window = virt_ref.shape[1]

    @pl.when(p == 0)
    def _():
        me = lax.axis_index("col")
        for first in range(2):
            for s in range(slots):
                number = tiles_ref[s]
                offset = ((number >> 2) + 4 - (me >> 2)) & 3
                plane = ((number >> 1) + (me >> 1)) & 1
                side = (number + me) & 1
                apart = (offset == 1) | (offset == 2)
                dst = wsel.at[pl.ds(2 * first, 2), pl.ds(s * tile, tile), :]

                def fetch(source, at, dst=dst, done=sem.at[first, s], first=first):
                    pltpu.make_async_copy(source.at[at, pl.ds(2 * first, 2)], dst, done).start()

                @pl.when(jnp.logical_not(apart) | ((plane == 0) & (side == 1)))
                def _(number=number, fetch=fetch):
                    fetch(wall_ref, number)

                for source, at_plane, at_side in ((far_ref, 0, 0), (side_ref, 1, 0), (twin_ref, 1, 1)):

                    @pl.when(apart & (plane == at_plane) & (side == at_side))
                    def _(source=source, offset=offset, fetch=fetch):
                        fetch(source, offset - 1)

        along = lax.broadcasted_iota(jnp.int32, pick.shape, 0)
        picked = window_index(tiles_ref, count_ref, tile, (1, width), 1)
        pick[...] = jnp.where(along == picked, 1.0, 0.0).astype(pick.dtype)
        picked = window_index(tiles_ref, count_ref, tile, (width, 1), 0)
        along = lax.broadcasted_iota(jnp.int32, (width, window), 1)
        levels = jnp.sum(jnp.where(along == picked, virt_ref[...], 0.0), axis=1, keepdims=True)
        lane = lax.broadcasted_iota(jnp.int32, (1, 128), 1)
        sums = jnp.zeros((1, 128), jnp.float32)
        for i in range(2):
            for j in range(2):
                sums = jnp.where(lane == 2 * i + j, occ_ref[0, i] + occ_ref[1, j], sums)
        live = jnp.where(picked >= 0, 1.0, 0.0)
        down_ref[...] = jnp.where(lane < 4, sums - levels, live)
        line = lax.broadcasted_iota(jnp.int32, (8, 1), 0)
        wide_levels = jnp.broadcast_to(levels, (width, 128)).T[:8, :]
        wide_live = jnp.broadcast_to(live, (width, 128)).T[:8, :]
        along_ref[...] = jnp.where(line == 0, wide_levels, wide_live)

    for first in range(2):

        @pl.when(p == 2 * first)
        def _(first=first):
            for s in range(slots):
                pltpu.make_async_copy(
                    wall_ref.at[0, pl.ds(0, 2)],
                    wsel.at[pl.ds(2 * first, 2), pl.ds(s * tile, tile), :],
                    sem.at[first, s],
                ).wait()
            for k in range(2):
                wd[k] = dot(wsel[2 * first + k], pick[...]).astype(wd.dtype)
                for cut in strips(width, 256):
                    wdt_ref[k, :, cut] = wd[k, cut, :].T

    cyc_ref[0] = (dot(wd[0], a0_ref[0]) + dot(wd[1], a1_ref[0])).astype(cyc_ref.dtype)


def own_cycle(tiles, count, occ, virt, wall, far, side, twin, amp4):
    width = amp4.shape[1]
    slots, window = tiles.shape[0], wall.shape[3]
    smem = pl.BlockSpec(memory_space=pltpu.SMEM)
    hbm = pl.BlockSpec(memory_space=pl.ANY)
    f32, bf16 = jnp.float32, jnp.bfloat16
    return pl.pallas_call(
        own_cycle_kernel,
        out_shape=(
            jax.ShapeDtypeStruct((4, width, width), bf16),
            jax.ShapeDtypeStruct((4, width, width), bf16),
            jax.ShapeDtypeStruct((width, 128), f32),
            jax.ShapeDtypeStruct((8, width), f32),
        ),
        grid=(4,),
        in_specs=[
            smem,
            smem,
            smem,
            pl.BlockSpec((1, window), lambda p: (0, 0)),
            hbm,
            hbm,
            hbm,
            hbm,
            pl.BlockSpec((1, width, width), lambda p: (p % 2, 0, 0)),
            pl.BlockSpec((1, width, width), lambda p: (2 + p % 2, 0, 0)),
        ],
        out_specs=(
            pl.BlockSpec((2, width, width), lambda p: (p // 2, 0, 0)),
            pl.BlockSpec((1, width, width), lambda p: (p, 0, 0)),
            pl.BlockSpec((width, 128), lambda p: (0, 0)),
            pl.BlockSpec((8, width), lambda p: (0, 0)),
        ),
        scratch_shapes=[
            pltpu.VMEM((4, width, window), bf16),
            pltpu.VMEM((2, width, width), bf16),
            pltpu.VMEM((window, width), bf16),
            pltpu.SemaphoreType.DMA((2, slots)),
        ],
        compiler_params=pltpu.CompilerParams(vmem_limit_bytes=VMEM_LIMIT),
        name="own_cycle",
    )(tiles, count, occ, virt, wall, far, side, twin, amp4, amp4)


class Mover:
    def __init__(self, plan, in_sem, out_sem):
        self.out_sem = out_sem
        self.outs = []
        self.loads = {}
        for at, (name, (src, dst)) in enumerate(plan.items()):
            self.loads[name] = pltpu.make_async_copy(src, dst, in_sem.at[at])
            self.loads[name].start()

    def need(self, *names):
        for name in names:
            if name in self.loads:
                self.loads.pop(name).wait()

    def put(self, src, dst):
        copy = pltpu.make_async_copy(src, dst, self.out_sem.at[len(self.outs)])
        copy.start()
        self.outs.append(copy)

    def drain(self):
        for copy in self.outs:
            copy.wait()


def emit(mover, pair, j, rows, raw, down, along, part, amps, res, upd, res_hbm, upd_hbm):
    mask = down[rows, 4:5] * along[1:2, :]
    raw = (raw + part[j, rows, :].astype(jnp.float32)) * mask
    own = amps[j, rows, :].astype(jnp.float32) * mask
    gap = down[rows, pair:pair + 1] - along[0:1, :]
    inverse = pl.reciprocal(gap, approx=True)
    inverse = inverse * (2.0 - gap * inverse)
    res[j, rows, :] = raw
    mover.put(res.at[j, rows, :], res_hbm.at[pair, rows, :])
    upd[j, rows, :] = (own + raw * inverse).astype(upd.dtype)
    mover.put(upd.at[j, rows, :], upd_hbm.at[pair, rows, :])


def emit_behind(products, emit_one):
    waiting = None
    for j, rows, product in products:
        raw = product()
        if waiting is not None:
            emit_one(*waiting)
        waiting = (j, rows, raw)
    emit_one(*waiting)


def row_kernel(
    i, down_hbm, along_hbm, b0_hbm, b1_hbm, xt_hbm, x_hbm, coret_hbm, wt_hbm, wdt_hbm,
    amps_hbm, part_hbm, res_hbm, upd_hbm, x, coret, wt, right, left, part, amps, proj, total, res, upd, down, along,
    sem, osem,
):
    width, points = x_hbm.shape
    early = b0_hbm.shape[1]
    head = pl.ds(0, points)
    blocks = [pl.ds(points + k * width, width) for k in range(2)]
    plan = {
        "b0": (b0_hbm, left.at[:, pl.ds(points, early)]),
        "b1": (b1_hbm, left.at[:, pl.ds(points + early, 2 * width - early)]),
        "xt0": (xt_hbm, right.at[0, head, :]),
        "x": (x_hbm, x),
        "wt": (wt_hbm.at[pl.ds(2 * i, 2)], wt),
        "coret": (coret_hbm, coret),
        "down": (down_hbm, down),
        "along": (along_hbm, along),
    }
    for j in range(2):
        for k in range(2):
            plan["w%d%d" % (j, k)] = (wdt_hbm.at[2 * j + k], right.at[j, blocks[k], :])
        plan["part%d" % j] = (part_hbm.at[2 * i + j], part.at[j])
        plan["amps%d" % j] = (amps_hbm.at[2 * i + j], amps.at[j])
        if j == 0:
            plan["xt1"] = (xt_hbm, right.at[1, head, :])
    mover = Mover(plan, sem, osem)
    for j in range(2):
        mover.need("b0", "b1", "xt0")
        proj[...] = dot(right[0, head, :], left[:, blocks[j]]).astype(proj.dtype)
        mover.need("x", "coret", "wt")
        inner = dot(proj[...], x[...])
        total[j] = (
            wt[j].astype(jnp.float32) + coret[...].astype(jnp.float32) * inner
        ).astype(total.dtype)
    def products():
        for j in range(2):
            for at, rows in enumerate(strips(width, STRIP)):

                def product(j=j, at=at, rows=rows):
                    if at == 0:
                        left[:, head] = dot(x[...], total[j]).astype(left.dtype)
                        mover.need("down", "along", "xt%d" % j, "w%d0" % j, "w%d1" % j, "part%d" % j, "amps%d" % j)
                    return dot(left[rows, :], right[j])

                yield j, rows, product

    def emit_one(j, rows, raw):
        emit(
            mover, 2 * i + j, j, rows, raw, down, along, part, amps, res, upd, res_hbm, upd_hbm,
        )

    emit_behind(products(), emit_one)
    mover.drain()


def row(i, down, along, b0, b1, xt, x, coret, wt, wdt, amp4, part):
    width, points = x.shape
    hbm = pl.BlockSpec(memory_space=pl.ANY)
    f32, bf16 = jnp.float32, jnp.bfloat16
    depth = points + 2 * width
    return pl.pallas_call(
        functools.partial(row_kernel, i),
        out_shape=[jax.ShapeDtypeStruct(part.shape, f32), jax.ShapeDtypeStruct(part.shape, bf16)],
        in_specs=[hbm] * 11,
        out_specs=[hbm] * 2,
        scratch_shapes=[
            pltpu.VMEM((points, width), bf16),
            pltpu.VMEM((points, points), bf16),
            pltpu.VMEM((2, points, points), bf16),
            pltpu.VMEM((2, depth, width), bf16),
            pltpu.VMEM((width, depth), bf16),
            pltpu.VMEM((2, width, width), bf16),
            pltpu.VMEM((2, width, width), bf16),
            pltpu.VMEM((points, width), bf16),
            pltpu.VMEM((2, points, points), bf16),
            pltpu.VMEM((2, width, width), f32),
            pltpu.VMEM((2, width, width), bf16),
            pltpu.VMEM((width, 128), f32),
            pltpu.VMEM((8, width), f32),
            pltpu.SemaphoreType.DMA((17,)),
            pltpu.SemaphoreType.DMA((4 * (width // STRIP),)),
        ],
        compiler_params=pltpu.CompilerParams(vmem_limit_bytes=VMEM_LIMIT),
        name="row_%d" % i,
    )(down, along, b0, b1, xt, x, coret, wt, wdt, amp4, part)


def piece_kernel(i, k, low, high, end, down_hbm, along_hbm, *refs):
    last = k == 1 and end
    scratch = 15
    refs, (x, coret, before, right, left, part, amps, proj, total, res, upd, down, along, sem, osem) = (
        refs[:-scratch], refs[-scratch:]
    )
    (b_hbm, xt_hbm, x_hbm, coret_hbm, before_hbm, wdt_hbm, amps_hbm, part_hbm) = refs[:8]
    outs = refs[8:]
    width, points = x_hbm.shape
    head, rest = pl.ds(0, points), pl.ds(points, high - low)
    cut = pl.ds(low, high - low)
    plan = {
        "b": (b_hbm, left.at[:, rest]),
        "xt": (xt_hbm, right.at[k, head, :]),
        "x": (x_hbm, x) if end else (x_hbm.at[cut], x.at[cut]),
        "coret": (coret_hbm, coret),
        "before": (before_hbm if low > 0 else before_hbm.at[2 * i + k], before),
    }
    if last:
        plan["down"] = (down_hbm, down)
        plan["along"] = (along_hbm, along)
    for j in (1 - k, k):
        plan["w%d" % j] = (wdt_hbm.at[2 * j + k, cut, :], right.at[j, rest, :])
        plan["part%d" % j] = (part_hbm.at[2 * i + j], part.at[j])
        if last:
            plan["amps%d" % j] = (amps_hbm.at[2 * i + j], amps.at[j])
    mover = Mover(plan, sem, osem)

    def products(plan):
        for j, columns in plan:
            for rows in tapered(width) if last and j == k else strips(width, STRIP):

                def product(j=j, columns=columns, rows=rows):
                    mover.need("down", "along", "w%d" % j, "part%d" % j, "amps%d" % j)
                    return dot(left[rows, columns], right[j, columns, :])

                yield j, rows, product

    def emit_one(j, rows, raw):
        if last:
            emit(
                mover, 2 * i + j, j, rows, raw, down, along, part, amps, res, upd, outs[-2], outs[-1],
            )
        else:
            part[j, rows, :] = (raw + part[j, rows, :].astype(jnp.float32)).astype(part.dtype)
            mover.put(part.at[j, rows, :], outs[0].at[2 * i + j, rows, :])

    mover.need("b", "xt")
    proj[...] = dot(right[k, head, :], left[:, rest]).astype(proj.dtype)
    mover.need("x")
    inner = dot(proj[...], x[cut, :])
    mover.need("coret", "before")
    total[...] = (
        before[...].astype(jnp.float32) + coret[...].astype(jnp.float32) * inner
    ).astype(total.dtype)
    if end:
        left[:, head] = dot(x[...], total[...]).astype(left.dtype)
        emit_behind(products([(1 - k, rest), (k, pl.ds(0, points + high - low))]), emit_one)
    else:
        mover.put(total, outs[1])
        emit_behind(products([(1 - k, rest), (k, rest)]), emit_one)
    mover.drain()


def piece(i, k, low, high, down, along, b, xt, x, coret, before, wdt, amp4, part, residual, updated):
    width, points = x.shape
    end = high == width
    last = k == 1 and end
    hbm = pl.BlockSpec(memory_space=pl.ANY)
    f32, bf16 = jnp.float32, jnp.bfloat16
    operands = [down, along, b, xt, x, coret, before, wdt, amp4, part]
    if last:
        out_shape = [jax.ShapeDtypeStruct(part.shape, f32), jax.ShapeDtypeStruct(part.shape, bf16)]
        alias = {len(operands): 0, len(operands) + 1: 1}
        operands += [residual, updated]
    else:
        out_shape = [jax.ShapeDtypeStruct(part.shape, bf16)]
        alias = {len(operands) - 1: 0}
        if not end:
            out_shape.append(jax.ShapeDtypeStruct((points, points), bf16))
    return pl.pallas_call(
        functools.partial(piece_kernel, i, k, low, high, end),
        out_shape=out_shape,
        in_specs=[hbm] * len(operands),
        out_specs=[hbm] * len(out_shape),
        scratch_shapes=[
            pltpu.VMEM((points, width), bf16),
            pltpu.VMEM((points, points), bf16),
            pltpu.VMEM((points, points), bf16),
            pltpu.VMEM((2, points + high - low, width), bf16),
            pltpu.VMEM((width, points + high - low), bf16),
            pltpu.VMEM((2, width, width), bf16),
            pltpu.VMEM((2, width, width), bf16),
            pltpu.VMEM((points, high - low), bf16),
            pltpu.VMEM((points, points), bf16),
            pltpu.VMEM((2, width, width), f32),
            pltpu.VMEM((2, width, width), bf16),
            pltpu.VMEM((width, 128), f32),
            pltpu.VMEM((8, width), f32),
            pltpu.SemaphoreType.DMA((13,)),
            pltpu.SemaphoreType.DMA((10,)),
        ],
        input_output_aliases=alias,
        compiler_params=pltpu.CompilerParams(vmem_limit_bytes=VMEM_LIMIT),
        name="piece_%d%d_%d" % (i, k, low),
    )(*operands)


def per_device(
    amps, x_factor, core, cycle_w, domain_tiles, domain_count, tile_slot, occ_energy, virt_energy
):
    occ = amps.shape[2]
    width = amps.shape[4]
    tile_width = x_factor.shape[1]
    grid_points = x_factor.shape[2]
    window = cycle_w.shape[4]
    cols = lax.axis_size("col")
    amp4 = amps[0, 0].reshape(occ * occ, width, width)
    shard = cycle_w[0].reshape(occ * occ, tile_width, window)

    early, split = 256, 512
    tiles, count = domain_tiles[0, 0], domain_count
    xall, wall, far, first, coret, *turned = gather_parts(x_factor, shard, amp4, core, early, split)
    xall = xall.reshape(-1, tile_width, grid_points)
    mirror = [(i, (i + cols // 2) % cols) for i in range(cols)]
    second, third, fourth = [lax.ppermute(part, "col", mirror) for part in turned[:3]]
    side = lax.ppermute(far, "col", [(i, i ^ 2) for i in range(cols)])

    x, xt, wt = own_ladder(tiles, count, tile_slot, xall, amp4, core)
    side, tail, wt = lax.optimization_barrier((side, turned[3], wt))
    fifth = lax.ppermute(tail, "col", mirror)
    twin = lax.ppermute(side, "col", [(i, i ^ 1) for i in range(cols)])
    wdt, part, down, along = own_cycle(tiles, count, occ_energy[0, 0], virt_energy[None, :], wall, far, side, twin, amp4)
    energies = (down, along)
    residual, updated = row(0, *energies, first, second, xt, x, coret, wt, wdt, amp4, part)
    fixed = (xt, x, coret)
    part, = piece(1, 0, 0, width, *energies, third, *fixed, wt, wdt, amp4, part, None, None)
    part, total = piece(1, 1, 0, split, *energies, fourth, *fixed, wt, wdt, amp4, part, None, None)
    residual, updated = piece(
        1, 1, split, width, *energies, fifth, *fixed, total, wdt, amp4, part, residual, updated
    )
    return residual.reshape(amps.shape), updated.reshape(amps.shape)


def solution(mesh):
    in_specs = (
        P("row", "col", None, None, None, None),
        P("row", None, None),
        P(),
        P("row", None, None, "col", None),
        P("row", "col", None),
        P("row", "col"),
        P(),
        P("row", "col", None, None),
        P(),
    )
    out_specs = (P("row", "col", None, None, None, None), P("row", "col", None, None, None, None))
    return jax.shard_map(
        per_device, mesh=mesh, in_specs=in_specs, out_specs=out_specs, check_vma=False
    )
```

```python
import functools

import jax
import jax.numpy as jnp
from jax import lax
from jax.experimental import pallas as pl
from jax.experimental.pallas import tpu as pltpu
from jax.sharding import PartitionSpec as P

MESH = pl.DeviceIdType.MESH
VMEM_LIMIT = 65300 * 1024
STRIP = 384


def dot(a, b):
    return jnp.dot(a, b, preferred_element_type=jnp.float32)


def tapered(width):
    return [pl.ds(0, width // 2), pl.ds(width // 2, width // 3), pl.ds(width // 2 + width // 3, width // 6)]


def strips(width, step):
    return [pl.ds(start, step) for start in range(0, width, step)]


def remote(src, dst, sems, index, device):
    return pltpu.make_async_remote_copy(
        src_ref=src, dst_ref=dst, send_sem=sems[0].at[index], recv_sem=sems[1].at[index],
        device_id=device, device_id_type=MESH,
    )


def greet(devices):
    barrier = pltpu.get_barrier_semaphore()
    for device in devices:
        pl.semaphore_signal(barrier, inc=1, device_id=device, device_id_type=MESH)
    pl.semaphore_wait(barrier, len(devices))


def gather_kernel(
    x_ref, w_ref, amps_ref, core_ref, xall_ref, wall_ref, far_ref, first_ref, coret_ref, *refs
):
    cuts, (plain, turned, fixed, wsend, wrecv, xsend, xrecv, msend, mrecv, local, tsem) = refs[:-11], refs[-11:]
    r = lax.axis_index("row")
    c = lax.axis_index("col")
    rows = lax.axis_size("row")
    cols = lax.axis_size("col")
    forth = (r, (c + 4) % cols)
    back = (r, (c + cols - 4) % cols)
    mirror = (r, (c + cols // 2) % cols)
    zside = (r, c + 2 - 4 * ((c // 2) % 2))
    twin = (r, c + 1 - 2 * (c % 2))
    beside = r + 1 - 2 * (r % 2)
    core = c % 2
    half = w_ref.shape[0] // 2
    width = plain.shape[1]
    y_steps = range(1, rows // 2)

    amps_in = [pltpu.make_async_copy(amps_ref.at[q], plain.at[q], tsem.at[q]) for q in range(4)]
    core_in = pltpu.make_async_copy(core_ref, fixed.at[0], tsem.at[4])
    for copy in amps_in + [core_in]:
        copy.start()
    greet(
        [forth, back, mirror, zside, twin, (beside, c)]
        + [((r + 2 * step) % rows, c) for step in y_steps]
    )
    wsems, xsems = (wsend, wrecv), (xsend, xrecv)
    started = []

    def send(*args):
        copy = remote(*args)
        copy.start()
        started.append(copy)

    def arrived(part, sems, index):
        remote(part, part, sems, index, twin).wait_recv()

    def shard(offset, plane, side):
        if offset in (1, 2) and plane + side == 0:
            return far_ref.at[offset - 1]
        x = (c // 4 + offset) % (cols // 4)
        z = (c // 2) % 2
        z = z + plane * (1 - 2 * z)
        k = core + side * (1 - 2 * core)
        return wall_ref.at[x * 4 + z * 2 + k]

    def to_twin(offset):
        x = (c // 4 + offset) % (cols // 4)
        send(shard(offset, 0, 0), wall_ref.at[x * 4 + c % 4], wsems, 6 + offset, twin)

    def transpose(q, p):
        amps_in[q].wait()
        for cut in strips(width, 256):
            turned[p, :, cut] = plain[q, cut, :].T

    own = wall_ref.at[c]
    send(w_ref, own, wsems, 0, forth)
    send(w_ref, far_ref.at[0], wsems, 1, back)
    send(x_ref.at[core], xall_ref.at[r, core], xsems, 0, (beside, c))
    send(w_ref, own, wsems, 4, zside)
    for step in y_steps:
        send(x_ref.at[core], xall_ref.at[r, core], xsems, step, ((r + 2 * step) % rows, c))
    send(w_ref, own, wsems, 6, twin)
    own_w = pltpu.make_async_copy(w_ref, own, local.at[0])
    own_x = pltpu.make_async_copy(x_ref, xall_ref.at[r], local.at[1])
    own_w.start()
    own_x.start()
    transpose(0, 0)

    chunks = first_ref.shape[1] // 128

    def send_first(at):
        columns = pl.ds(at * 128, 128)
        send(turned.at[0, :, columns], first_ref.at[:, columns], (msend, mrecv), at, mirror)

    send_first(0)

    part = xall_ref.at[beside, core]
    arrived(part, xsems, 0)
    for step in y_steps:
        send(part, part, xsems, 3 + step, ((r + 2 * step) % rows, c))
    send(part, part, xsems, 7, twin)

    part = shard(3, 0, 0)
    arrived(part, wsems, 0)
    send(part.at[:half], far_ref.at[1, :half], wsems, 2, forth)
    send(part, part, wsems, 5, zside)
    arrived(far_ref.at[0], wsems, 1)
    send(far_ref.at[0, half:], far_ref.at[1, half:], wsems, 3, back)
    for at in range(1, chunks):
        send_first(at)
    to_twin(3)
    to_twin(1)
    transpose(2, 1)
    for step in y_steps:
        origin = (r + rows - 2 * step) % rows
        arrived(xall_ref.at[origin, core], xsems, step)
        send(xall_ref.at[origin, core], xall_ref.at[origin, core], xsems, 7 + step, twin)
    transpose(1, 2)
    part = shard(0, 1, 0)
    arrived(part, wsems, 4)
    send(part, part, wsems, 10, twin)
    for step in y_steps:
        origin = (r + rows - 2 * step) % rows
        origin = origin + 1 - 2 * (origin % 2)
        arrived(xall_ref.at[origin, core], xsems, 3 + step)
        send(xall_ref.at[origin, core], xall_ref.at[origin, core], xsems, 10 + step, twin)
    arrived(far_ref.at[1, :half], wsems, 2)
    arrived(far_ref.at[1, half:], wsems, 3)
    to_twin(2)
    transpose(3, 3)
    early, split = first_ref.shape[1], cuts[2].shape[1]
    moves = (
        (0, pl.ds(early, width - early), 0, pl.ds(0, width - early)),
        (1, pl.ds(0, width), 0, pl.ds(width - early, width)),
        (2, pl.ds(0, width), 1, pl.ds(0, width)),
        (3, pl.ds(0, split), 2, pl.ds(0, split)),
        (3, pl.ds(split, width - split), 3, pl.ds(0, width - split)),
    )
    outs = [
        pltpu.make_async_copy(turned.at[p, :, source], cuts[q].at[:, target], local.at[3 + at])
        for at, (p, source, q, target) in enumerate(moves)
    ]
    core_in.wait()
    for cut in strips(width, 256):
        fixed[1, :, cut] = fixed[0, cut, :].T
    outs.append(pltpu.make_async_copy(fixed.at[1], coret_ref, local.at[2]))
    for copy in outs:
        copy.start()
    part = shard(3, 1, 0)
    arrived(part, wsems, 5)
    send(part, part, wsems, 11, twin)

    for offset in range(4):
        arrived(shard(offset, 0, 1), wsems, 6 + offset)
    arrived(shard(0, 1, 1), wsems, 10)
    arrived(shard(3, 1, 1), wsems, 11)
    arrived(xall_ref.at[beside, 1 - core], xsems, 7)
    for step in y_steps:
        origin = (r + rows - 2 * step) % rows
        arrived(xall_ref.at[origin, 1 - core], xsems, 7 + step)
        origin = origin + 1 - 2 * (origin % 2)
        arrived(xall_ref.at[origin, 1 - core], xsems, 10 + step)
    for at in range(chunks):
        arrived(first_ref.at[:, pl.ds(at * 128, 128)], (msend, mrecv), at)
    for copy in started:
        copy.wait_send()
    for copy in outs + [own_w, own_x]:
        copy.wait()


def gather_parts(x_factor, shard, amp4, core, early, split):
    rows = lax.axis_size("row")
    cols = lax.axis_size("col")
    width = amp4.shape[1]
    hbm = pl.BlockSpec(memory_space=pl.ANY)
    bf16 = jnp.bfloat16
    dma = pltpu.SemaphoreType.DMA
    shapes = [(rows,) + x_factor.shape, (cols,) + shard.shape, (2,) + shard.shape, (width, early), core.shape]
    shapes += [(width, 2 * width - early), (width, width)]
    shapes += [(width, split), (width, width - split)]
    return pl.pallas_call(
        gather_kernel,
        out_shape=[jax.ShapeDtypeStruct(shape, bf16) for shape in shapes],
        in_specs=[hbm] * 4,
        out_specs=[hbm] * len(shapes),
        scratch_shapes=[
            pltpu.VMEM(amp4.shape, bf16),
            pltpu.VMEM(amp4.shape, bf16),
            pltpu.VMEM((2,) + core.shape, bf16),
            dma((12,)),
            dma((12,)),
            dma((14,)),
            dma((14,)),
            dma((early // 128,)),
            dma((early // 128,)),
            dma((8,)),
            dma((5,)),
        ],
        compiler_params=pltpu.CompilerParams(
            collective_id=0, has_side_effects=True, vmem_limit_bytes=VMEM_LIMIT
        ),
        name="gather_parts",
    )(x_factor, shard, amp4, core)


def own_ladder_kernel(
    tiles_ref, count_ref, slot_ref, xall_ref, amps_ref, core_ref, x_ref, xt_ref, wt_ref, gathered, proj, sem
):
    @pl.when(pl.program_id(0) == 0)
    def _():
        tile = xall_ref.shape[1]
        copies = []
        for s in range(tiles_ref.shape[0]):
            copy = pltpu.make_async_copy(
                xall_ref.at[slot_ref[tiles_ref[s]]], gathered.at[pl.ds(s * tile, tile), :], sem.at[s]
            )
            copy.start()
            copies.append(copy)
        for copy in copies:
            copy.wait()
        live = lax.broadcasted_iota(jnp.int32, (x_ref.shape[0], 1), 0) < count_ref[0, 0] * tile
        x_ref[...] = jnp.where(live, gathered[...].astype(jnp.float32), 0.0).astype(x_ref.dtype)
        for cut in strips(x_ref.shape[0], 256):
            xt_ref[:, cut] = x_ref[cut, :].T

    proj[...] = dot(xt_ref[...], amps_ref[0]).astype(proj.dtype)
    inner = dot(proj[...], x_ref[...])
    wt_ref[0] = (core_ref[...].astype(jnp.float32) * inner).astype(wt_ref.dtype)


def own_ladder(tiles, count, tile_slot, xall, amp4, core):
    width = amp4.shape[1]
    points = core.shape[0]
    smem = pl.BlockSpec(memory_space=pltpu.SMEM)
    bf16 = jnp.bfloat16

    def whole(shape):
        return pl.BlockSpec(shape, lambda p: (0, 0))

    return pl.pallas_call(
        own_ladder_kernel,
        out_shape=(
            jax.ShapeDtypeStruct((width, points), bf16),
            jax.ShapeDtypeStruct((points, width), bf16),
            jax.ShapeDtypeStruct((4, points, points), bf16),
        ),
        grid=(4,),
        in_specs=[
            smem, smem, smem, pl.BlockSpec(memory_space=pl.ANY),
            pl.BlockSpec((1, width, width), lambda p: (p, 0, 0)), whole((points, points)),
        ],
        out_specs=(
            whole((width, points)), whole((points, width)),
            pl.BlockSpec((1, points, points), lambda p: (p, 0, 0)),
        ),
        scratch_shapes=[
            pltpu.VMEM((width, points), bf16),
            pltpu.VMEM((points, width), bf16),
            pltpu.SemaphoreType.DMA((tiles.shape[0],)),
        ],
        compiler_params=pltpu.CompilerParams(vmem_limit_bytes=VMEM_LIMIT),
        name="own_ladder",
    )(tiles, count, tile_slot, xall, amp4, core)


def window_index(tiles_ref, count_ref, tile, shape, axis):
    at = lax.broadcasted_iota(jnp.int32, shape, axis)
    index = jnp.full(shape, -1, jnp.int32)
    for s in range(tiles_ref.shape[0]):
        inside = (at >= s * tile) & (at < (s + 1) * tile) & (s < count_ref[0, 0])
        index = jnp.where(inside, at + (tiles_ref[s] - s) * tile, index)
    return index


def own_cycle_kernel(
    tiles_ref, count_ref, occ_ref, virt_ref, wall_ref, far_ref, side_ref, twin_ref, a0_ref, a1_ref,
    wdt_ref, cyc_ref, down_ref, along_ref, wsel, wd, pick, sem,
):
    p = pl.program_id(0)
    tile = wall_ref.shape[2]
    slots = tiles_ref.shape[0]
    width = wd.shape[1]
    window = virt_ref.shape[1]

    @pl.when(p == 0)
    def _():
        me = lax.axis_index("col")
        for first in range(2):
            for s in range(slots):
                number = tiles_ref[s]
                offset = ((number >> 2) + 4 - (me >> 2)) & 3
                plane = ((number >> 1) + (me >> 1)) & 1
                side = (number + me) & 1
                apart = (offset == 1) | (offset == 2)
                dst = wsel.at[pl.ds(2 * first, 2), pl.ds(s * tile, tile), :]

                def fetch(source, at, dst=dst, done=sem.at[first, s], first=first):
                    pltpu.make_async_copy(source.at[at, pl.ds(2 * first, 2)], dst, done).start()

                @pl.when(jnp.logical_not(apart) | ((plane == 0) & (side == 1)))
                def _(number=number, fetch=fetch):
                    fetch(wall_ref, number)

                for source, at_plane, at_side in ((far_ref, 0, 0), (side_ref, 1, 0), (twin_ref, 1, 1)):

                    @pl.when(apart & (plane == at_plane) & (side == at_side))
                    def _(source=source, offset=offset, fetch=fetch):
                        fetch(source, offset - 1)

        along = lax.broadcasted_iota(jnp.int32, pick.shape, 0)
        picked = window_index(tiles_ref, count_ref, tile, (1, width), 1)
        pick[...] = jnp.where(along == picked, 1.0, 0.0).astype(pick.dtype)
        picked = window_index(tiles_ref, count_ref, tile, (width, 1), 0)
        along = lax.broadcasted_iota(jnp.int32, (width, window), 1)
        levels = jnp.sum(jnp.where(along == picked, virt_ref[...], 0.0), axis=1, keepdims=True)
        lane = lax.broadcasted_iota(jnp.int32, (1, 128), 1)
        sums = jnp.zeros((1, 128), jnp.float32)
        for i in range(2):
            for j in range(2):
                sums = jnp.where(lane == 2 * i + j, occ_ref[0, i] + occ_ref[1, j], sums)
        live = jnp.where(picked >= 0, 1.0, 0.0)
        down_ref[...] = jnp.where(lane < 4, sums - levels, live)
        line = lax.broadcasted_iota(jnp.int32, (8, 1), 0)
        wide_levels = jnp.broadcast_to(levels, (width, 128)).T[:8, :]
        wide_live = jnp.broadcast_to(live, (width, 128)).T[:8, :]
        along_ref[...] = jnp.where(line == 0, wide_levels, wide_live)

    for first in range(2):

        @pl.when(p == 2 * first)
        def _(first=first):
            for s in range(slots):
                pltpu.make_async_copy(
                    wall_ref.at[0, pl.ds(0, 2)],
                    wsel.at[pl.ds(2 * first, 2), pl.ds(s * tile, tile), :],
                    sem.at[first, s],
                ).wait()
            for k in range(2):
                wd[k] = dot(wsel[2 * first + k], pick[...]).astype(wd.dtype)
                for cut in strips(width, 256):
                    wdt_ref[k, :, cut] = wd[k, cut, :].T

    cyc_ref[0] = (dot(wd[0], a0_ref[0]) + dot(wd[1], a1_ref[0])).astype(cyc_ref.dtype)


def own_cycle(tiles, count, occ, virt, wall, far, side, twin, amp4):
    width = amp4.shape[1]
    slots, window = tiles.shape[0], wall.shape[3]
    smem = pl.BlockSpec(memory_space=pltpu.SMEM)
    hbm = pl.BlockSpec(memory_space=pl.ANY)
    f32, bf16 = jnp.float32, jnp.bfloat16
    return pl.pallas_call(
        own_cycle_kernel,
        out_shape=(
            jax.ShapeDtypeStruct((4, width, width), bf16),
            jax.ShapeDtypeStruct((4, width, width), bf16),
            jax.ShapeDtypeStruct((width, 128), f32),
            jax.ShapeDtypeStruct((8, width), f32),
        ),
        grid=(4,),
        in_specs=[
            smem,
            smem,
            smem,
            pl.BlockSpec((1, window), lambda p: (0, 0)),
            hbm,
            hbm,
            hbm,
            hbm,
            pl.BlockSpec((1, width, width), lambda p: (p % 2, 0, 0)),
            pl.BlockSpec((1, width, width), lambda p: (2 + p % 2, 0, 0)),
        ],
        out_specs=(
            pl.BlockSpec((2, width, width), lambda p: (p // 2, 0, 0)),
            pl.BlockSpec((1, width, width), lambda p: (p, 0, 0)),
            pl.BlockSpec((width, 128), lambda p: (0, 0)),
            pl.BlockSpec((8, width), lambda p: (0, 0)),
        ),
        scratch_shapes=[
            pltpu.VMEM((4, width, window), bf16),
            pltpu.VMEM((2, width, width), bf16),
            pltpu.VMEM((window, width), bf16),
            pltpu.SemaphoreType.DMA((2, slots)),
        ],
        compiler_params=pltpu.CompilerParams(vmem_limit_bytes=VMEM_LIMIT),
        name="own_cycle",
    )(tiles, count, occ, virt, wall, far, side, twin, amp4, amp4)


class Mover:
    def __init__(self, plan, in_sem, out_sem):
        self.out_sem = out_sem
        self.outs = []
        self.loads = {}
        for at, (name, (src, dst)) in enumerate(plan.items()):
            self.loads[name] = pltpu.make_async_copy(src, dst, in_sem.at[at])
            self.loads[name].start()

    def need(self, *names):
        for name in names:
            if name in self.loads:
                self.loads.pop(name).wait()

    def put(self, src, dst):
        copy = pltpu.make_async_copy(src, dst, self.out_sem.at[len(self.outs)])
        copy.start()
        self.outs.append(copy)

    def drain(self):
        for copy in self.outs:
            copy.wait()


def emit(mover, pair, j, rows, raw, down, along, part, amps, res, upd, res_hbm, upd_hbm):
    mask = down[rows, 4:5] * along[1:2, :]
    raw = (raw + part[j, rows, :].astype(jnp.float32)) * mask
    own = amps[j, rows, :].astype(jnp.float32) * mask
    gap = down[rows, pair:pair + 1] - along[0:1, :]
    inverse = pl.reciprocal(gap, approx=True)
    inverse = inverse * (2.0 - gap * inverse)
    res[j, rows, :] = raw
    mover.put(res.at[j, rows, :], res_hbm.at[pair, rows, :])
    upd[j, rows, :] = (own + raw * inverse).astype(upd.dtype)
    mover.put(upd.at[j, rows, :], upd_hbm.at[pair, rows, :])


def emit_behind(products, emit_one):
    waiting = None
    for j, rows, product in products:
        raw = product()
        if waiting is not None:
            emit_one(*waiting)
        waiting = (j, rows, raw)
    emit_one(*waiting)


def row_kernel(
    i, down_hbm, along_hbm, b0_hbm, b1_hbm, xt_hbm, x_hbm, coret_hbm, wt_hbm, wdt_hbm,
    amps_hbm, part_hbm, res_hbm, upd_hbm, x, coret, wt, right, left, part, amps, proj, total, res, upd, down, along,
    sem, osem,
):
    width, points = x_hbm.shape
    early = b0_hbm.shape[1]
    head = pl.ds(0, points)
    blocks = [pl.ds(points + k * width, width) for k in range(2)]
    plan = {
        "b0": (b0_hbm, left.at[:, pl.ds(points, early)]),
        "b1": (b1_hbm, left.at[:, pl.ds(points + early, 2 * width - early)]),
        "xt0": (xt_hbm, right.at[0, head, :]),
        "x": (x_hbm, x),
        "wt": (wt_hbm.at[pl.ds(2 * i, 2)], wt),
        "coret": (coret_hbm, coret),
        "down": (down_hbm, down),
        "along": (along_hbm, along),
    }
    for j in range(2):
        for k in range(2):
            plan["w%d%d" % (j, k)] = (wdt_hbm.at[2 * j + k], right.at[j, blocks[k], :])
        plan["part%d" % j] = (part_hbm.at[2 * i + j], part.at[j])
        plan["amps%d" % j] = (amps_hbm.at[2 * i + j], amps.at[j])
        if j == 0:
            plan["xt1"] = (xt_hbm, right.at[1, head, :])
    mover = Mover(plan, sem, osem)
    for j in range(2):
        mover.need("b0", "b1", "xt0")
        proj[...] = dot(right[0, head, :], left[:, blocks[j]]).astype(proj.dtype)
        mover.need("x", "coret", "wt")
        inner = dot(proj[...], x[...])
        total[j] = (
            wt[j].astype(jnp.float32) + coret[...].astype(jnp.float32) * inner
        ).astype(total.dtype)
    def products():
        for j in range(2):
            for at, rows in enumerate(strips(width, STRIP)):

                def product(j=j, at=at, rows=rows):
                    if at == 0:
                        left[:, head] = dot(x[...], total[j]).astype(left.dtype)
                        mover.need("down", "along", "xt%d" % j, "w%d0" % j, "w%d1" % j, "part%d" % j, "amps%d" % j)
                    return dot(left[rows, :], right[j])

                yield j, rows, product

    def emit_one(j, rows, raw):
        emit(
            mover, 2 * i + j, j, rows, raw, down, along, part, amps, res, upd, res_hbm, upd_hbm,
        )

    emit_behind(products(), emit_one)
    mover.drain()


def row(i, down, along, b0, b1, xt, x, coret, wt, wdt, amp4, part):
    width, points = x.shape
    hbm = pl.BlockSpec(memory_space=pl.ANY)
    f32, bf16 = jnp.float32, jnp.bfloat16
    depth = points + 2 * width
    return pl.pallas_call(
        functools.partial(row_kernel, i),
        out_shape=[jax.ShapeDtypeStruct(part.shape, f32), jax.ShapeDtypeStruct(part.shape, bf16)],
        in_specs=[hbm] * 11,
        out_specs=[hbm] * 2,
        scratch_shapes=[
            pltpu.VMEM((points, width), bf16),
            pltpu.VMEM((points, points), bf16),
            pltpu.VMEM((2, points, points), bf16),
            pltpu.VMEM((2, depth, width), bf16),
            pltpu.VMEM((width, depth), bf16),
            pltpu.VMEM((2, width, width), bf16),
            pltpu.VMEM((2, width, width), bf16),
            pltpu.VMEM((points, width), bf16),
            pltpu.VMEM((2, points, points), bf16),
            pltpu.VMEM((2, width, width), f32),
            pltpu.VMEM((2, width, width), bf16),
            pltpu.VMEM((width, 128), f32),
            pltpu.VMEM((8, width), f32),
            pltpu.SemaphoreType.DMA((17,)),
            pltpu.SemaphoreType.DMA((4 * (width // STRIP),)),
        ],
        compiler_params=pltpu.CompilerParams(vmem_limit_bytes=VMEM_LIMIT),
        name="row_%d" % i,
    )(down, along, b0, b1, xt, x, coret, wt, wdt, amp4, part)


def piece_kernel(i, k, low, high, end, down_hbm, along_hbm, *refs):
    last = k == 1 and end
    scratch = 15
    refs, (x, coret, before, right, left, part, amps, proj, total, res, upd, down, along, sem, osem) = (
        refs[:-scratch], refs[-scratch:]
    )
    (b_hbm, xt_hbm, x_hbm, coret_hbm, before_hbm, wdt_hbm, amps_hbm, part_hbm) = refs[:8]
    outs = refs[8:]
    width, points = x_hbm.shape
    head, rest = pl.ds(0, points), pl.ds(points, high - low)
    cut = pl.ds(low, high - low)
    plan = {
        "b": (b_hbm, left.at[:, rest]),
        "xt": (xt_hbm, right.at[k, head, :]),
        "x": (x_hbm, x) if end else (x_hbm.at[cut], x.at[cut]),
        "coret": (coret_hbm, coret),
        "before": (before_hbm if low > 0 else before_hbm.at[2 * i + k], before),
    }
    if last:
        plan["down"] = (down_hbm, down)
        plan["along"] = (along_hbm, along)
    for j in (1 - k, k):
        plan["w%d" % j] = (wdt_hbm.at[2 * j + k, cut, :], right.at[j, rest, :])
        plan["part%d" % j] = (part_hbm.at[2 * i + j], part.at[j])
        if last:
            plan["amps%d" % j] = (amps_hbm.at[2 * i + j], amps.at[j])
    mover = Mover(plan, sem, osem)

    def products(plan):
        for j, columns in plan:
            for rows in tapered(width) if last and j == k else strips(width, STRIP):

                def product(j=j, columns=columns, rows=rows):
                    mover.need("down", "along", "w%d" % j, "part%d" % j, "amps%d" % j)
                    return dot(left[rows, columns], right[j, columns, :])

                yield j, rows, product

    def emit_one(j, rows, raw):
        if last:
            emit(
                mover, 2 * i + j, j, rows, raw, down, along, part, amps, res, upd, outs[-2], outs[-1],
            )
        else:
            part[j, rows, :] = (raw + part[j, rows, :].astype(jnp.float32)).astype(part.dtype)
            mover.put(part.at[j, rows, :], outs[0].at[2 * i + j, rows, :])

    mover.need("b", "xt")
    proj[...] = dot(right[k, head, :], left[:, rest]).astype(proj.dtype)
    mover.need("x")
    inner = dot(proj[...], x[cut, :])
    mover.need("coret", "before")
    total[...] = (
        before[...].astype(jnp.float32) + coret[...].astype(jnp.float32) * inner
    ).astype(total.dtype)
    if end:
        left[:, head] = dot(x[...], total[...]).astype(left.dtype)
        emit_behind(products([(1 - k, rest), (k, pl.ds(0, points + high - low))]), emit_one)
    else:
        mover.put(total, outs[1])
        emit_behind(products([(1 - k, rest), (k, rest)]), emit_one)
    mover.drain()


def piece(i, k, low, high, down, along, b, xt, x, coret, before, wdt, amp4, part, residual, updated):
    width, points = x.shape
    end = high == width
    last = k == 1 and end
    hbm = pl.BlockSpec(memory_space=pl.ANY)
    f32, bf16 = jnp.float32, jnp.bfloat16
    operands = [down, along, b, xt, x, coret, before, wdt, amp4, part]
    if last:
        out_shape = [jax.ShapeDtypeStruct(part.shape, f32), jax.ShapeDtypeStruct(part.shape, bf16)]
        alias = {len(operands): 0, len(operands) + 1: 1}
        operands += [residual, updated]
    else:
        out_shape = [jax.ShapeDtypeStruct(part.shape, bf16)]
        alias = {len(operands) - 1: 0}
        if not end:
            out_shape.append(jax.ShapeDtypeStruct((points, points), bf16))
    return pl.pallas_call(
        functools.partial(piece_kernel, i, k, low, high, end),
        out_shape=out_shape,
        in_specs=[hbm] * len(operands),
        out_specs=[hbm] * len(out_shape),
        scratch_shapes=[
            pltpu.VMEM((points, width), bf16),
            pltpu.VMEM((points, points), bf16),
            pltpu.VMEM((points, points), bf16),
            pltpu.VMEM((2, points + high - low, width), bf16),
            pltpu.VMEM((width, points + high - low), bf16),
            pltpu.VMEM((2, width, width), bf16),
            pltpu.VMEM((2, width, width), bf16),
            pltpu.VMEM((points, high - low), bf16),
            pltpu.VMEM((points, points), bf16),
            pltpu.VMEM((2, width, width), f32),
            pltpu.VMEM((2, width, width), bf16),
            pltpu.VMEM((width, 128), f32),
            pltpu.VMEM((8, width), f32),
            pltpu.SemaphoreType.DMA((13,)),
            pltpu.SemaphoreType.DMA((10,)),
        ],
        input_output_aliases=alias,
        compiler_params=pltpu.CompilerParams(vmem_limit_bytes=VMEM_LIMIT),
        name="piece_%d%d_%d" % (i, k, low),
    )(*operands)


def per_device(
    amps, x_factor, core, cycle_w, domain_tiles, domain_count, tile_slot, occ_energy, virt_energy
):
    occ = amps.shape[2]
    width = amps.shape[4]
    tile_width = x_factor.shape[1]
    grid_points = x_factor.shape[2]
    window = cycle_w.shape[4]
    cols = lax.axis_size("col")
    amp4 = amps[0, 0].reshape(occ * occ, width, width)
    shard = cycle_w[0].reshape(occ * occ, tile_width, window)

    early, split = 384, 512
    tiles, count = domain_tiles[0, 0], domain_count
    xall, wall, far, first, coret, *turned = gather_parts(x_factor, shard, amp4, core, early, split)
    xall = xall.reshape(-1, tile_width, grid_points)
    mirror = [(i, (i + cols // 2) % cols) for i in range(cols)]
    second, third, fourth = [lax.ppermute(part, "col", mirror) for part in turned[:3]]
    side = lax.ppermute(far, "col", [(i, i ^ 2) for i in range(cols)])

    x, xt, wt = own_ladder(tiles, count, tile_slot, xall, amp4, core)
    side, tail, wt = lax.optimization_barrier((side, turned[3], wt))
    fifth = lax.ppermute(tail, "col", mirror)
    twin = lax.ppermute(side, "col", [(i, i ^ 1) for i in range(cols)])
    wdt, part, down, along = own_cycle(tiles, count, occ_energy[0, 0], virt_energy[None, :], wall, far, side, twin, amp4)
    energies = (down, along)
    residual, updated = row(0, *energies, first, second, xt, x, coret, wt, wdt, amp4, part)
    fixed = (xt, x, coret)
    part, = piece(1, 0, 0, width, *energies, third, *fixed, wt, wdt, amp4, part, None, None)
    part, total = piece(1, 1, 0, split, *energies, fourth, *fixed, wt, wdt, amp4, part, None, None)
    residual, updated = piece(
        1, 1, split, width, *energies, fifth, *fixed, total, wdt, amp4, part, residual, updated
    )
    return residual.reshape(amps.shape), updated.reshape(amps.shape)


def solution(mesh):
    in_specs = (
        P("row", "col", None, None, None, None),
        P("row", None, None),
        P(),
        P("row", None, None, "col", None),
        P("row", "col", None),
        P("row", "col"),
        P(),
        P("row", "col", None, None),
        P(),
    )
    out_specs = (P("row", "col", None, None, None, None), P("row", "col", None, None, None, None))
    return jax.shard_map(
        per_device, mesh=mesh, in_specs=in_specs, out_specs=out_specs, check_vma=False
    )
```
